128 devices in a mesh: owner: 32 (over z, y, core), head: 4 (over x).
Axes of the slice: x: 4, y: 4, z: 4, core: 2. Of those that a mesh axis runs over, the one named last changes fastest.
Arguments:
- nodes: bfloat16 [65536, 768], P('owner'), may hold values from -6 to 6
- qkv_weight: bfloat16 [3, 768, 768], P(None, None, 'head'), may hold values from -12 to 12
- out_weight: bfloat16 [768, 768], replicated, may hold values from -0.6484375 to 0.6484375
- hop_bias: float32 [32, 24], P(None, 'head'), may hold values from -4 to 4
- up_weight: bfloat16 [768, 3072], replicated, may hold values from -0.21875 to 0.21875
- down_weight: bfloat16 [3072, 768], replicated, may hold values from -0.109375 to 0.109375
- key_owner: int32 [1024, 1], replicated, may hold values from 0 to 31; in each aligned block of 32 rows (0 to 31, 32 to 63, ...) at most 2 rows name the same one
- key_local: int32 [1024], replicated, may hold values from 0 to 7
- query_owner: int32 [1024, 1], replicated, may hold values from 0 to 31; in each aligned block of 32 rows (0 to 31, 32 to 63, ...) at most 2 rows name the same one
- query_local: int32 [1024], replicated, may hold values from 0 to 7
- hop_bucket: int32 [1024], P('owner'), may hold values from 0 to 31
Outputs:
- layer_out: bfloat16 [65536, 768], P('owner', 'head')
The draws below stay inside these ranges and needn't reach their ends.
Inputs may be any that keep to these rules, and one draw needn't show every extreme that they name: `key_owner`: among the 32 tiles of one worker (rows w * 32 to (w + 1) * 32 - 1) no owner is named more than 2 times; every draw has workers that name some owner exactly 2 times. `query_owner`: among the 32 tiles of one worker no owner is named more than 2 times; every draw has workers that name some owner exactly 2 times.
All inputs are finite; a program needn't handle non-finite values.
Results may differ from the reference program's by a relative error of at most 0.0099.
Values may be sent and summed in bfloat16 or wider, within the bound.
A program may use at most 192 MiB of HBM per device.

```python
import math
import jax
import jax.numpy as jnp
import numpy as np
from jax import lax

D = 768
HEADS = 24
FF = 3072
BUCKETS = 32
CSIZE = 256
KEY_CAP = 2
QUERY_CAP = 2
CL_DEV = 8
CLUSTERS = 256
NODES = 65536
TILES_DEV = 32
TILES = 1024
N_OWNER = 32


def draw_qkv_weight(key, part):
    key = jax.random.fold_in(key, 11)
    base = jax.random.normal(key, (3, D, D), jnp.float32) * (1.5 * D ** (-0.5))
    return base.astype(jnp.bfloat16)


def place_ends(entries, key, least, top_value):
    place = [jax.random.randint(jax.random.fold_in(key, axis), (), 0, length) for axis, length in enumerate(entries.shape)]
    widest = entries.shape.index(max(entries.shape))
    neighbour = place[:widest] + [(place[widest] + 1) % entries.shape[widest]] + place[widest + 1:]
    return entries.at[tuple(place)].set(least).at[tuple(neighbour)].set(top_value)


def level_of(stream_key, dims, cuts, low, largest):
    gain = 1.0
    for axis_at, shards_of in cuts:
        draws = jax.random.uniform(jax.random.fold_in(jax.random.fold_in(stream_key, 6), axis_at), (shards_of,), jnp.float32, low / len(cuts), largest / len(cuts))
        gain = gain * jnp.repeat(jnp.exp(draws), dims[axis_at] // shards_of).reshape((-1,) + (1,) * (len(dims) - 1 - axis_at))
    return gain


def deal_out(key, own, number, rows, count, top, bound, skew):
    order = jax.random.permutation(key, count)
    packed, ordinary = load_shares(count, rows * top, bound, skew, True), load_shares(count, rows * top, bound, skew, False)
    places = jnp.arange(count)

    def named(lengths, offset_by):
        used = int((lengths > 0).sum())
        fixed = max(1, used // 4)
        moved = fixed + (places - fixed + offset_by * (used - fixed)) % max(1, count - fixed)
        return jnp.zeros((count,), jnp.int32).at[order[jnp.where(places < fixed, places, moved)]].set(jnp.asarray(lengths, jnp.int32))

    lengths = jnp.where(number % 4 == 0, named(packed, number // 4), named(ordinary, number - number // 4 - 1))
    mixed = jax.random.permutation(jax.random.fold_in(own, 3), count)
    donor, sink = mixed[0:count // 2 * 2:2], mixed[1:count // 2 * 2:2]
    margin = jnp.minimum(lengths[donor] - 1, bound - lengths[sink]) // 2
    margin = jnp.where((donor == order[0]) | (sink == order[0]) | (lengths[sink] == 0), 0, jnp.maximum(margin, 0))
    moved = jax.random.randint(jax.random.fold_in(own, 4), (count // 2,), 0, 1 << 20) % (margin + 1)
    lengths = lengths.at[donor].add(-moved).at[sink].add(moved)
    items = jnp.searchsorted(jnp.cumsum(lengths), jnp.arange(rows * top), side="right").astype(jnp.int32)
    table = items.reshape(top, rows).T
    table = table[jax.random.permutation(jax.random.fold_in(own, 1), rows)]
    offset_by = jax.random.randint(jax.random.fold_in(own, 2), (rows, 1), 0, top)
    return jnp.take_along_axis(table, (jnp.arange(top)[None, :] + offset_by) % top, axis=1)


def load_shares(amount, total, bound, slope, full):
    weights = [(1 << 20) // math.isqrt(rank ** slope) + 1 for rank in range(1, amount + 1)]
    largest = bound if full else min(bound, max(-(-total // amount), total * weights[0] // sum(weights)))
    least = 1 if total - largest >= amount - 1 else 0
    holding, spare = [largest] + [least] * (amount - 1), total - largest - least * (amount - 1)
    while spare > 0:
        free = [i for i in range(1, amount) if holding[i] < largest] or [i for i in range(1, amount) if holding[i] < bound]
        whole, left = sum([weights[i] for i in free]), spare
        for i in free:
            more = min(bound - holding[i], max(1, left * weights[i] // whole), spare)
            holding[i] = holding[i] + more
            spare = spare - more
    return np.array(holding)


def noise(stream_key, shape, scale, most, split=(), kind=jnp.bfloat16):
    array = jax.random.normal(stream_key, shape, jnp.float32) * scale
    if len(split) > 0:
        array = level_of(stream_key, shape, split, -0.22, 0.18) * array
    return jnp.clip(array, min=-most, max=most).astype(kind)


def setup_inputs(seed: int = 0) -> dict:
    arg_keys = jax.random.split(jax.random.key(seed), 12)
    nodes = noise(arg_keys[0], (NODES, D), 1.0, 6.0, ((0, 32),))
    qkv_weight = draw_qkv_weight(jax.random.fold_in(arg_keys[11], 71), 0)
    out_weight = noise(arg_keys[2], (D, D), (3.0 / D ** 0.5), 0.6484375)
    hop_bias = noise(arg_keys[3], (BUCKETS, HEADS), 1.0, 4.0, ((1, 4),), jnp.float32)
    up_weight = noise(arg_keys[4], (D, FF), D ** -0.5, 0.21875)
    down_weight = noise(arg_keys[5], (FF, D), FF ** -0.5, 0.109375)
    key_owner_keys = jax.random.split(jax.random.fold_in(arg_keys[6], 1), TILES // TILES_DEV)
    key_owner_turns = jax.random.permutation(jax.random.fold_in(arg_keys[6], 3), TILES // TILES_DEV)
    key_owner = jax.vmap(lambda own, number: deal_out(jax.random.fold_in(arg_keys[6], 2), own, number, TILES_DEV, N_OWNER, 1, KEY_CAP, 2))(key_owner_keys, key_owner_turns).reshape((TILES, 1))
    key_local = place_ends(jax.random.randint(arg_keys[7], (TILES,), 0, CL_DEV), jax.random.fold_in(arg_keys[7], 1), 0, CL_DEV - 1).astype(jnp.int32)
    query_owner_keys = jax.random.split(jax.random.fold_in(arg_keys[8], 1), TILES // TILES_DEV)
    query_owner_turns = jax.random.permutation(jax.random.fold_in(arg_keys[8], 3), TILES // TILES_DEV)
    query_owner = jax.vmap(lambda own, number: deal_out(jax.random.fold_in(arg_keys[8], 2), own, number, TILES_DEV, N_OWNER, 1, QUERY_CAP, 2))(query_owner_keys, query_owner_turns).reshape((TILES, 1))
    query_local = place_ends(jax.random.randint(arg_keys[9], (TILES,), 0, CL_DEV), jax.random.fold_in(arg_keys[9], 1), 0, CL_DEV - 1).astype(jnp.int32)
    hop_bucket = place_ends(jax.random.randint(arg_keys[10], (TILES,), 0, BUCKETS), jax.random.fold_in(arg_keys[10], 1), 0, BUCKETS - 1).astype(jnp.int32)
    return {"nodes": nodes, "qkv_weight": qkv_weight, "out_weight": out_weight, "hop_bias": hop_bias, "up_weight": up_weight, "down_weight": down_weight, "key_owner": key_owner, "key_local": key_local, "query_owner": query_owner, "query_local": query_local, "hop_bucket": hop_bucket}


EPSILON = 1e-05

def norm_rows(values):
    center = values - lax.optimization_barrier(jnp.mean(values, axis=-1, keepdims=True))
    spread = lax.optimization_barrier(jnp.mean(center * center, axis=-1, keepdims=True))
    return center * lax.rsqrt(spread + EPSILON)

def tile_partial(query_block, pair_block, bias_rows):
    batch, length, feature_count = query_block.shape
    head_count = bias_rows.shape[1]
    head_size = feature_count // head_count
    scale = 1.0 / math.sqrt(head_size)
    queries = query_block.astype(jnp.float32).reshape(batch, length, head_count, head_size)
    keys = pair_block[..., :feature_count].astype(jnp.float32).reshape(batch, length, head_count, head_size)
    values = pair_block[..., feature_count:].astype(jnp.float32).reshape(batch, length, head_count, head_size)
    scores = jnp.einsum('bqhd,bkhd->bhqk', queries, keys, precision=lax.Precision.HIGHEST) * scale + bias_rows[:, :, None, None]
    highest = lax.optimization_barrier(jnp.max(scores, axis=-1))
    expo = jnp.exp(scores - highest[..., None])
    totals = lax.optimization_barrier(jnp.sum(expo, axis=-1))
    weights = expo.astype(jnp.bfloat16)
    mixed = jnp.einsum('bhqk,bkhd->bqhd', weights.astype(jnp.float32), values, precision=lax.Precision.HIGHEST)
    partial_value = mixed / jnp.transpose(totals, (0, 2, 1))[..., None]
    return (highest + jnp.log(totals), partial_value.reshape(batch, length, feature_count))

def reference(nodes, qkv_weight, out_weight, hop_bias, up_weight, down_weight, key_owner, key_local, query_owner, query_local, hop_bucket):
    head_size = D // HEADS
    normed = norm_rows(nodes.astype(jnp.float32)).astype(jnp.bfloat16)
    projected = [jnp.dot(normed, qkv_weight[index], preferred_element_type=jnp.float32).astype(jnp.bfloat16) for index in range(3)]
    query_blocks = projected[0].reshape(CLUSTERS, CSIZE, D)
    pair_blocks = jnp.concatenate([projected[1], projected[2]], axis=-1).reshape(CLUSTERS, CSIZE, 2 * D)
    self_bias = jnp.broadcast_to(hop_bias[0], (CLUSTERS, HEADS))

    def self_group(inputs):
        return tile_partial(inputs[0], inputs[1], inputs[2])
    self_log, self_part = lax.map(self_group, (query_blocks.reshape(CLUSTERS // 4, 4, CSIZE, D), pair_blocks.reshape(CLUSTERS // 4, 4, CSIZE, 2 * D), self_bias.reshape(CLUSTERS // 4, 4, HEADS)))
    best = self_log.reshape(CLUSTERS, HEADS, CSIZE)
    totals = jnp.ones((CLUSTERS, HEADS, CSIZE), jnp.float32)
    accum = self_part.reshape(CLUSTERS, CSIZE, HEADS, head_size)
    query_ids = (query_owner[:, 0] * CL_DEV + query_local).astype(jnp.int32)
    key_ids = (key_owner[:, 0] * CL_DEV + key_local).astype(jnp.int32)
    tile_bias = hop_bias[hop_bucket]

    def absorb(carry, item):
        best, totals, accum = carry
        query_id, key_id, bias_row = item
        log_total, partial_value = tile_partial(query_blocks[query_id][None], pair_blocks[key_id][None], bias_row[None])
        old_log = lax.dynamic_index_in_dim(best, query_id, 0, keepdims=False)
        old_total = lax.dynamic_index_in_dim(totals, query_id, 0, keepdims=False)
        old_accum = lax.dynamic_index_in_dim(accum, query_id, 0, keepdims=False)
        new_log = jnp.maximum(old_log, log_total[0])
        keep = jnp.exp(old_log - new_log)
        fresh = jnp.exp(log_total[0] - new_log)
        new_total = old_total * keep + fresh
        new_accum = old_accum * jnp.transpose(keep)[..., None] + jnp.transpose(fresh)[..., None] * partial_value[0].reshape(CSIZE, HEADS, head_size)
        best = lax.dynamic_update_index_in_dim(best, new_log, query_id, 0)
        totals = lax.dynamic_update_index_in_dim(totals, new_total, query_id, 0)
        accum = lax.dynamic_update_index_in_dim(accum, new_accum, query_id, 0)
        return ((best, totals, accum), None)
    (best, totals, accum), unused = lax.scan(absorb, (best, totals, accum), (query_ids, key_ids, tile_bias))
    attention = (accum / jnp.transpose(totals, (0, 2, 1))[..., None]).reshape(NODES, D).astype(jnp.bfloat16)
    resid = nodes.astype(jnp.float32) + jnp.dot(attention, out_weight, preferred_element_type=jnp.float32)
    normed_again = norm_rows(resid).astype(jnp.bfloat16)
    hidden = jax.nn.gelu(jnp.dot(normed_again, up_weight, preferred_element_type=jnp.float32)).astype(jnp.bfloat16)
    return (resid + jnp.dot(hidden, down_weight, preferred_element_type=jnp.float32)).astype(jnp.bfloat16)
```

```python
import functools
import math

import jax
import jax.numpy as jnp
from jax import lax
from jax.experimental import pallas as pl
from jax.experimental.pallas import tpu as pltpu
from jax.sharding import PartitionSpec as P

CSIZE = 256
EPSILON = 1e-05
RING = 4
LOCAL = 8
PLAN_HEADS = 3
HEAD_SIZE = 32
PLAN_FEATURES = PLAN_HEADS * HEAD_SIZE
LIST_MAX = 544
UNROLL = 4
MESH = pl.DeviceIdType.MESH
LOG2E = math.log2(math.e)
NEVER = -1e30


def norm_rows(values):
    center = values - jnp.mean(values, axis=-1, keepdims=True)
    spread = jnp.mean(center * center, axis=-1, keepdims=True)
    return center * lax.rsqrt(spread + EPSILON)


def coordinates():
    me = lax.axis_index("owner")
    return lax.div(me, 8), lax.rem(lax.div(me, 2), 4), lax.rem(me, 2)


def ring_at(axis, step):
    z, y, c = coordinates()
    if axis == "z":
        z = lax.rem(z + step + RING, RING)
    else:
        y = lax.rem(y + step + RING, RING)
    return ((z * 4 + y) * 2 + c, lax.axis_index("head"))


def sibling():
    z, y, c = coordinates()
    return ((z * 4 + y) * 2 + 1 - c, lax.axis_index("head"))


def greet(partners):
    barrier = pltpu.get_barrier_semaphore()
    for partner in partners:
        pl.semaphore_signal(barrier, inc=1, device_id=partner, device_id_type=MESH)
    pl.semaphore_wait(barrier, len(partners))


def gather_kernel(q_ref, kv_ref, qg_ref, kvg_ref, ring_send, ring_recv, pair_send, pair_recv, own_sem):
    z, y, c = coordinates()
    greet([ring_at("z", 1), ring_at("z", -1), ring_at("y", 1), ring_at("y", -1), sibling()])
    half = LOCAL // 2
    sent = []
    own = []

    def part(h):
        return pl.ds(h * half, half)

    streams = []
    for plan in range(2):
        q_axis, kv_axis = ("z", "y") if plan == 0 else ("y", "z")
        for kind, axis in (("kv", kv_axis), ("q", q_axis)):
            at = z if axis == "z" else y
            if kind == "q":
                source = lambda h, plan=plan: q_ref.at[plan, part(h)]
                slot = lambda p, h, plan=plan: qg_ref.at[plan, p, part(h)]
            else:
                source = lambda h, plan=plan: kv_ref.at[plan, part(h)]
                slot = lambda p, h, plan=plan: kvg_ref.at[plan, p, c, part(h)]
            streams.append((len(streams), plan, kind, axis, at, source, slot))

    def send(src, dst, send_sem, recv_sem, device):
        copy = pltpu.make_async_remote_copy(
            src_ref=src, dst_ref=dst, send_sem=send_sem, recv_sem=recv_sem,
            device_id=device, device_id_type=MESH,
        )
        copy.start()
        sent.append(copy)

    def arrived(ref, sem):
        pltpu.make_async_remote_copy(
            src_ref=ref, dst_ref=ref, send_sem=ring_send.at[0, 0], recv_sem=sem,
            device_id=sibling(), device_id_type=MESH,
        ).wait_recv()

    for turn in range(2):
        for number, plan, kind, axis, at, source, slot in streams:
            up, down = turn, 1 - turn
            send(source(up), slot(at, up), ring_send.at[number, up], ring_recv.at[number, up], ring_at(axis, 1))
            send(source(down), slot(at, down), ring_send.at[number, 2 + down], ring_recv.at[number, 2 + down], ring_at(axis, -1))
    for number, plan, kind, axis, at, source, slot in streams:
        if kind == "kv":
            for h in range(2):
                send(source(h), slot(at, h), pair_send.at[plan, h], pair_recv.at[plan, h], sibling())
        for h in range(2):
            copy = pltpu.make_async_copy(source(h), slot(at, h), own_sem.at[number, h])
            copy.start()
            own.append(copy)

    def place(at, step):
        return lax.rem(at + step + RING, RING)

    for number, plan, kind, axis, at, source, slot in streams:
        before, after = slot(place(at, -1), 0), slot(place(at, 1), 1)
        arrived(before, ring_recv.at[number, 0])
        send(before, before, ring_send.at[number, 4], ring_recv.at[number, 4], ring_at(axis, 1))
        arrived(after, ring_recv.at[number, 3])
        send(after, after, ring_send.at[number, 5], ring_recv.at[number, 5], ring_at(axis, -1))
        if kind == "kv":
            send(before, before, pair_send.at[plan, 2], pair_recv.at[plan, 2], sibling())
            send(after, after, pair_send.at[plan, 5], pair_recv.at[plan, 5], sibling())
    for number, plan, kind, axis, at, source, slot in streams:
        before, after = slot(place(at, -1), 1), slot(place(at, 1), 0)
        arrived(before, ring_recv.at[number, 1])
        arrived(after, ring_recv.at[number, 2])
        if kind == "kv":
            send(before, before, pair_send.at[plan, 3], pair_recv.at[plan, 3], sibling())
            send(after, after, pair_send.at[plan, 4], pair_recv.at[plan, 4], sibling())
    for number, plan, kind, axis, at, source, slot in streams:
        for h in range(2):
            far = slot(place(at, 2), h)
            arrived(far, ring_recv.at[number, 4 + h])
            if kind == "kv":
                send(far, far, pair_send.at[plan, 6 + h], pair_recv.at[plan, 6 + h], sibling())
    for number, plan, kind, axis, at, source, slot in streams:
        if kind == "kv":
            for index, step in enumerate((0, -1, 1, 2)):
                for h in range(2):
                    arrived(kvg_ref.at[plan, place(at, step), 1 - c, part(h)], pair_recv.at[plan, 2 * index + h])
    for copy in sent:
        copy.wait_send()
    for copy in own:
        copy.wait()


def gather(q_blocks, kv_blocks):
    any_space = pl.BlockSpec(memory_space=pl.ANY)
    dma = pltpu.SemaphoreType.DMA
    return pl.pallas_call(
        gather_kernel,
        out_shape=[
            jax.ShapeDtypeStruct((2, RING, LOCAL, PLAN_FEATURES, CSIZE), jnp.bfloat16),
            jax.ShapeDtypeStruct((2, RING, 2, LOCAL, 2 * PLAN_FEATURES, CSIZE), jnp.bfloat16),
        ],
        in_specs=[any_space] * 2,
        out_specs=[any_space] * 2,
        scratch_shapes=[dma((4, 6)), dma((4, 6)), dma((2, 8)), dma((2, 8)), dma((4, 2))],
        compiler_params=pltpu.CompilerParams(collective_id=0, has_side_effects=True),
        name="gather",
    )(q_blocks, kv_blocks)


def tile_kernel(list_ref, bucket_ref, bias_ref, q_ref, kv_ref, part_ref, log_ref, m_ref, l_ref, acc_ref):
    heads = range(PLAN_HEADS)
    queries = q_ref.shape[0]
    m_ref[...] = jnp.full(m_ref.shape, NEVER, jnp.float32)
    l_ref[...] = jnp.zeros(l_ref.shape, jnp.float32)
    acc_ref[...] = jnp.zeros(acc_ref.shape, jnp.float32)
    ones = jnp.ones((16, CSIZE), jnp.bfloat16)

    def rows(h):
        return slice(HEAD_SIZE * h, HEAD_SIZE * (h + 1))

    def batch(step, carry):
        loaded = []
        for u in range(UNROLL):
            item = list_ref[step * UNROLL + u]
            state = lax.bitwise_and(item, 127)
            key = lax.bitwise_and(lax.shift_right_logical(item, 7), 127)
            tile = lax.bitwise_and(lax.shift_right_logical(item, 14), 2047)
            query = jnp.minimum(state, queries - 1)
            head0 = jnp.where(key >= kv_ref.shape[0] // 2, PLAN_HEADS, 0)
            bucket = jnp.where(tile >= 1024, 0, bucket_ref[jnp.minimum(tile, 1023)])
            bias = [bias_ref[bucket * (2 * PLAN_HEADS) + head0 + h] * LOG2E for h in heads]
            scores = [
                lax.dot_general(
                    kv_ref[key, rows(h), :], q_ref[query, rows(h), :],
                    (((0,), (0,)), ((), ())), preferred_element_type=jnp.float32,
                )
                for h in heads
            ]
            loaded.append((state, key, bias, scores))
        done = []
        for state, key, bias, scores in loaded:
            highest = [jnp.max(s, axis=0, keepdims=True) for s in scores]
            weights = [jnp.exp2(s - top).astype(jnp.bfloat16) for s, top in zip(scores, highest)]
            mixed = [
                jnp.dot(
                    jnp.concatenate([kv_ref[key, slice(PLAN_FEATURES + HEAD_SIZE * h, PLAN_FEATURES + HEAD_SIZE * (h + 1)), :], ones], 0),
                    weights[h], preferred_element_type=jnp.float32,
                )
                for h in heads
            ]
            done.append((state, [top + b for top, b in zip(highest, bias)], mixed))
        for state, tops, mixed in done:
            old_m = [m_ref[state, h : h + 1, :] for h in heads]
            old_l = [l_ref[state, h : h + 1, :] for h in heads]
            old_acc = [acc_ref[state, rows(h), :] for h in heads]
            new_m = [jnp.maximum(a, b) for a, b in zip(old_m, tops)]
            keep = [jnp.exp2(a - b) for a, b in zip(old_m, new_m)]
            fresh = [jnp.exp2(a - b) for a, b in zip(tops, new_m)]
            for h in heads:
                m_ref[state, h : h + 1, :] = new_m[h]
                l_ref[state, h : h + 1, :] = old_l[h] * keep[h] + mixed[h][HEAD_SIZE : HEAD_SIZE + 1] * fresh[h]
                acc_ref[state, rows(h), :] = old_acc[h] * keep[h] + mixed[h][:HEAD_SIZE] * fresh[h]
        return carry

    lax.fori_loop(0, lax.div(list_ref[LIST_MAX] + UNROLL - 1, UNROLL), batch, 0)

    def finish(group, carry):
        for local in range(LOCAL):
            state = group * LOCAL + local
            for h in heads:
                total = l_ref[state, h : h + 1, :]
                held = total > 0
                safe = jnp.where(held, total, 1.0)
                part_ref[state, rows(h), :] = (acc_ref[state, rows(h), :] * (1.0 / safe)).astype(jnp.bfloat16)
                row = local * PLAN_HEADS + h
                log_ref[group, row : row + 1, :] = m_ref[state, h : h + 1, :] + jnp.log2(safe)
        return carry

    lax.fori_loop(0, queries // LOCAL, finish, 0)


def tiles(items, buckets, bias, q_all, kv_all):
    queries = q_all.shape[0]
    whole = lambda shape: pl.BlockSpec(shape, lambda i, *_: (0,) * len(shape))
    log_shape = (queries // LOCAL, LOCAL * PLAN_HEADS, CSIZE)
    return pl.pallas_call(
        tile_kernel,
        grid_spec=pltpu.PrefetchScalarGridSpec(
            num_scalar_prefetch=3,
            grid=(1,),
            in_specs=[whole(q_all.shape), whole(kv_all.shape)],
            out_specs=[whole(q_all.shape), whole(log_shape)],
            scratch_shapes=[
                pltpu.VMEM((queries + 1, 8, CSIZE), jnp.float32),
                pltpu.VMEM((queries + 1, 8, CSIZE), jnp.float32),
                pltpu.VMEM((queries + 1, PLAN_FEATURES, CSIZE), jnp.float32),
            ],
        ),
        out_shape=[
            jax.ShapeDtypeStruct(q_all.shape, jnp.bfloat16),
            jax.ShapeDtypeStruct(log_shape, jnp.float32),
        ],
        compiler_params=pltpu.CompilerParams(vmem_limit_bytes=56 * 2**20),
        name="tiles",
    )(items, buckets, bias, q_all, kv_all)


def tile_list(key_owner, key_local, query_owner, query_local):
    z, y, c = coordinates()
    key_owner, query_owner = key_owner.reshape(8, 128), query_owner.reshape(8, 128)
    key_local, query_local = key_local.reshape(8, 128), query_local.reshape(8, 128)
    qz, qy, qc = query_owner // 8, query_owner // 2 % 4, query_owner % 2
    kz, ky, kc = key_owner // 8, key_owner // 2 % 4, key_owner % 2
    number = jnp.arange(1024, dtype=jnp.int32).reshape(8, 128)
    mine_a = (qy == y) & (qc == c) & (kz == z)
    mine_b = (qz == z) & (qc == c) & (ky == y)
    item_a = (qz * 8 + query_local) + ((ky * 16 + kc * 8 + key_local) << 7) + (number << 14)
    item_b = (32 + qy * 8 + query_local) + ((64 + kz * 16 + kc * 8 + key_local) << 7) + (number << 14)
    mine = jnp.concatenate([mine_a, mine_b], 0)
    items = jnp.concatenate([item_a, item_b], 0)
    ones = mine.astype(jnp.float32)
    lane = jnp.arange(128)
    row = jnp.arange(16)
    inside = jnp.dot(ones, (lane[:, None] < lane[None, :]).astype(jnp.float32))
    counts = jnp.sum(ones, axis=1)
    ahead = jnp.sum(jnp.where(row[None, :] < row[:, None], counts[None, :], 0.0), axis=1)
    rank = (inside + ahead[:, None]).astype(jnp.int32) + 16
    rank = jnp.where(mine, rank, -1).reshape(2048)
    own = jnp.arange(8, dtype=jnp.int32)
    own_a = (z * 8 + own) + ((y * 16 + c * 8 + own) << 7) + (1024 << 14)
    own_b = (32 + y * 8 + own) + ((64 + z * 16 + c * 8 + own) << 7) + (1024 << 14)
    place = jnp.arange(LIST_MAX, dtype=jnp.int32)
    total = jnp.sum(counts).astype(jnp.int32) + 16
    listed = jnp.sum(jnp.where(place[:, None] == rank[None, :], items.reshape(2048)[None, :], 0), axis=1)
    listed = jnp.where(place < total, listed, 64 + (1024 << 14))
    return jnp.concatenate([own_a, own_b, listed[16:], total[None]])


def per_device(
    nodes, qkv_weight, out_weight, hop_bias, up_weight, down_weight,
    key_owner, key_local, query_owner, query_local, hop_bucket,
):
    head_rank = lax.axis_index("head")
    model_width = nodes.shape[1]
    items = tile_list(key_owner, key_local, query_owner, query_local)
    buckets = lax.all_gather(hop_bucket, "owner", axis=0, tiled=True)
    normed = norm_rows(nodes.astype(jnp.float32)).astype(jnp.bfloat16)
    projected = jnp.einsum("sdf,rd->sfr", qkv_weight, normed, preferred_element_type=jnp.float32)
    q_rows = (projected[0] * (LOG2E / math.sqrt(HEAD_SIZE))).astype(jnp.bfloat16)
    kv_rows = projected[1:].astype(jnp.bfloat16)
    q_blocks = q_rows.reshape(2, PLAN_FEATURES, LOCAL, CSIZE).transpose(0, 2, 1, 3)
    kv_blocks = (
        kv_rows.reshape(2, 2, PLAN_FEATURES, LOCAL, CSIZE)
        .transpose(1, 3, 0, 2, 4)
        .reshape(2, LOCAL, 2 * PLAN_FEATURES, CSIZE)
    )
    q_all, kv_all = gather(q_blocks, kv_blocks)
    parts, logs = tiles(
        items, buckets, hop_bias.reshape(-1),
        q_all.reshape(2 * RING * LOCAL, PLAN_FEATURES, CSIZE),
        kv_all.reshape(2 * RING * 2 * LOCAL, 2 * PLAN_FEATURES, CSIZE),
    )
    parts = parts.reshape(2, RING, LOCAL, PLAN_HEADS, HEAD_SIZE, CSIZE)
    logs = logs.reshape(2, RING, LOCAL, PLAN_HEADS, CSIZE)
    along_z = [[(z * 4 + y) * 2 + c for z in range(4)] for y in range(4) for c in range(2)]
    along_y = [[(z * 4 + y) * 2 + c for y in range(4)] for z in range(4) for c in range(2)]
    back = lambda x, groups: lax.all_to_all(x, "owner", 0, 0, axis_index_groups=groups, tiled=True)
    merged = []
    for plan, groups in enumerate((along_z, along_y)):
        part, log = back(parts[plan], groups), back(logs[plan], groups)
        share = jnp.exp2(log - jnp.max(log, axis=0))
        share = share / jnp.sum(share, axis=0)
        merged.append(jnp.sum(share[:, :, :, None, :] * part.astype(jnp.float32), axis=0).astype(jnp.bfloat16))
    attention = jnp.concatenate(merged, axis=1).reshape(LOCAL, 2 * PLAN_FEATURES, CSIZE)
    attention = lax.all_to_all(attention, "head", 0, 0, tiled=True).reshape(4, 2, 2 * PLAN_FEATURES, CSIZE)
    mixed = jnp.einsum(
        "xcfr,xfd->crd", attention, out_weight.reshape(4, 2 * PLAN_FEATURES, model_width),
        preferred_element_type=jnp.float32,
    ).reshape(2 * CSIZE, model_width)
    resid = lax.dynamic_slice_in_dim(nodes, head_rank * 2 * CSIZE, 2 * CSIZE, 0).astype(jnp.float32) + mixed
    normed_again = norm_rows(resid).astype(jnp.bfloat16)
    hidden = jax.nn.gelu(
        jnp.dot(normed_again, up_weight, preferred_element_type=jnp.float32)
    ).astype(jnp.bfloat16)
    out = (resid + jnp.dot(hidden, down_weight, preferred_element_type=jnp.float32)).astype(jnp.bfloat16)
    return lax.all_to_all(out, "head", 1, 0, tiled=True)


def solution(mesh):
    placed = (
        P("owner", None), P(None, None, "head"), P(), P(None, "head"), P(), P(),
        P(), P(), P(), P(), P("owner"),
    )
    return jax.shard_map(
        per_device, mesh=mesh, in_specs=placed, out_specs=P("owner", "head"), check_vma=False
    )
```

```python
import functools
import math

import jax
import jax.numpy as jnp
from jax import lax
from jax.experimental import pallas as pl
from jax.experimental.pallas import tpu as pltpu
from jax.sharding import PartitionSpec as P

CSIZE = 256
EPSILON = 1e-05
RING = 4
LOCAL = 8
PLAN_HEADS = 3
HEAD_SIZE = 32
PLAN_FEATURES = PLAN_HEADS * HEAD_SIZE
LIST_MAX = 544
UNROLL = 4
MESH = pl.DeviceIdType.MESH
LOG2E = math.log2(math.e)
NEVER = -1e30


def norm_rows(values):
    center = values - jnp.mean(values, axis=-1, keepdims=True)
    spread = jnp.mean(center * center, axis=-1, keepdims=True)
    return center * lax.rsqrt(spread + EPSILON)


def coordinates():
    me = lax.axis_index("owner")
    return lax.div(me, 8), lax.rem(lax.div(me, 2), 4), lax.rem(me, 2)


def place(at, step):
    return lax.rem(at + step + RING, RING)


def ring_at(axis, step):
    z, y, c = coordinates()
    if axis == "z":
        z = place(z, step)
    else:
        y = place(y, step)
    return ((z * 4 + y) * 2 + c, lax.axis_index("head"))


def sibling():
    z, y, c = coordinates()
    return ((z * 4 + y) * 2 + 1 - c, lax.axis_index("head"))


def greet(partners):
    barrier = pltpu.get_barrier_semaphore()
    for partner in partners:
        pl.semaphore_signal(barrier, inc=1, device_id=partner, device_id_type=MESH)
    pl.semaphore_wait(barrier, len(partners))


def gather_kernel(
    q_ref, kv_ref, bucket_ref, qg_ref, kvg_ref, table_ref,
    ring_send, ring_recv, pair_send, pair_recv, table_send, table_recv, own_sem,
):
    z, y, c = coordinates()
    own = pltpu.make_async_copy(bucket_ref, table_ref.at[c, z, y], own_sem)
    own.start()
    greet([ring_at(axis, step) for axis in "zy" for step in (1, 2, 3)] + [sibling()])
    half = LOCAL // 2
    sent = []

    def part(h):
        return pl.ds(h * half, half)

    streams = []
    for plan in range(2):
        q_axis, kv_axis = ("z", "y") if plan == 0 else ("y", "z")
        for kind, axis in (("kv", kv_axis), ("q", q_axis)):
            at = z if axis == "z" else y
            if kind == "q":
                source = lambda h, plan=plan: q_ref.at[plan, part(h)]
                slot = lambda p, h, plan=plan: qg_ref.at[plan, p, part(h)]
            else:
                source = lambda h, plan=plan: kv_ref.at[plan, part(h)]
                slot = lambda p, h, plan=plan: kvg_ref.at[plan, p, c, part(h)]
            streams.append((len(streams), plan, kind, axis, at, source, slot))

    def send(src, dst, send_sem, recv_sem, device):
        copy = pltpu.make_async_remote_copy(
            src_ref=src, dst_ref=dst, send_sem=send_sem, recv_sem=recv_sem,
            device_id=device, device_id_type=MESH,
        )
        copy.start()
        sent.append(copy)

    def arrived(ref, sem):
        pltpu.make_async_remote_copy(
            src_ref=ref, dst_ref=ref, send_sem=ring_send.at[0, 0], recv_sem=sem,
            device_id=sibling(), device_id_type=MESH,
        ).wait_recv()

    for step in (1, 2, 3):
        send(bucket_ref, table_ref.at[c, z, y], table_send.at[step - 1], table_recv.at[step - 1], ring_at("y", step))
    for turn in range(2):
        for number, plan, kind, axis, at, source, slot in streams:
            up, down = turn, 1 - turn
            send(source(up), slot(at, up), ring_send.at[number, up], ring_recv.at[number, up], ring_at(axis, 1))
            send(source(down), slot(at, down), ring_send.at[number, 2 + down], ring_recv.at[number, 2 + down], ring_at(axis, -1))
    for number, plan, kind, axis, at, source, slot in streams:
        if kind == "kv":
            for h in range(2):
                send(source(h), slot(at, h), pair_send.at[plan, h], pair_recv.at[plan, h], sibling())

    own.wait()
    for step in (1, 2, 3):
        arrived(table_ref.at[c, z, place(y, -step)], table_recv.at[step - 1])
    for step in (1, 2, 3):
        send(table_ref.at[c, z], table_ref.at[c, z], table_send.at[2 + step], table_recv.at[2 + step], ring_at("z", step))
    for number, plan, kind, axis, at, source, slot in streams:
        before, after = slot(place(at, -1), 0), slot(place(at, 1), 1)
        arrived(before, ring_recv.at[number, 0])
        send(before, before, ring_send.at[number, 4], ring_recv.at[number, 4], ring_at(axis, 1))
        arrived(after, ring_recv.at[number, 3])
        send(after, after, ring_send.at[number, 5], ring_recv.at[number, 5], ring_at(axis, -1))
        if kind == "kv":
            send(before, before, pair_send.at[plan, 2], pair_recv.at[plan, 2], sibling())
            send(after, after, pair_send.at[plan, 5], pair_recv.at[plan, 5], sibling())
    for step in (1, 2, 3):
        arrived(table_ref.at[c, place(z, -step)], table_recv.at[2 + step])
    send(table_ref.at[c], table_ref.at[c], table_send.at[6], table_recv.at[6], sibling())
    for number, plan, kind, axis, at, source, slot in streams:
        before, after = slot(place(at, -1), 1), slot(place(at, 1), 0)
        arrived(before, ring_recv.at[number, 1])
        arrived(after, ring_recv.at[number, 2])
        if kind == "kv":
            send(before, before, pair_send.at[plan, 3], pair_recv.at[plan, 3], sibling())
            send(after, after, pair_send.at[plan, 4], pair_recv.at[plan, 4], sibling())
    for number, plan, kind, axis, at, source, slot in streams:
        for h in range(2):
            far = slot(place(at, 2), h)
            arrived(far, ring_recv.at[number, 4 + h])
            if kind == "kv":
                send(far, far, pair_send.at[plan, 6 + h], pair_recv.at[plan, 6 + h], sibling())
    for number, plan, kind, axis, at, source, slot in streams:
        if kind == "kv":
            for index, step in enumerate((0, -1, 1, 2)):
                for h in range(2):
                    arrived(kvg_ref.at[plan, place(at, step), 1 - c, part(h)], pair_recv.at[plan, 2 * index + h])
    arrived(table_ref.at[1 - c], table_recv.at[6])
    for copy in sent:
        copy.wait_send()


def gather(q_blocks, kv_blocks, buckets):
    any_space = pl.BlockSpec(memory_space=pl.ANY)
    dma = pltpu.SemaphoreType.DMA
    return pl.pallas_call(
        gather_kernel,
        out_shape=[
            jax.ShapeDtypeStruct((2, RING, LOCAL, PLAN_FEATURES, CSIZE), jnp.bfloat16),
            jax.ShapeDtypeStruct((2, RING, 2, LOCAL, 2 * PLAN_FEATURES, CSIZE), jnp.bfloat16),
            jax.ShapeDtypeStruct((2, RING, RING, 1, 128), jnp.int32),
        ],
        in_specs=[any_space] * 3,
        out_specs=[any_space] * 3,
        scratch_shapes=[dma((4, 6)), dma((4, 6)), dma((2, 8)), dma((2, 8)), dma((7,)), dma((7,)), dma(())],
        compiler_params=pltpu.CompilerParams(collective_id=0, has_side_effects=True),
        name="gather",
    )(q_blocks, kv_blocks, buckets)


def tile_kernel(
    list_ref, bias_ref, own_q_ref, own_kv_ref, qg_ref, kvg_ref, table_hbm, part_ref, log_ref,
    q_ref, kv_ref, table_ref, m_ref, l_ref, acc_ref, own_sem, q_sem, kv_sem, table_sem,
):
    heads = range(PLAN_HEADS)
    z, y, c = coordinates()
    queries = part_ref.shape[0]
    keys = 2 * queries

    def load(source, target, sem):
        copy = pltpu.make_async_copy(source, target, sem)
        copy.start()
        return copy

    own, later = [load(table_hbm, table_ref, table_sem)], ([], [])
    for plan in range(2):
        q_at, kv_at = (z, y) if plan == 0 else (y, z)
        q_own = pl.ds((plan * RING + q_at) * LOCAL, LOCAL)
        kv_own = pl.ds(((plan * RING + kv_at) * 2 + c) * LOCAL, LOCAL)
        own.append(load(own_q_ref.at[plan], q_ref.at[q_own], own_sem.at[plan, 0]))
        own.append(load(own_kv_ref.at[plan], kv_ref.at[kv_own], own_sem.at[plan, 1]))
    for plan in range(2):
        q_at, kv_at = (z, y) if plan == 0 else (y, z)
        for step in range(RING):
            p = place(q_at, step)
            if step > 0:
                later[plan].append(load(
                    qg_ref.at[plan, p], q_ref.at[pl.ds((plan * RING + p) * LOCAL, LOCAL)], q_sem.at[plan, step - 1]
                ))
            p = place(kv_at, step)
            for other in range(2):
                if step + other > 0:
                    core = c if other == 0 else 1 - c
                    later[plan].append(load(
                        kvg_ref.at[plan, p, core],
                        kv_ref.at[pl.ds(((plan * RING + p) * 2 + core) * LOCAL, LOCAL)],
                        kv_sem.at[plan, 2 * step + other - 1],
                    ))
    m_ref[...] = jnp.full(m_ref.shape, NEVER, jnp.float32)
    l_ref[...] = jnp.zeros(l_ref.shape, jnp.float32)
    acc_ref[...] = jnp.zeros(acc_ref.shape, jnp.float32)
    ones = jnp.ones((16, CSIZE), jnp.bfloat16)

    def rows(h):
        return slice(HEAD_SIZE * h, HEAD_SIZE * (h + 1))

    def batch(step, carry):
        loaded = []
        for u in range(UNROLL):
            item = list_ref[step * UNROLL + u]
            state = lax.bitwise_and(item, 127)
            key = lax.bitwise_and(lax.shift_right_logical(item, 7), 127)
            tile = lax.bitwise_and(lax.shift_right_logical(item, 14), 2047)
            query = jnp.minimum(state, queries - 1)
            head0 = jnp.where(key >= keys // 2, PLAN_HEADS, 0)
            named = jnp.minimum(tile, 1023)
            worker = lax.shift_right_logical(named, 5)
            bucket = table_ref[
                lax.bitwise_and(worker, 1), lax.shift_right_logical(worker, 3),
                lax.bitwise_and(lax.shift_right_logical(worker, 1), 3), 0, lax.bitwise_and(named, 31),
            ]
            bucket = jnp.where(tile >= 1024, 0, bucket)
            bias = [bias_ref[bucket * (2 * PLAN_HEADS) + head0 + h] * LOG2E for h in heads]
            scores = [
                lax.dot_general(
                    kv_ref[key, rows(h), :], q_ref[query, rows(h), :],
                    (((0,), (0,)), ((), ())), preferred_element_type=jnp.float32,
                )
                for h in heads
            ]
            loaded.append((state, key, bias, scores))
        done = []
        for state, key, bias, scores in loaded:
            highest = [jnp.max(s, axis=0, keepdims=True) for s in scores]
            weights = [jnp.exp2(s - top).astype(jnp.bfloat16) for s, top in zip(scores, highest)]
            mixed = [
                jnp.dot(
                    jnp.concatenate([kv_ref[key, slice(PLAN_FEATURES + HEAD_SIZE * h, PLAN_FEATURES + HEAD_SIZE * (h + 1)), :], ones], 0),
                    weights[h], preferred_element_type=jnp.float32,
                )
                for h in heads
            ]
            done.append((state, [top + b for top, b in zip(highest, bias)], mixed))
        for state, tops, mixed in done:
            old_m = [m_ref[state, h : h + 1, :] for h in heads]
            old_l = [l_ref[state, h : h + 1, :] for h in heads]
            old_acc = [acc_ref[state, rows(h), :] for h in heads]
            new_m = [jnp.maximum(a, b) for a, b in zip(old_m, tops)]
            keep = [jnp.exp2(a - b) for a, b in zip(old_m, new_m)]
            fresh = [jnp.exp2(a - b) for a, b in zip(tops, new_m)]
            for h in heads:
                m_ref[state, h : h + 1, :] = new_m[h]
                l_ref[state, h : h + 1, :] = old_l[h] * keep[h] + mixed[h][HEAD_SIZE : HEAD_SIZE + 1] * fresh[h]
                acc_ref[state, rows(h), :] = old_acc[h] * keep[h] + mixed[h][:HEAD_SIZE] * fresh[h]
        return carry

    for copy in own:
        copy.wait()
    lax.fori_loop(0, 2 * LOCAL // UNROLL, batch, 0)
    for copy in later[0]:
        copy.wait()
    split = lax.div(list_ref[LIST_MAX], UNROLL)
    lax.fori_loop(2 * LOCAL // UNROLL, split, batch, 0)
    for copy in later[1]:
        copy.wait()
    lax.fori_loop(split, lax.div(list_ref[LIST_MAX + 1] + UNROLL - 1, UNROLL), batch, 0)

    def finish(group, carry):
        for local in range(LOCAL):
            state = group * LOCAL + local
            for h in heads:
                total = l_ref[state, h : h + 1, :]
                held = total > 0
                safe = jnp.where(held, total, 1.0)
                part_ref[state, rows(h), :] = (acc_ref[state, rows(h), :] * (1.0 / safe)).astype(jnp.bfloat16)
                row = local % 2 * PLAN_HEADS + h
                log_ref[group, local // 2, row : row + 1, :] = m_ref[state, h : h + 1, :] + jnp.log2(safe)
        return carry

    lax.fori_loop(0, queries // LOCAL, finish, 0)


def tiles(items, bias, own_q, own_kv, q_all, kv_all, table):
    queries, keys = 2 * RING * LOCAL, 2 * RING * 2 * LOCAL
    any_space = pl.BlockSpec(memory_space=pl.ANY)
    whole = lambda shape: pl.BlockSpec(shape, lambda i, *_: (0,) * len(shape))
    part_shape = (queries, PLAN_FEATURES, CSIZE)
    log_shape = (2 * RING, RING, 8, CSIZE)
    dma = pltpu.SemaphoreType.DMA
    return pl.pallas_call(
        tile_kernel,
        grid_spec=pltpu.PrefetchScalarGridSpec(
            num_scalar_prefetch=2,
            grid=(1,),
            in_specs=[any_space] * 5,
            out_specs=[whole(part_shape), whole(log_shape)],
            scratch_shapes=[
                pltpu.VMEM((queries, PLAN_FEATURES, CSIZE), jnp.bfloat16),
                pltpu.VMEM((keys, 2 * PLAN_FEATURES, CSIZE), jnp.bfloat16),
                pltpu.SMEM((2, RING, RING, 1, 128), jnp.int32),
                pltpu.VMEM((queries + 1, 8, CSIZE), jnp.float32),
                pltpu.VMEM((queries + 1, 8, CSIZE), jnp.float32),
                pltpu.VMEM((queries + 1, PLAN_FEATURES, CSIZE), jnp.float32),
                dma((2, 2)), dma((2, 3)), dma((2, 7)), dma(()),
            ],
        ),
        out_shape=[
            jax.ShapeDtypeStruct(part_shape, jnp.bfloat16),
            jax.ShapeDtypeStruct(log_shape, jnp.float32),
        ],
        compiler_params=pltpu.CompilerParams(vmem_limit_bytes=56 * 2**20),
        name="tiles",
    )(items, bias, own_q, own_kv, q_all, kv_all, table)


def tail_kernel(
    part_ref, log_ref, nodes_ref, wo_hbm, up_hbm, down_hbm, out_ref,
    wo_ref, up_ref, down_ref, rows_ref, part_in, log_in, own_part, own_log, merged, gathered, resid_ref, normed_ref, staged,
    weight_sem, own_sem, part_send, part_recv, log_send, log_recv, x_send, x_recv, out_send, out_recv, out_own,
):
    z, y, c = coordinates()
    me = lax.axis_index("owner")
    x = lax.axis_index("head")
    heads = range(PLAN_HEADS)
    features = 2 * PLAN_FEATURES

    def load(source, target, sem):
        copy = pltpu.make_async_copy(source, target, sem)
        copy.start()
        return copy

    def across(step):
        return (me, place(x, step))

    ready = []
    for plan in range(2):
        at = z if plan == 0 else y
        ready.append(load(part_ref.at[plan, at], own_part.at[plan], own_sem.at[plan, 0]))
        ready.append(load(log_ref.at[plan, at], own_log.at[plan], own_sem.at[plan, 1]))
    weights = [
        load(nodes_ref.at[pl.ds(x * 2 * CSIZE, 2 * CSIZE)], rows_ref, weight_sem.at[0]),
        load(wo_hbm, wo_ref, weight_sem.at[1]),
        load(up_hbm, up_ref, weight_sem.at[2]),
        load(down_hbm, down_ref, weight_sem.at[3]),
    ]
    greet([ring_at(axis, step) for axis in "zy" for step in (1, 2, 3)] + [across(step) for step in (1, 2, 3)])
    sent = []

    def send(src, dst, send_sem, recv_sem, device):
        copy = pltpu.make_async_remote_copy(
            src_ref=src, dst_ref=dst, send_sem=send_sem, recv_sem=recv_sem,
            device_id=device, device_id_type=MESH,
        )
        copy.start()
        sent.append(copy)

    def arrived(ref, sem):
        pltpu.make_async_remote_copy(
            src_ref=ref, dst_ref=ref, send_sem=x_send.at[0], recv_sem=sem,
            device_id=across(1), device_id_type=MESH,
        ).wait_recv()

    for turn in range(RING):
        chunk = place(x, turn + 1)
        for plan, axis in enumerate("zy"):
            at = z if plan == 0 else y
            for step in (2, 1, 3):
                to = place(at, step)
                send(
                    part_ref.at[plan, to, pl.ds(chunk * 2, 2)], part_in.at[plan, step - 1, pl.ds(chunk * 2, 2)],
                    part_send.at[plan, step - 1, turn], part_recv.at[plan, step - 1, turn], ring_at(axis, step),
                )
                send(
                    log_ref.at[plan, to, chunk], log_in.at[plan, step - 1, chunk],
                    log_send.at[plan, step - 1, turn], log_recv.at[plan, step - 1, turn], ring_at(axis, step),
                )
    for copy in ready:
        copy.wait()
    for turn in range(RING):
        chunk = place(x, turn + 1)
        for plan in range(2):
            for step in (2, 1, 3):
                arrived(part_in.at[plan, step - 1, pl.ds(chunk * 2, 2)], part_recv.at[plan, step - 1, turn])
                arrived(log_in.at[plan, step - 1, chunk], log_recv.at[plan, step - 1, turn])
        for plan in range(2):
            logs = [own_log[plan, chunk]] + [log_in[plan, i, chunk] for i in range(3)]
            best = jnp.maximum(jnp.maximum(logs[0], logs[1]), jnp.maximum(logs[2], logs[3]))
            shares = [jnp.exp2(log - best) for log in logs]
            scale = 1.0 / (shares[0] + shares[1] + shares[2] + shares[3])
            shares = [share * scale for share in shares]
            for local in range(2):
                for h in heads:
                    row = local * PLAN_HEADS + h
                    rows = slice(HEAD_SIZE * h, HEAD_SIZE * (h + 1))
                    total = own_part[plan, chunk * 2 + local, rows, :].astype(jnp.float32) * shares[0][row : row + 1]
                    for i in range(3):
                        total += part_in[plan, i, chunk * 2 + local, rows, :].astype(jnp.float32) * shares[i + 1][row : row + 1]
                    first = plan * PLAN_FEATURES + HEAD_SIZE * h
                    merged[turn, local, first : first + HEAD_SIZE, :] = total.astype(jnp.bfloat16)
        if turn < RING - 1:
            send(
                merged.at[turn], gathered.at[:, pl.ds(pl.multiple_of(x * features, 64), features), :],
                x_send.at[turn], x_recv.at[turn], across(turn + 1),
            )
    gathered[:, pl.ds(pl.multiple_of(x * features, 64), features), :] = merged[RING - 1]
    for turn in range(RING - 1):
        source = place(x, -(turn + 1))
        arrived(gathered.at[:, pl.ds(pl.multiple_of(source * features, 64), features), :], x_recv.at[turn])
    for copy in weights:
        copy.wait()
    out_copies = []
    for local in range(2):
        rows = slice(local * CSIZE, (local + 1) * CSIZE)
        mixed = lax.dot_general(
            gathered[local], wo_ref[...], (((0,), (0,)), ((), ())), preferred_element_type=jnp.float32
        )
        resid = rows_ref[rows, :].astype(jnp.float32) + mixed
        resid_ref[rows, :] = resid
        normed_ref[rows, :] = norm_rows(resid).astype(jnp.bfloat16)
    wide = up_ref.shape[1] // RING
    for local in range(2):
        rows = slice(local * CSIZE, (local + 1) * CSIZE)

        def block(step, carry):
            units = pl.ds(pl.multiple_of(step * wide, 128), wide)
            hidden = jax.nn.gelu(
                jnp.dot(normed_ref[rows, :], up_ref[:, units], preferred_element_type=jnp.float32)
            ).astype(jnp.bfloat16)
            resid_ref[rows, :] += jnp.dot(hidden, down_ref[units, :], preferred_element_type=jnp.float32)
            return carry

        lax.fori_loop(0, RING, block, 0)
        result = resid_ref[rows, :].astype(jnp.bfloat16)
        for j in range(RING):
            staged[j, rows, :] = result[:, features * j : features * (j + 1)]
        target = out_ref.at[pl.ds(x * 2 * CSIZE + local * CSIZE, CSIZE)]
        for step in (2, 1, 3):
            send(
                staged.at[place(x, step), rows], target,
                out_send.at[local, step - 1], out_recv.at[local, step - 1], across(step),
            )
        out_copies.append(load(staged.at[x, rows], target, out_own.at[local]))
    for local in range(2):
        for step in (1, 2, 3):
            source = place(x, -step)
            arrived(out_ref.at[pl.ds(source * 2 * CSIZE + local * CSIZE, CSIZE)], out_recv.at[local, step - 1])
    for copy in out_copies:
        copy.wait()
    for copy in sent:
        copy.wait_send()


def tail(parts, logs, nodes, out_weight, up_weight, down_weight):
    any_space = pl.BlockSpec(memory_space=pl.ANY)
    dma, vmem = pltpu.SemaphoreType.DMA, pltpu.VMEM
    width = nodes.shape[1]
    features = 2 * PLAN_FEATURES
    return pl.pallas_call(
        tail_kernel,
        out_shape=jax.ShapeDtypeStruct((nodes.shape[0], features), jnp.bfloat16),
        in_specs=[any_space] * 6,
        out_specs=any_space,
        scratch_shapes=[
            vmem(out_weight.shape, jnp.bfloat16),
            vmem(up_weight.shape, jnp.bfloat16),
            vmem(down_weight.shape, jnp.bfloat16),
            vmem((2 * CSIZE, width), jnp.bfloat16),
            vmem((2, 3, LOCAL, PLAN_FEATURES, CSIZE), jnp.bfloat16),
            vmem((2, 3, RING, 8, CSIZE), jnp.float32),
            vmem((2, LOCAL, PLAN_FEATURES, CSIZE), jnp.bfloat16),
            vmem((2, RING, 8, CSIZE), jnp.float32),
            vmem((RING, 2, features, CSIZE), jnp.bfloat16),
            vmem((2, width, CSIZE), jnp.bfloat16),
            vmem((2 * CSIZE, width), jnp.float32),
            vmem((2 * CSIZE, width), jnp.bfloat16),
            vmem((RING, 2 * CSIZE, features), jnp.bfloat16),
            dma((4,)), dma((2, 2)), dma((2, 3, 4)), dma((2, 3, 4)), dma((2, 3, 4)), dma((2, 3, 4)),
            dma((3,)), dma((3,)), dma((2, 3)), dma((2, 3)), dma((2,)),
        ],
        compiler_params=pltpu.CompilerParams(
            collective_id=1, has_side_effects=True, vmem_limit_bytes=56 * 2**20
        ),
        name="tail",
    )(parts, logs, nodes, out_weight, up_weight, down_weight)


def tile_list(key_owner, key_local, query_owner, query_local):
    z, y, c = coordinates()
    key_owner, query_owner = key_owner.reshape(8, 128), query_owner.reshape(8, 128)
    key_local, query_local = key_local.reshape(8, 128), query_local.reshape(8, 128)
    qz, qy, qc = query_owner // 8, query_owner // 2 % 4, query_owner % 2
    kz, ky, kc = key_owner // 8, key_owner // 2 % 4, key_owner % 2
    number = jnp.arange(1024, dtype=jnp.int32).reshape(8, 128)
    mine_a = (qy == y) & (qc == c) & (kz == z)
    mine_b = (qz == z) & (qc == c) & (ky == y)
    item_a = (qz * 8 + query_local) + ((ky * 16 + kc * 8 + key_local) << 7) + (number << 14)
    item_b = (32 + qy * 8 + query_local) + ((64 + kz * 16 + kc * 8 + key_local) << 7) + (number << 14)
    mine = jnp.concatenate([mine_a, mine_b], 0)
    items = jnp.concatenate([item_a, item_b], 0)
    ones = mine.astype(jnp.float32)
    lane = jnp.arange(128)
    row = jnp.arange(16)
    inside = jnp.dot(ones, (lane[:, None] < lane[None, :]).astype(jnp.float32))
    counts = jnp.sum(ones, axis=1)
    filler = -jnp.sum(counts[:8]).astype(jnp.int32) % UNROLL
    ahead = jnp.sum(jnp.where(row[None, :] < row[:, None], counts[None, :], 0.0), axis=1)
    rank = (inside + ahead[:, None]).astype(jnp.int32) + 16
    rank = rank + jnp.where(row[:, None] < 8, 0, filler)
    rank = jnp.where(mine, rank, -1).reshape(2048)
    own = jnp.arange(8, dtype=jnp.int32)
    own_a = (z * 8 + own) + ((y * 16 + c * 8 + own) << 7) + (1024 << 14)
    own_b = (32 + y * 8 + own) + ((64 + z * 16 + c * 8 + own) << 7) + (1024 << 14)
    slot = jnp.arange(LIST_MAX, dtype=jnp.int32)
    total = jnp.sum(counts).astype(jnp.int32) + 16 + filler
    split = jnp.sum(counts[:8]).astype(jnp.int32) + 16 + filler
    nothing = 64 + (1024 << 14)
    listed = nothing + jnp.sum(
        jnp.where(slot[:, None] == rank[None, :], items.reshape(2048)[None, :] - nothing, 0), axis=1
    )
    return jnp.concatenate([own_a, own_b, listed[16:], split[None], total[None]])


def per_device(
    nodes, qkv_weight, out_weight, hop_bias, up_weight, down_weight,
    key_owner, key_local, query_owner, query_local, hop_bucket,
):
    items = tile_list(key_owner, key_local, query_owner, query_local)
    normed = norm_rows(nodes.astype(jnp.float32)).astype(jnp.bfloat16)
    projected = jnp.einsum("sdf,rd->sfr", qkv_weight, normed, preferred_element_type=jnp.float32)
    q_rows = (projected[0] * (LOG2E / math.sqrt(HEAD_SIZE))).astype(jnp.bfloat16)
    kv_rows = projected[1:].astype(jnp.bfloat16)
    q_blocks = q_rows.reshape(2, PLAN_FEATURES, LOCAL, CSIZE).transpose(0, 2, 1, 3)
    kv_blocks = (
        kv_rows.reshape(2, 2, PLAN_FEATURES, LOCAL, CSIZE)
        .transpose(1, 3, 0, 2, 4)
        .reshape(2, LOCAL, 2 * PLAN_FEATURES, CSIZE)
    )
    buckets = jnp.pad(hop_bucket, (0, 128 - hop_bucket.shape[0]))[None]
    q_all, kv_all, table = gather(q_blocks, kv_blocks, buckets)
    parts, logs = tiles(items, hop_bias.reshape(-1), q_blocks, kv_blocks, q_all, kv_all, table)
    return tail(
        parts.reshape(2, RING, LOCAL, PLAN_FEATURES, CSIZE), logs.reshape(2, RING, RING, 8, CSIZE),
        nodes, out_weight, up_weight, down_weight,
    )


def solution(mesh):
    placed = (
        P("owner", None), P(None, None, "head"), P(), P(None, "head"), P(), P(),
        P(), P(), P(), P(), P("owner"),
    )
    return jax.shard_map(
        per_device, mesh=mesh, in_specs=placed, out_specs=P("owner", "head"), check_vma=False
    )
```

```python
import functools
import math

import jax
import jax.numpy as jnp
from jax import lax
from jax.experimental import pallas as pl
from jax.experimental.pallas import tpu as pltpu
from jax.sharding import PartitionSpec as P

CSIZE = 256
EPSILON = 1e-05
RING = 4
LOCAL = 8
PLAN_HEADS = 3
HEAD_SIZE = 32
PLAN_FEATURES = PLAN_HEADS * HEAD_SIZE
LIST_MAX = 640
UNROLL = 4
MESH = pl.DeviceIdType.MESH
LOG2E = math.log2(math.e)
NEVER = -1e30
NOTHING = 64


def norm_rows(values):
    center = values - jnp.mean(values, axis=-1, keepdims=True)
    spread = jnp.mean(center * center, axis=-1, keepdims=True)
    return center * lax.rsqrt(spread + EPSILON)


def coordinates():
    me = lax.axis_index("owner")
    return lax.div(me, 8), lax.rem(lax.div(me, 2), 4), lax.rem(me, 2)


def place(at, step):
    return lax.rem(at + step + RING, RING)


def ring_at(axis, step):
    z, y, c = coordinates()
    if axis == "z":
        z = place(z, step)
    else:
        y = place(y, step)
    return ((z * 4 + y) * 2 + c, lax.axis_index("head"))


def sibling():
    z, y, c = coordinates()
    return ((z * 4 + y) * 2 + 1 - c, lax.axis_index("head"))


def greet(partners):
    barrier = pltpu.get_barrier_semaphore()
    for partner in partners:
        pl.semaphore_signal(barrier, inc=1, device_id=partner, device_id_type=MESH)
    pl.semaphore_wait(barrier, len(partners))


def rows(h, first=0):
    return slice(first + HEAD_SIZE * h, first + HEAD_SIZE * (h + 1))


def attend(pairs):
    heads = range(PLAN_HEADS)
    ones = jnp.ones((16, CSIZE), jnp.bfloat16)
    scored = [
        [
            lax.dot_general(key(h), query(h), (((0,), (0,)), ((), ())), preferred_element_type=jnp.float32)
            for h in heads
        ]
        for query, key, value in pairs
    ]
    done = []
    for (query, key, value), scores in zip(pairs, scored):
        highest = [jnp.max(s, axis=0, keepdims=True) for s in scores]
        weights = [jnp.exp2(s - top).astype(jnp.bfloat16) for s, top in zip(scores, highest)]
        mixed = [
            jnp.dot(jnp.concatenate([value(h), ones], 0), weights[h], preferred_element_type=jnp.float32)
            for h in heads
        ]
        done.append((highest, mixed))
    return done


def make_list(query_owner, query_local, key_owner, key_local):
    z, y, c = coordinates()
    div, rem = lax.div, lax.rem
    qz, qy, qc = div(query_owner, 8), rem(div(query_owner, 2), 4), rem(query_owner, 2)
    kz, ky, kc = div(key_owner, 8), rem(div(key_owner, 2), 4), rem(key_owner, 2)
    iota = lax.broadcasted_iota
    number = iota(jnp.int32, (8, 128), 0) * 128 + iota(jnp.int32, (8, 128), 1)
    mine_a = (qy == y) & (qc == c) & (kz == z)
    mine_b = (qz == z) & (qc == c) & (ky == y)
    item_a = (qz * 8 + query_local) + (ky * 16 + kc * 8 + key_local) * 128 + number * 16384
    item_b = (32 + qy * 8 + query_local) + (64 + kz * 16 + kc * 8 + key_local) * 128 + number * 16384
    zero, one = jnp.zeros((8, 128), jnp.float32), jnp.ones((8, 128), jnp.float32)
    ones = jnp.concatenate([jnp.where(mine_a, one, zero), jnp.where(mine_b, one, zero)], 0)
    items = jnp.concatenate([item_a, item_b], 0).astype(jnp.float32)
    before = jnp.where(iota(jnp.int32, (128, 128), 0) < iota(jnp.int32, (128, 128), 1), 1.0, 0.0)
    inside = jnp.dot(ones, before, preferred_element_type=jnp.float32)
    counts = jnp.sum(ones, axis=1, keepdims=True)
    row = iota(jnp.int32, (16, 128), 0)
    wide = jnp.broadcast_to(counts, (16, 128))
    first = jnp.sum(jnp.where(row < 8, wide, 0.0), axis=0, keepdims=True)
    filled = jnp.floor((first + (UNROLL - 1)) * (1.0 / UNROLL)) * UNROLL
    total = filled + jnp.sum(jnp.where(row >= 8, wide, 0.0), axis=0, keepdims=True)
    ahead = [jnp.zeros((1, 128), jnp.float32)]
    for r in range(15):
        ahead.append(ahead[-1] + wide[r : r + 1] if r != 7 else filled)
    rank = jnp.where(ones > 0, inside + jnp.concatenate(ahead, 0), -1.0).T
    values = items.T - NOTHING
    place = iota(jnp.int32, (128, LIST_MAX), 1).astype(jnp.float32)
    listed = jnp.zeros((128, LIST_MAX), jnp.float32)
    for r in range(16):
        listed += jnp.where(rank[:, r : r + 1] == place, values[:, r : r + 1], 0.0)
    listed = jnp.sum(listed, axis=0, keepdims=True) + NOTHING
    at = iota(jnp.int32, (1, LIST_MAX), 1)
    repeat = lambda v: jnp.concatenate([v] * (LIST_MAX // 128), 1)
    listed = jnp.where(at == LIST_MAX - 2, repeat(filled), listed)
    listed = jnp.where(at == LIST_MAX - 1, repeat(total), listed)
    return listed.astype(jnp.int32)


def gather_kernel(
    nodes_hbm, weight_hbm, bias_ref, bucket_ref, ko_ref, kl_ref, qo_ref, ql_ref,
    qg_ref, kvg_ref, table_ref, list_out, m_out, l_out, acc_out,
    nodes_ref, weight_ref, turned_ref, q_ref, kv_ref, bucket_row, list_ref, m_ref, l_ref, acc_ref,
    ring_send, ring_recv, pair_send, pair_recv, table_send, table_recv, own_sem, load_sem, weight_sem, store_sem,
):
    z, y, c = coordinates()
    half = LOCAL // 2
    heads = range(PLAN_HEADS)

    def local_copy(source, target, sem):
        copy = pltpu.make_async_copy(source, target, sem)
        copy.start()
        return copy

    weight_loads = [local_copy(weight_hbm.at[i], weight_ref.at[i], weight_sem.at[i]) for i in range(3)]
    node_rows = lambda h: pl.ds(h * half * CSIZE, half * CSIZE)
    node_loads = [local_copy(nodes_hbm.at[node_rows(h)], nodes_ref.at[node_rows(h)], load_sem.at[h]) for h in range(2)]
    bucket_row[...] = jnp.zeros(bucket_row.shape, jnp.int32)
    bucket_row[:, : bucket_ref.shape[1]] = bucket_ref[...]
    stores = [local_copy(bucket_row, table_ref.at[c, z, y], store_sem.at[4])]
    greet([ring_at(axis, step) for axis in "zy" for step in (1, 2, 3)] + [sibling()])
    sent = []

    def part(h):
        return pl.ds(h * half, half)

    streams = []
    for plan in range(2):
        q_axis, kv_axis = ("z", "y") if plan == 0 else ("y", "z")
        for kind, axis in (("kv", kv_axis), ("q", q_axis)):
            at = z if axis == "z" else y
            if kind == "q":
                source = lambda h, plan=plan: q_ref.at[plan, part(h)]
                slot = lambda p, h, plan=plan: qg_ref.at[plan, p, part(h)]
            else:
                source = lambda h, plan=plan: kv_ref.at[plan, part(h)]
                slot = lambda p, h, plan=plan: kvg_ref.at[plan, p, c, part(h)]
            streams.append((len(streams), plan, kind, axis, at, source, slot))

    def send(src, dst, send_sem, recv_sem, device):
        copy = pltpu.make_async_remote_copy(
            src_ref=src, dst_ref=dst, send_sem=send_sem, recv_sem=recv_sem,
            device_id=device, device_id_type=MESH,
        )
        copy.start()
        sent.append(copy)

    def arrived(ref, sem):
        pltpu.make_async_remote_copy(
            src_ref=ref, dst_ref=ref, send_sem=ring_send.at[0, 0], recv_sem=sem,
            device_id=sibling(), device_id_type=MESH,
        ).wait_recv()

    for step in (1, 2, 3):
        send(bucket_row, table_ref.at[c, z, y], table_send.at[step - 1], table_recv.at[step - 1], ring_at("y", step))
    for copy in weight_loads:
        copy.wait()
    for i in range(3):
        turned_ref[i] = weight_ref[i].T
    features = 2 * PLAN_FEATURES

    def project(cluster, carry):
        normed = norm_rows(nodes_ref[pl.ds(cluster * CSIZE, CSIZE), :].astype(jnp.float32)).astype(jnp.bfloat16)
        for i in range(3):
            projected = lax.dot_general(
                turned_ref[i], normed, (((1,), (1,)), ((), ())), preferred_element_type=jnp.float32
            )
            if i == 0:
                projected = projected * (LOG2E / math.sqrt(HEAD_SIZE))
            projected = projected.astype(jnp.bfloat16)
            for plan in range(2):
                block = projected[plan * PLAN_FEATURES : (plan + 1) * PLAN_FEATURES]
                if i == 0:
                    q_ref[plan, cluster] = block
                else:
                    kv_ref[plan, cluster, (i - 1) * PLAN_FEATURES : i * PLAN_FEATURES, :] = block
        return carry

    for h in range(2):
        node_loads[h].wait()
        lax.fori_loop(h * half, (h + 1) * half, project, 0)
        for wanted in ("kv", "q"):
            for number, plan, kind, axis, at, source, slot in streams:
                if kind == wanted:
                    send(source(h), slot(at, h), ring_send.at[number, h], ring_recv.at[number, h], ring_at(axis, 1))
                    send(source(h), slot(at, h), ring_send.at[number, 2 + h], ring_recv.at[number, 2 + h], ring_at(axis, -1))
        for number, plan, kind, axis, at, source, slot in streams:
            if kind == "kv":
                send(source(h), slot(at, h), pair_send.at[plan, h], pair_recv.at[plan, h], sibling())
            stores.append(local_copy(source(h), slot(at, h), own_sem.at[number, h]))
    list_ref[...] = make_list(qo_ref[...], ql_ref[...], ko_ref[...], kl_ref[...])
    stores.append(local_copy(list_ref, list_out, store_sem.at[0]))

    for plan in range(2):
        bias = [bias_ref[plan * PLAN_HEADS + h] * LOG2E for h in heads]

        def own_tiles(step, carry):
            group = [step * UNROLL + u for u in range(UNROLL)]
            pairs = [
                (
                    lambda h, i=i: q_ref[plan, i, rows(h), :],
                    lambda h, i=i: kv_ref[plan, i, rows(h), :],
                    lambda h, i=i: kv_ref[plan, i, rows(h, PLAN_FEATURES), :],
                )
                for i in group
            ]
            for i, (highest, mixed) in zip(group, attend(pairs)):
                for h in heads:
                    m_ref[plan, i, h : h + 1, :] = highest[h] + bias[h]
                    l_ref[plan, i, h : h + 1, :] = mixed[h][HEAD_SIZE : HEAD_SIZE + 1]
                    acc_ref[plan, i, rows(h), :] = mixed[h][:HEAD_SIZE]
            return carry

        lax.fori_loop(0, LOCAL // UNROLL, own_tiles, 0)
    stores.append(local_copy(m_ref, m_out, store_sem.at[1]))
    stores.append(local_copy(l_ref, l_out, store_sem.at[2]))
    stores.append(local_copy(acc_ref, acc_out, store_sem.at[3]))
    stores[0].wait()
    for step in (1, 2, 3):
        arrived(table_ref.at[c, z, place(y, -step)], table_recv.at[step - 1])
    for step in (1, 2, 3):
        send(table_ref.at[c, z], table_ref.at[c, z], table_send.at[2 + step], table_recv.at[2 + step], ring_at("z", step))
    for number, plan, kind, axis, at, source, slot in streams:
        before, after = slot(place(at, -1), 0), slot(place(at, 1), 1)
        arrived(before, ring_recv.at[number, 0])
        send(before, before, ring_send.at[number, 4], ring_recv.at[number, 4], ring_at(axis, 1))
        arrived(after, ring_recv.at[number, 3])
        send(after, after, ring_send.at[number, 5], ring_recv.at[number, 5], ring_at(axis, -1))
        if kind == "kv":
            send(before, before, pair_send.at[plan, 2], pair_recv.at[plan, 2], sibling())
            send(after, after, pair_send.at[plan, 5], pair_recv.at[plan, 5], sibling())
    for step in (1, 2, 3):
        arrived(table_ref.at[c, place(z, -step)], table_recv.at[2 + step])
    send(table_ref.at[c], table_ref.at[c], table_send.at[6], table_recv.at[6], sibling())
    for number, plan, kind, axis, at, source, slot in streams:
        before, after = slot(place(at, -1), 1), slot(place(at, 1), 0)
        arrived(before, ring_recv.at[number, 1])
        arrived(after, ring_recv.at[number, 2])
        if kind == "kv":
            send(before, before, pair_send.at[plan, 3], pair_recv.at[plan, 3], sibling())
            send(after, after, pair_send.at[plan, 4], pair_recv.at[plan, 4], sibling())
    for number, plan, kind, axis, at, source, slot in streams:
        for h in range(2):
            far = slot(place(at, 2), h)
            arrived(far, ring_recv.at[number, 4 + h])
            if kind == "kv":
                send(far, far, pair_send.at[plan, 6 + h], pair_recv.at[plan, 6 + h], sibling())
    for number, plan, kind, axis, at, source, slot in streams:
        if kind == "kv":
            for index, step in enumerate((0, -1, 1, 2)):
                for h in range(2):
                    arrived(kvg_ref.at[plan, place(at, step), 1 - c, part(h)], pair_recv.at[plan, 2 * index + h])
    arrived(table_ref.at[1 - c], table_recv.at[6])
    for copy in stores[1:]:
        copy.wait()
    for copy in sent:
        copy.wait_send()


def gather(nodes, qkv_weight, bias, bucket, key_owner, key_local, query_owner, query_local):
    any_space, in_vmem = pl.BlockSpec(memory_space=pl.ANY), pl.BlockSpec(memory_space=pltpu.VMEM)
    dma, vmem = pltpu.SemaphoreType.DMA, pltpu.VMEM
    shape = jax.ShapeDtypeStruct
    q_shape, kv_shape = (PLAN_FEATURES, CSIZE), (2 * PLAN_FEATURES, CSIZE)
    m_shape, acc_shape = (2, LOCAL, 8, CSIZE), (2, LOCAL, PLAN_FEATURES, CSIZE)
    return pl.pallas_call(
        gather_kernel,
        out_shape=[
            shape((2, RING, LOCAL) + q_shape, jnp.bfloat16),
            shape((2, RING, 2, LOCAL) + kv_shape, jnp.bfloat16),
            shape((2, RING, RING, 1, 128), jnp.int32),
            shape((1, LIST_MAX), jnp.int32),
            shape(m_shape, jnp.float32),
            shape(m_shape, jnp.float32),
            shape(acc_shape, jnp.float32),
        ],
        in_specs=[any_space] * 2 + [pl.BlockSpec(memory_space=pltpu.SMEM)] + [in_vmem] * 5,
        out_specs=[any_space] * 7,
        scratch_shapes=[
            vmem(nodes.shape, jnp.bfloat16),
            vmem(qkv_weight.shape, jnp.bfloat16),
            vmem((3, qkv_weight.shape[2], qkv_weight.shape[1]), jnp.bfloat16),
            vmem((2, LOCAL) + q_shape, jnp.bfloat16),
            vmem((2, LOCAL) + kv_shape, jnp.bfloat16),
            vmem((1, 128), jnp.int32),
            vmem((1, LIST_MAX), jnp.int32),
            vmem(m_shape, jnp.float32),
            vmem(m_shape, jnp.float32),
            vmem(acc_shape, jnp.float32),
            dma((4, 6)), dma((4, 6)), dma((2, 8)), dma((2, 8)), dma((7,)), dma((7,)),
            dma((4, 2)), dma((2,)), dma((3,)), dma((5,)),
        ],
        compiler_params=pltpu.CompilerParams(
            collective_id=0, has_side_effects=True, vmem_limit_bytes=56 * 2**20
        ),
        name="gather",
    )(nodes, qkv_weight, bias, bucket, key_owner, key_local, query_owner, query_local)


def tile_kernel(
    bias_ref, list_hbm, table_hbm, m_hbm, l_hbm, acc_hbm, qg_ref, kvg_ref, part_ref, log_ref,
    q_ref, kv_ref, list_ref, table_ref, m_ref, l_ref, acc_ref, q_sem, kv_sem, table_sem, state_sem,
):
    heads = range(PLAN_HEADS)
    z, y, c = coordinates()
    queries = part_ref.shape[0]
    keys = 2 * queries
    waits = ([], [])

    def load(plan, source, target, sem):
        copy = pltpu.make_async_copy(source, target, sem)
        copy.start()
        waits[plan].append(copy)

    load(0, list_hbm, list_ref, table_sem.at[0])
    load(0, table_hbm, table_ref, table_sem.at[1])
    for plan in range(2):
        side = pl.ds(plan * queries // 2, queries // 2)
        load(plan, qg_ref.at[side], q_ref.at[side], q_sem.at[plan])
        side = pl.ds(plan * keys // 2, keys // 2)
        load(plan, kvg_ref.at[side], kv_ref.at[side], kv_sem.at[plan])
    for plan in range(2):
        own = (z if plan == 0 else y) + plan * RING

        def clear(group, carry):
            @pl.when(group != own)
            def _():
                side = pl.ds(group * LOCAL, LOCAL)
                m_ref[side] = jnp.full((LOCAL, 8, CSIZE), NEVER, jnp.float32)
                l_ref[side] = jnp.zeros((LOCAL, 8, CSIZE), jnp.float32)
                acc_ref[side] = jnp.zeros((LOCAL, PLAN_FEATURES, CSIZE), jnp.float32)
            return carry

        side = pl.ds(own * LOCAL, LOCAL)
        load(plan, m_hbm.at[plan], m_ref.at[side], state_sem.at[plan, 0])
        load(plan, l_hbm.at[plan], l_ref.at[side], state_sem.at[plan, 1])
        load(plan, acc_hbm.at[plan], acc_ref.at[side], state_sem.at[plan, 2])
        lax.fori_loop(plan * RING, (plan + 1) * RING, clear, 0)
    m_ref[queries] = jnp.full((8, CSIZE), NEVER, jnp.float32)
    l_ref[queries] = jnp.zeros((8, CSIZE), jnp.float32)
    acc_ref[queries] = jnp.zeros((PLAN_FEATURES, CSIZE), jnp.float32)

    def batch(step, carry):
        items, pairs = [], []
        for u in range(UNROLL):
            item = list_ref[0, step * UNROLL + u]
            state = lax.bitwise_and(item, 127)
            key = lax.bitwise_and(lax.shift_right_logical(item, 7), 127)
            tile = lax.shift_right_logical(item, 14)
            query = jnp.minimum(state, queries - 1)
            worker = lax.shift_right_logical(tile, 5)
            bucket = table_ref[
                lax.bitwise_and(worker, 1), lax.shift_right_logical(worker, 3),
                lax.bitwise_and(lax.shift_right_logical(worker, 1), 3), 0, lax.bitwise_and(tile, 31),
            ]
            first = bucket * (2 * PLAN_HEADS) + jnp.where(key >= keys // 2, PLAN_HEADS, 0)
            items.append((state, [bias_ref[first + h] * LOG2E for h in heads]))
            pairs.append((
                lambda h, i=query: q_ref[i, rows(h), :],
                lambda h, i=key: kv_ref[i, rows(h), :],
                lambda h, i=key: kv_ref[i, rows(h, PLAN_FEATURES), :],
            ))
        for (state, bias), (highest, mixed) in zip(items, attend(pairs)):
            tops = [top + b for top, b in zip(highest, bias)]
            old_m = [m_ref[state, h : h + 1, :] for h in heads]
            old_l = [l_ref[state, h : h + 1, :] for h in heads]
            old_acc = [acc_ref[state, rows(h), :] for h in heads]
            new_m = [jnp.maximum(a, b) for a, b in zip(old_m, tops)]
            keep = [jnp.exp2(a - b) for a, b in zip(old_m, new_m)]
            fresh = [jnp.exp2(a - b) for a, b in zip(tops, new_m)]
            for h in heads:
                m_ref[state, h : h + 1, :] = new_m[h]
                l_ref[state, h : h + 1, :] = old_l[h] * keep[h] + mixed[h][HEAD_SIZE : HEAD_SIZE + 1] * fresh[h]
                acc_ref[state, rows(h), :] = old_acc[h] * keep[h] + mixed[h][:HEAD_SIZE] * fresh[h]
        return carry

    for copy in waits[0]:
        copy.wait()
    split = lax.div(list_ref[0, LIST_MAX - 2], UNROLL)
    lax.fori_loop(0, split, batch, 0)
    for copy in waits[1]:
        copy.wait()
    lax.fori_loop(split, lax.div(list_ref[0, LIST_MAX - 1] + UNROLL - 1, UNROLL), batch, 0)

    def finish(group, carry):
        for local in range(LOCAL):
            state = group * LOCAL + local
            for h in heads:
                total = l_ref[state, h : h + 1, :]
                held = total > 0
                safe = jnp.where(held, total, 1.0)
                part_ref[group * LOCAL + local % 2 * RING + local // 2, rows(h), :] = (acc_ref[state, rows(h), :] * (1.0 / safe)).astype(jnp.bfloat16)
                row = local // 2 * PLAN_HEADS + h
                log_ref[group, local % 2, row : row + 1, :] = m_ref[state, h : h + 1, :] + jnp.log2(safe)
        return carry

    lax.fori_loop(0, queries // LOCAL, finish, 0)


def tiles(bias, items, table, m, l, acc, q_all, kv_all):
    queries, keys = 2 * RING * LOCAL, 2 * RING * 2 * LOCAL
    any_space = pl.BlockSpec(memory_space=pl.ANY)
    whole = lambda shape: pl.BlockSpec(shape, lambda i, *_: (0,) * len(shape))
    part_shape = (queries, PLAN_FEATURES, CSIZE)
    log_shape = (2 * RING, 2, 16, CSIZE)
    dma, vmem = pltpu.SemaphoreType.DMA, pltpu.VMEM
    return pl.pallas_call(
        tile_kernel,
        grid_spec=pltpu.PrefetchScalarGridSpec(
            num_scalar_prefetch=1,
            grid=(1,),
            in_specs=[any_space] * 7,
            out_specs=[whole(part_shape), whole(log_shape)],
            scratch_shapes=[
                vmem((queries, PLAN_FEATURES, CSIZE), jnp.bfloat16),
                vmem((keys, 2 * PLAN_FEATURES, CSIZE), jnp.bfloat16),
                pltpu.SMEM((1, LIST_MAX), jnp.int32),
                pltpu.SMEM((2, RING, RING, 1, 128), jnp.int32),
                vmem((queries + 1, 8, CSIZE), jnp.float32),
                vmem((queries + 1, 8, CSIZE), jnp.float32),
                vmem((queries + 1, PLAN_FEATURES, CSIZE), jnp.float32),
                dma((2,)), dma((2,)), dma((2,)), dma((2, 3)),
            ],
        ),
        out_shape=[
            jax.ShapeDtypeStruct(part_shape, jnp.bfloat16),
            jax.ShapeDtypeStruct(log_shape, jnp.float32),
        ],
        compiler_params=pltpu.CompilerParams(vmem_limit_bytes=56 * 2**20),
        name="tiles",
    )(
        bias, items, table, m, l, acc,
        q_all.reshape(queries, PLAN_FEATURES, CSIZE), kv_all.reshape(keys, 2 * PLAN_FEATURES, CSIZE),
    )


def tail_kernel(
    part_ref, log_ref, nodes_ref, wo_hbm, up_hbm, down_hbm, out_ref,
    wo_ref, up_ref, down_ref, rows_ref, part_in, log_in, own_part, own_log, merged, gathered, resid_ref, normed_ref, staged,
    weight_sem, own_sem, part_send, part_recv, log_send, log_recv, x_send, x_recv, out_send, out_recv, out_own,
):
    z, y, c = coordinates()
    me = lax.axis_index("owner")
    x = lax.axis_index("head")
    heads = range(PLAN_HEADS)
    features = 2 * PLAN_FEATURES

    def load(source, target, sem):
        copy = pltpu.make_async_copy(source, target, sem)
        copy.start()
        return copy

    def across(step):
        return (me, place(x, step))

    ready = []
    for plan in range(2):
        at = z if plan == 0 else y
        ready.append(load(part_ref.at[plan, at], own_part.at[plan], own_sem.at[plan, 0]))
        ready.append(load(log_ref.at[plan, at], own_log.at[plan], own_sem.at[plan, 1]))
    weights = [
        load(nodes_ref.at[pl.ds(x * 2 * CSIZE, 2 * CSIZE)], rows_ref, weight_sem.at[0]),
        load(wo_hbm, wo_ref, weight_sem.at[1]),
        load(up_hbm, up_ref, weight_sem.at[2]),
        load(down_hbm, down_ref, weight_sem.at[3]),
    ]
    greet([ring_at(axis, step) for axis in "zy" for step in (1, 2, 3)] + [across(step) for step in (1, 2, 3)])
    sent = []

    def send(src, dst, send_sem, recv_sem, device):
        copy = pltpu.make_async_remote_copy(
            src_ref=src, dst_ref=dst, send_sem=send_sem, recv_sem=recv_sem,
            device_id=device, device_id_type=MESH,
        )
        copy.start()
        sent.append(copy)

    def arrived(ref, sem):
        pltpu.make_async_remote_copy(
            src_ref=ref, dst_ref=ref, send_sem=x_send.at[0, 0], recv_sem=sem,
            device_id=across(1), device_id_type=MESH,
        ).wait_recv()

    for turn in range(2):
        for plan, axis in enumerate("zy"):
            at = z if plan == 0 else y
            for step in (2, 1, 3):
                to = place(at, step)
                send(
                    part_ref.at[plan, to, turn], part_in.at[plan, step - 1, turn],
                    part_send.at[plan, step - 1, turn], part_recv.at[plan, step - 1, turn], ring_at(axis, step),
                )
                send(
                    log_ref.at[plan, to, turn], log_in.at[plan, step - 1, turn],
                    log_send.at[plan, step - 1, turn], log_recv.at[plan, step - 1, turn], ring_at(axis, step),
                )
    for copy in ready:
        copy.wait()
    mine = pl.ds(pl.multiple_of(x * features, 64), features)

    def merge(turn):
        for plan in range(2):
            for step in (2, 1, 3):
                arrived(part_in.at[plan, step - 1, turn], part_recv.at[plan, step - 1, turn])
                arrived(log_in.at[plan, step - 1, turn], log_recv.at[plan, step - 1, turn])
        for plan in range(2):
            logs = [own_log[plan, turn]] + [log_in[plan, i, turn] for i in range(3)]
            best = jnp.maximum(jnp.maximum(logs[0], logs[1]), jnp.maximum(logs[2], logs[3]))
            shares = [jnp.exp2(log - best) for log in logs]
            scale = 1.0 / (shares[0] + shares[1] + shares[2] + shares[3])
            shares = [share * scale for share in shares]
            for to in range(RING):
                for h in heads:
                    row = to * PLAN_HEADS + h
                    total = own_part[plan, turn, to, rows(h), :].astype(jnp.float32) * shares[0][row : row + 1]
                    for i in range(3):
                        total += part_in[plan, i, turn, to, rows(h), :].astype(jnp.float32) * shares[i + 1][row : row + 1]
                    merged[turn, to, rows(h, plan * PLAN_FEATURES), :] = total.astype(jnp.bfloat16)
        for step in (2, 1, 3):
            send(
                merged.at[turn, place(x, step)], gathered.at[turn, mine],
                x_send.at[turn, step - 1], x_recv.at[turn, step - 1], across(step),
            )
        gathered[turn, mine, :] = merged[turn, x]

    wide = up_ref.shape[1] // RING
    out_copies = []

    def begin(turn):
        part = slice(turn * CSIZE, (turn + 1) * CSIZE)
        for step in (1, 2, 3):
            source = place(x, -step)
            arrived(gathered.at[turn, pl.ds(pl.multiple_of(source * features, 64), features)], x_recv.at[turn, step - 1])
        mixed = lax.dot_general(
            gathered[turn], wo_ref[...], (((0,), (0,)), ((), ())), preferred_element_type=jnp.float32
        )
        resid = rows_ref[part, :].astype(jnp.float32) + mixed
        resid_ref[part, :] = resid
        normed_ref[part, :] = norm_rows(resid).astype(jnp.bfloat16)

    def feed(turn, first, last):
        part = slice(turn * CSIZE, (turn + 1) * CSIZE)

        def block(step, carry):
            units = pl.ds(pl.multiple_of(step * wide, 128), wide)
            hidden = jax.nn.gelu(
                jnp.dot(normed_ref[part, :], up_ref[:, units], preferred_element_type=jnp.float32)
            ).astype(jnp.bfloat16)
            resid_ref[part, :] += jnp.dot(hidden, down_ref[units, :], preferred_element_type=jnp.float32)
            return carry

        lax.fori_loop(first, last, block, 0)

    def hand_out(turn):
        part = slice(turn * CSIZE, (turn + 1) * CSIZE)
        result = resid_ref[part, :].astype(jnp.bfloat16)
        for j in range(RING):
            staged[j, part, :] = result[:, features * j : features * (j + 1)]
        target = out_ref.at[pl.ds((x * 2 + turn) * CSIZE, CSIZE)]
        for step in (2, 1, 3):
            send(
                staged.at[place(x, step), part], target,
                out_send.at[turn, step - 1], out_recv.at[turn, step - 1], across(step),
            )
        out_copies.append(load(staged.at[x, part], target, out_own.at[turn]))

    merge(0)
    for copy in weights:
        copy.wait()
    begin(0)
    feed(0, 0, 2)
    merge(1)
    feed(0, 2, RING)
    hand_out(0)
    begin(1)
    feed(1, 0, RING)
    hand_out(1)
    for turn in range(2):
        for step in (1, 2, 3):
            source = place(x, -step)
            arrived(out_ref.at[pl.ds((source * 2 + turn) * CSIZE, CSIZE)], out_recv.at[turn, step - 1])
    for copy in out_copies:
        copy.wait()
    for copy in sent:
        copy.wait_send()


def tail(parts, logs, nodes, out_weight, up_weight, down_weight):
    any_space = pl.BlockSpec(memory_space=pl.ANY)
    dma, vmem = pltpu.SemaphoreType.DMA, pltpu.VMEM
    width = nodes.shape[1]
    features = 2 * PLAN_FEATURES
    return pl.pallas_call(
        tail_kernel,
        out_shape=jax.ShapeDtypeStruct((nodes.shape[0], features), jnp.bfloat16),
        in_specs=[any_space] * 6,
        out_specs=any_space,
        scratch_shapes=[
            vmem(out_weight.shape, jnp.bfloat16),
            vmem(up_weight.shape, jnp.bfloat16),
            vmem(down_weight.shape, jnp.bfloat16),
            vmem((2 * CSIZE, width), jnp.bfloat16),
            vmem((2, 3, 2, RING, PLAN_FEATURES, CSIZE), jnp.bfloat16),
            vmem((2, 3, 2, 16, CSIZE), jnp.float32),
            vmem((2, 2, RING, PLAN_FEATURES, CSIZE), jnp.bfloat16),
            vmem((2, 2, 16, CSIZE), jnp.float32),
            vmem((2, RING, features, CSIZE), jnp.bfloat16),
            vmem((2, width, CSIZE), jnp.bfloat16),
            vmem((2 * CSIZE, width), jnp.float32),
            vmem((2 * CSIZE, width), jnp.bfloat16),
            vmem((RING, 2 * CSIZE, features), jnp.bfloat16),
            dma((4,)), dma((2, 2)), dma((2, 3, 2)), dma((2, 3, 2)), dma((2, 3, 2)), dma((2, 3, 2)),
            dma((2, 3)), dma((2, 3)), dma((2, 3)), dma((2, 3)), dma((2,)),
        ],
        compiler_params=pltpu.CompilerParams(
            collective_id=1, has_side_effects=True, vmem_limit_bytes=56 * 2**20
        ),
        name="tail",
    )(parts, logs, nodes, out_weight, up_weight, down_weight)


def per_device(
    nodes, qkv_weight, out_weight, hop_bias, up_weight, down_weight,
    key_owner, key_local, query_owner, query_local, hop_bucket,
):
    bias = hop_bias.reshape(-1)
    lists = [array.reshape(8, 128) for array in (key_owner, key_local, query_owner, query_local)]
    q_all, kv_all, table, items, m, l, acc = gather(
        nodes, qkv_weight, bias, hop_bucket.reshape(1, -1), *lists
    )
    parts, logs = tiles(bias, items, table, m, l, acc, q_all, kv_all)
    return tail(
        parts.reshape(2, RING, 2, RING, PLAN_FEATURES, CSIZE), logs.reshape(2, RING, 2, 16, CSIZE),
        nodes, out_weight, up_weight, down_weight,
    )


def solution(mesh):
    placed = (
        P("owner", None), P(None, None, "head"), P(), P(None, "head"), P(), P(),
        P(), P(), P(), P(), P("owner"),
    )
    return jax.shard_map(
        per_device, mesh=mesh, in_specs=placed, out_specs=P("owner", "head"), check_vma=False
    )
```

```python
import functools
import math

import jax
import jax.numpy as jnp
from jax import lax
from jax.experimental import pallas as pl
from jax.experimental.pallas import tpu as pltpu
from jax.sharding import PartitionSpec as P

CSIZE = 256
EPSILON = 1e-05
RING = 4
LOCAL = 8
PLAN_HEADS = 3
HEAD_SIZE = 32
PLAN_FEATURES = PLAN_HEADS * HEAD_SIZE
LIST_MAX = 640
UNROLL = 4
MESH = pl.DeviceIdType.MESH
LOG2E = math.log2(math.e)
NEVER = -1e30
NOTHING = 64
PIECES = 4


def norm_rows(values):
    center = values - jnp.mean(values, axis=-1, keepdims=True)
    spread = jnp.mean(center * center, axis=-1, keepdims=True)
    return center * lax.rsqrt(spread + EPSILON)


def coordinates():
    me = lax.axis_index("owner")
    return lax.div(me, 8), lax.rem(lax.div(me, 2), 4), lax.rem(me, 2)


def place(at, step):
    return lax.rem(at + step + RING, RING)


def ring_at(axis, step):
    z, y, c = coordinates()
    if axis == "z":
        z = place(z, step)
    else:
        y = place(y, step)
    return ((z * 4 + y) * 2 + c, lax.axis_index("head"))


def sibling():
    z, y, c = coordinates()
    return ((z * 4 + y) * 2 + 1 - c, lax.axis_index("head"))


def greet(partners):
    for partner in partners:
        pl.semaphore_signal(pltpu.get_barrier_semaphore(), inc=1, device_id=partner, device_id_type=MESH)


def greeted(partners):
    pl.semaphore_wait(pltpu.get_barrier_semaphore(), len(partners))


def rows(h, first=0):
    return slice(first + HEAD_SIZE * h, first + HEAD_SIZE * (h + 1))


def attend(pairs):
    heads = range(PLAN_HEADS)
    ones = jnp.ones((16, CSIZE), jnp.bfloat16)
    scored = [
        [
            lax.dot_general(key(h), query(h), (((0,), (0,)), ((), ())), preferred_element_type=jnp.float32)
            for h in heads
        ]
        for query, key, value in pairs
    ]
    done = []
    for (query, key, value), scores in zip(pairs, scored):
        highest = [jnp.max(s, axis=0, keepdims=True) for s in scores]
        weights = [jnp.exp2(s - top).astype(jnp.bfloat16) for s, top in zip(scores, highest)]
        mixed = [
            jnp.dot(jnp.concatenate([value(h), ones], 0), weights[h], preferred_element_type=jnp.float32)
            for h in heads
        ]
        done.append((highest, mixed))
    return done


def make_list(query_owner, query_local, key_owner, key_local):
    z, y, c = coordinates()
    div, rem = lax.div, lax.rem
    qz, qy, qc = div(query_owner, 8), rem(div(query_owner, 2), 4), rem(query_owner, 2)
    kz, ky, kc = div(key_owner, 8), rem(div(key_owner, 2), 4), rem(key_owner, 2)
    iota = lax.broadcasted_iota
    number = iota(jnp.int32, (8, 128), 0) * 128 + iota(jnp.int32, (8, 128), 1)
    mine_a = (qy == y) & (qc == c) & (kz == z)
    mine_b = (qz == z) & (qc == c) & (ky == y)
    item_a = (qz * 8 + query_local) + (ky * 16 + kc * 8 + key_local) * 128 + number * 16384
    item_b = (32 + qy * 8 + query_local) + (64 + kz * 16 + kc * 8 + key_local) * 128 + number * 16384
    zero, one = jnp.zeros((8, 128), jnp.float32), jnp.ones((8, 128), jnp.float32)
    ones = jnp.concatenate([jnp.where(mine_a, one, zero), jnp.where(mine_b, one, zero)], 0)
    items = jnp.concatenate([item_a, item_b], 0).astype(jnp.float32)
    before = jnp.where(iota(jnp.int32, (128, 128), 0) < iota(jnp.int32, (128, 128), 1), 1.0, 0.0)
    inside = jnp.dot(ones, before, preferred_element_type=jnp.float32)
    counts = jnp.sum(ones, axis=1, keepdims=True)
    row = iota(jnp.int32, (16, 128), 0)
    wide = jnp.broadcast_to(counts, (16, 128))
    first = jnp.sum(jnp.where(row < 8, wide, 0.0), axis=0, keepdims=True)
    filled = jnp.floor((first + (UNROLL - 1)) * (1.0 / UNROLL)) * UNROLL
    total = filled + jnp.sum(jnp.where(row >= 8, wide, 0.0), axis=0, keepdims=True)
    ahead = [jnp.zeros((1, 128), jnp.float32)]
    for r in range(15):
        ahead.append(ahead[-1] + wide[r : r + 1] if r != 7 else filled)
    rank = jnp.where(ones > 0, inside + jnp.concatenate(ahead, 0), -1.0).T
    values = items.T - NOTHING
    place = iota(jnp.int32, (128, LIST_MAX), 1).astype(jnp.float32)
    listed = jnp.zeros((128, LIST_MAX), jnp.float32)
    for r in range(16):
        listed += jnp.where(rank[:, r : r + 1] == place, values[:, r : r + 1], 0.0)
    listed = jnp.sum(listed, axis=0, keepdims=True) + NOTHING
    at = iota(jnp.int32, (1, LIST_MAX), 1)
    repeat = lambda v: jnp.concatenate([v] * (LIST_MAX // 128), 1)
    listed = jnp.where(at == LIST_MAX - 2, repeat(filled), listed)
    listed = jnp.where(at == LIST_MAX - 1, repeat(total), listed)
    return listed.astype(jnp.int32)


def gather_kernel(
    nodes_hbm, weight_hbm, bias_in, bucket_ref, ko_ref, kl_ref, qo_ref, ql_ref,
    qg_ref, kvg_ref, table_ref, list_out, bias_out, m_out, l_out, acc_out,
    nodes_ref, weight_ref, q_ref, kv_ref, bucket_row, list_ref, bias_ref, m_ref, l_ref, acc_ref,
    ring_send, ring_recv, pair_send, pair_recv, table_send, table_recv, own_sem, load_sem, weight_sem, store_sem,
):
    z, y, c = coordinates()
    heads = range(PLAN_HEADS)
    size = LOCAL // PIECES
    partners = [ring_at(axis, step) for axis in "zy" for step in (1, 2, 3)] + [sibling()]
    greet(partners)

    def local_copy(source, target, sem):
        copy = pltpu.make_async_copy(source, target, sem)
        copy.start()
        return copy

    node_rows = lambda p: pl.ds(p * size * CSIZE, size * CSIZE)
    load_nodes = lambda p: local_copy(nodes_hbm.at[node_rows(p)], nodes_ref.at[node_rows(p)], load_sem.at[p])
    node_loads = [load_nodes(0)]
    weight_load = local_copy(weight_hbm, weight_ref, weight_sem)
    node_loads += [load_nodes(p) for p in range(1, PIECES)]
    bucket_row[...] = jnp.zeros(bucket_row.shape, jnp.int32)
    bucket_row[:, : bucket_ref.shape[1]] = bucket_ref[...]
    for i in range(2 * PLAN_HEADS):
        bias_ref[i, :, : bias_in.shape[1]] = bias_in[i : i + 1] * LOG2E
    stores = [local_copy(bucket_row, table_ref.at[c, z, y], store_sem.at[4])]
    sent = []

    def part(p):
        return pl.ds(p * size, size)

    def side(h):
        return pl.ds(h * (LOCAL // 2), LOCAL // 2)

    streams = []
    for plan in range(2):
        q_axis, kv_axis = ("z", "y") if plan == 0 else ("y", "z")
        for kind, axis in (("kv", kv_axis), ("q", q_axis)):
            at = z if axis == "z" else y
            if kind == "q":
                source = lambda r, plan=plan: q_ref.at[plan, r]
                slot = lambda p, r, plan=plan: qg_ref.at[plan, p, r]
            else:
                source = lambda r, plan=plan: kv_ref.at[plan, r]
                slot = lambda p, r, plan=plan: kvg_ref.at[plan, p, c, r]
            streams.append((len(streams), plan, kind, axis, at, source, slot))

    def send(src, dst, send_sem, recv_sem, device):
        copy = pltpu.make_async_remote_copy(
            src_ref=src, dst_ref=dst, send_sem=send_sem, recv_sem=recv_sem,
            device_id=device, device_id_type=MESH,
        )
        copy.start()
        sent.append(copy)

    def arrived(ref, sem):
        pltpu.make_async_remote_copy(
            src_ref=ref, dst_ref=ref, send_sem=ring_send.at[0, 0], recv_sem=sem,
            device_id=sibling(), device_id_type=MESH,
        ).wait_recv()

    weight_load.wait()
    features = 2 * PLAN_FEATURES

    def project(cluster, carry):
        normed = norm_rows(nodes_ref[pl.ds(cluster * CSIZE, CSIZE), :].astype(jnp.float32)).astype(jnp.bfloat16)
        for i in range(3):
            projected = lax.dot_general(
                weight_ref[i], normed, (((1,), (1,)), ((), ())), preferred_element_type=jnp.float32
            )
            if i == 0:
                projected = projected * (LOG2E / math.sqrt(HEAD_SIZE))
            projected = projected.astype(jnp.bfloat16)
            for plan in range(2):
                block = projected[plan * PLAN_FEATURES : (plan + 1) * PLAN_FEATURES]
                if i == 0:
                    q_ref[plan, cluster] = block
                else:
                    kv_ref[plan, cluster, (i - 1) * PLAN_FEATURES : i * PLAN_FEATURES, :] = block
        return carry

    ordered = [s for s in streams if s[2] == "kv"] + [s for s in streams if s[2] == "q"]
    for p in range(PIECES):
        node_loads[p].wait()
        lax.fori_loop(p * size, (p + 1) * size, project, 0)
        if p == 0:
            greeted(partners)
            for step in (1, 2, 3):
                send(bucket_row, table_ref.at[c, z, y], table_send.at[step - 1], table_recv.at[step - 1], ring_at("y", step))
        for number, plan, kind, axis, at, source, slot in ordered:
            for way, first in ((1, 0), (-1, PIECES)):
                send(
                    source(part(p)), slot(at, part(p)),
                    ring_send.at[number, first + p], ring_recv.at[number, first + p], ring_at(axis, way),
                )
        if p % (PIECES // 2) == PIECES // 2 - 1:
            h = p // (PIECES // 2)
            for number, plan, kind, axis, at, source, slot in ordered:
                if kind == "kv":
                    send(source(side(h)), slot(at, side(h)), pair_send.at[plan, h], pair_recv.at[plan, h], sibling())
                stores.append(local_copy(source(side(h)), slot(at, side(h)), own_sem.at[number, h]))
    list_ref[...] = make_list(qo_ref[...], ql_ref[...], ko_ref[...], kl_ref[...])
    stores.append(local_copy(list_ref, list_out, store_sem.at[0]))
    stores.append(local_copy(bias_ref, bias_out, store_sem.at[5]))

    for plan in range(2):
        bias = [bias_ref[plan * PLAN_HEADS + h, :, 0:1] for h in heads]

        def own_tiles(step, carry):
            group = [step * UNROLL + u for u in range(UNROLL)]
            pairs = [
                (
                    lambda h, i=i: q_ref[plan, i, rows(h), :],
                    lambda h, i=i: kv_ref[plan, i, rows(h), :],
                    lambda h, i=i: kv_ref[plan, i, rows(h, PLAN_FEATURES), :],
                )
                for i in group
            ]
            for i, (highest, mixed) in zip(group, attend(pairs)):
                for h in heads:
                    m_ref[plan, i, h : h + 1, :] = highest[h] + bias[h]
                    l_ref[plan, i, h : h + 1, :] = mixed[h][HEAD_SIZE : HEAD_SIZE + 1]
                    acc_ref[plan, i, rows(h), :] = mixed[h][:HEAD_SIZE]
            return carry

        lax.fori_loop(0, LOCAL // UNROLL, own_tiles, 0)
    stores.append(local_copy(m_ref, m_out, store_sem.at[1]))
    stores.append(local_copy(l_ref, l_out, store_sem.at[2]))
    stores.append(local_copy(acc_ref, acc_out, store_sem.at[3]))
    stores[0].wait()
    for step in (1, 2, 3):
        arrived(table_ref.at[c, z, place(y, -step)], table_recv.at[step - 1])
    for step in (1, 2, 3):
        send(table_ref.at[c, z], table_ref.at[c, z], table_send.at[2 + step], table_recv.at[2 + step], ring_at("z", step))
    for h in range(2):
        for p in range(h * PIECES // 2, (h + 1) * PIECES // 2):
            for number, plan, kind, axis, at, source, slot in ordered:
                before, after = slot(place(at, -1), part(p)), slot(place(at, 1), part(p))
                arrived(before, ring_recv.at[number, p])
                arrived(after, ring_recv.at[number, PIECES + p])
                onward, way = (before, 1) if h == 0 else (after, -1)
                far = 2 * PIECES + p
                send(onward, onward, ring_send.at[number, far], ring_recv.at[number, far], ring_at(axis, way))
        for number, plan, kind, axis, at, source, slot in ordered:
            if kind == "kv":
                for index, step in ((1, -1), (2, 1)):
                    block, sem = slot(place(at, step), side(h)), 2 * index + h
                    send(block, block, pair_send.at[plan, sem], pair_recv.at[plan, sem], sibling())
        if h == 0:
            for step in (1, 2, 3):
                arrived(table_ref.at[c, place(z, -step)], table_recv.at[2 + step])
            send(table_ref.at[c], table_ref.at[c], table_send.at[6], table_recv.at[6], sibling())
    for h in range(2):
        for number, plan, kind, axis, at, source, slot in ordered:
            for p in range(h * PIECES // 2, (h + 1) * PIECES // 2):
                arrived(slot(place(at, 2), part(p)), ring_recv.at[number, 2 * PIECES + p])
            if kind == "kv":
                far = slot(place(at, 2), side(h))
                send(far, far, pair_send.at[plan, 6 + h], pair_recv.at[plan, 6 + h], sibling())
    for number, plan, kind, axis, at, source, slot in streams:
        if kind == "kv":
            for index, step in enumerate((0, -1, 1, 2)):
                for h in range(2):
                    arrived(kvg_ref.at[plan, place(at, step), 1 - c, side(h)], pair_recv.at[plan, 2 * index + h])
    arrived(table_ref.at[1 - c], table_recv.at[6])
    for copy in stores[1:]:
        copy.wait()
    for copy in sent:
        copy.wait_send()


def gather(nodes, qkv_weight, bias, bucket, key_owner, key_local, query_owner, query_local):
    any_space, in_vmem = pl.BlockSpec(memory_space=pl.ANY), pl.BlockSpec(memory_space=pltpu.VMEM)
    dma, vmem = pltpu.SemaphoreType.DMA, pltpu.VMEM
    shape = jax.ShapeDtypeStruct
    q_shape, kv_shape = (PLAN_FEATURES, CSIZE), (2 * PLAN_FEATURES, CSIZE)
    m_shape, acc_shape = (2, LOCAL, 8, CSIZE), (2, LOCAL, PLAN_FEATURES, CSIZE)
    return pl.pallas_call(
        gather_kernel,
        out_shape=[
            shape((2, RING, LOCAL) + q_shape, jnp.bfloat16),
            shape((2, RING, 2, LOCAL) + kv_shape, jnp.bfloat16),
            shape((2, RING, RING, 1, 128), jnp.int32),
            shape((1, LIST_MAX), jnp.int32),
            shape((2 * PLAN_HEADS, 1, 128), jnp.float32),
            shape(m_shape, jnp.float32),
            shape(m_shape, jnp.float32),
            shape(acc_shape, jnp.float32),
        ],
        in_specs=[any_space] * 2 + [in_vmem] * 6,
        out_specs=[any_space] * 8,
        scratch_shapes=[
            vmem(nodes.shape, jnp.bfloat16),
            vmem(qkv_weight.shape, jnp.bfloat16),
            vmem((2, LOCAL) + q_shape, jnp.bfloat16),
            vmem((2, LOCAL) + kv_shape, jnp.bfloat16),
            vmem((1, 128), jnp.int32),
            vmem((1, LIST_MAX), jnp.int32),
            vmem((2 * PLAN_HEADS, 1, 128), jnp.float32),
            vmem(m_shape, jnp.float32),
            vmem(m_shape, jnp.float32),
            vmem(acc_shape, jnp.float32),
            dma((4, 3 * PIECES)), dma((4, 3 * PIECES)), dma((2, 8)), dma((2, 8)), dma((7,)), dma((7,)),
            dma((4, 2)), dma((PIECES,)), dma(()), dma((6,)),
        ],
        compiler_params=pltpu.CompilerParams(
            collective_id=0, has_side_effects=True, vmem_limit_bytes=56 * 2**20
        ),
        name="gather",
    )(nodes, qkv_weight, bias, bucket, key_owner, key_local, query_owner, query_local)


def tile_kernel(
    list_hbm, bias_hbm, table_hbm, m_hbm, l_hbm, acc_hbm, qg_ref, kvg_ref, part_ref, log_ref,
    q_ref, kv_ref, list_ref, bias_ref, table_ref, m_ref, l_ref, acc_ref, q_sem, kv_sem, table_sem, state_sem,
):
    heads = range(PLAN_HEADS)
    z, y, c = coordinates()
    queries = part_ref.shape[0]
    keys = 2 * queries
    waits = ([], [])

    def load(plan, source, target, sem):
        copy = pltpu.make_async_copy(source, target, sem)
        copy.start()
        waits[plan].append(copy)

    load(0, list_hbm, list_ref, table_sem.at[0])
    load(0, table_hbm, table_ref, table_sem.at[1])
    load(0, bias_hbm, bias_ref, table_sem.at[2])
    for plan in range(2):
        side = pl.ds(plan * queries // 2, queries // 2)
        load(plan, qg_ref.at[side], q_ref.at[side], q_sem.at[plan])
        side = pl.ds(plan * keys // 2, keys // 2)
        load(plan, kvg_ref.at[side], kv_ref.at[side], kv_sem.at[plan])
    for plan in range(2):
        own = (z if plan == 0 else y) + plan * RING

        def clear(group, carry):
            @pl.when(group != own)
            def _():
                side = pl.ds(group * LOCAL, LOCAL)
                m_ref[side] = jnp.full((LOCAL, 8, CSIZE), NEVER, jnp.float32)
                l_ref[side] = jnp.zeros((LOCAL, 8, CSIZE), jnp.float32)
                acc_ref[side] = jnp.zeros((LOCAL, PLAN_FEATURES, CSIZE), jnp.float32)
            return carry

        side = pl.ds(own * LOCAL, LOCAL)
        load(plan, m_hbm.at[plan], m_ref.at[side], state_sem.at[plan, 0])
        load(plan, l_hbm.at[plan], l_ref.at[side], state_sem.at[plan, 1])
        load(plan, acc_hbm.at[plan], acc_ref.at[side], state_sem.at[plan, 2])
        lax.fori_loop(plan * RING, (plan + 1) * RING, clear, 0)
    m_ref[queries] = jnp.full((8, CSIZE), NEVER, jnp.float32)
    l_ref[queries] = jnp.zeros((8, CSIZE), jnp.float32)
    acc_ref[queries] = jnp.zeros((PLAN_FEATURES, CSIZE), jnp.float32)

    def batch(step, carry):
        items, pairs = [], []
        for u in range(UNROLL):
            item = list_ref[0, step * UNROLL + u]
            state = lax.bitwise_and(item, 127)
            key = lax.bitwise_and(lax.shift_right_logical(item, 7), 127)
            tile = lax.shift_right_logical(item, 14)
            query = jnp.minimum(state, queries - 1)
            worker = lax.shift_right_logical(tile, 5)
            bucket = table_ref[
                lax.bitwise_and(worker, 1), lax.shift_right_logical(worker, 3),
                lax.bitwise_and(lax.shift_right_logical(worker, 1), 3), 0, lax.bitwise_and(tile, 31),
            ]
            first = jnp.where(key >= keys // 2, PLAN_HEADS, 0)
            items.append((state, [bias_ref[first + h, 0, bucket] for h in heads]))
            pairs.append((
                lambda h, i=query: q_ref[i, rows(h), :],
                lambda h, i=key: kv_ref[i, rows(h), :],
                lambda h, i=key: kv_ref[i, rows(h, PLAN_FEATURES), :],
            ))
        for (state, bias), (highest, mixed) in zip(items, attend(pairs)):
            tops = [top + b for top, b in zip(highest, bias)]
            old_m = [m_ref[state, h : h + 1, :] for h in heads]
            old_l = [l_ref[state, h : h + 1, :] for h in heads]
            old_acc = [acc_ref[state, rows(h), :] for h in heads]
            new_m = [jnp.maximum(a, b) for a, b in zip(old_m, tops)]
            keep = [jnp.exp2(a - b) for a, b in zip(old_m, new_m)]
            fresh = [jnp.exp2(a - b) for a, b in zip(tops, new_m)]
            for h in heads:
                m_ref[state, h : h + 1, :] = new_m[h]
                l_ref[state, h : h + 1, :] = old_l[h] * keep[h] + mixed[h][HEAD_SIZE : HEAD_SIZE + 1] * fresh[h]
                acc_ref[state, rows(h), :] = old_acc[h] * keep[h] + mixed[h][:HEAD_SIZE] * fresh[h]
        return carry

    for copy in waits[0]:
        copy.wait()
    split = lax.div(list_ref[0, LIST_MAX - 2], UNROLL)
    lax.fori_loop(0, split, batch, 0)
    for copy in waits[1]:
        copy.wait()
    lax.fori_loop(split, lax.div(list_ref[0, LIST_MAX - 1] + UNROLL - 1, UNROLL), batch, 0)

    def finish(group, carry):
        for local in range(LOCAL):
            state = group * LOCAL + local
            for h in heads:
                total = l_ref[state, h : h + 1, :]
                held = total > 0
                safe = jnp.where(held, total, 1.0)
                part_ref[group * LOCAL + local % 2 * RING + local // 2, rows(h), :] = (acc_ref[state, rows(h), :] * (1.0 / safe)).astype(jnp.bfloat16)
                row = local // 2 % 2 * PLAN_HEADS + h
                log_ref[group, local % 2, local // 4, row : row + 1, :] = m_ref[state, h : h + 1, :] + jnp.log2(safe)
        return carry

    lax.fori_loop(0, queries // LOCAL, finish, 0)


def tiles(items, bias, table, m, l, acc, q_all, kv_all):
    queries, keys = 2 * RING * LOCAL, 2 * RING * 2 * LOCAL
    any_space = pl.BlockSpec(memory_space=pl.ANY)
    whole = lambda shape: pl.BlockSpec(shape, lambda i, *_: (0,) * len(shape))
    part_shape = (queries, PLAN_FEATURES, CSIZE)
    log_shape = (2 * RING, 2, 2, 8, CSIZE)
    dma, vmem = pltpu.SemaphoreType.DMA, pltpu.VMEM
    return pl.pallas_call(
        tile_kernel,
        grid_spec=pltpu.PrefetchScalarGridSpec(
            num_scalar_prefetch=0,
            grid=(1,),
            in_specs=[any_space] * 8,
            out_specs=[whole(part_shape), whole(log_shape)],
            scratch_shapes=[
                vmem((queries, PLAN_FEATURES, CSIZE), jnp.bfloat16),
                vmem((keys, 2 * PLAN_FEATURES, CSIZE), jnp.bfloat16),
                pltpu.SMEM((1, LIST_MAX), jnp.int32),
                pltpu.SMEM((2 * PLAN_HEADS, 1, 128), jnp.float32),
                pltpu.SMEM((2, RING, RING, 1, 128), jnp.int32),
                vmem((queries + 1, 8, CSIZE), jnp.float32),
                vmem((queries + 1, 8, CSIZE), jnp.float32),
                vmem((queries + 1, PLAN_FEATURES, CSIZE), jnp.float32),
                dma((2,)), dma((2,)), dma((3,)), dma((2, 3)),
            ],
        ),
        out_shape=[
            jax.ShapeDtypeStruct(part_shape, jnp.bfloat16),
            jax.ShapeDtypeStruct(log_shape, jnp.float32),
        ],
        compiler_params=pltpu.CompilerParams(vmem_limit_bytes=56 * 2**20),
        name="tiles",
    )(
        items, bias, table, m, l, acc,
        q_all.reshape(queries, PLAN_FEATURES, CSIZE), kv_all.reshape(keys, 2 * PLAN_FEATURES, CSIZE),
    )


def tail_kernel(
    part_ref, log_ref, nodes_ref, wo_hbm, up_hbm, down_hbm, out_ref,
    wo_ref, up_ref, down_ref, rows_ref, part_in, log_in, far_part, far_log, own_part, own_log, near_part, near_log,
    both_part, both_log, merged, gathered, resid_ref, normed_ref, staged,
    weight_sem, own_sem, near_sem, back_send, back_recv, x_send, x_recv, out_send, out_recv, out_own,
):
    z, y, c = coordinates()
    me = lax.axis_index("owner")
    x = lax.axis_index("head")
    heads = range(PLAN_HEADS)
    features = 2 * PLAN_FEATURES

    def load(source, target, sem):
        copy = pltpu.make_async_copy(source, target, sem)
        copy.start()
        return copy

    def across(step):
        return (me, place(x, step))

    partners = [ring_at(axis, step) for axis in "zy" for step in (1, 3)] + [across(step) for step in (1, 2, 3)]
    greet(partners)
    ways = ((0, 1), (1, -1))
    ring = [(0, "z", z), (1, "y", y)]
    half = lambda h: pl.ds(h * (RING // 2), RING // 2)
    near, ready = [], []
    for plan, axis, at in ring:
        for way, step in ways:
            for turn in range(2):
                near.append(load(
                    part_ref.at[plan, place(at, step), turn, half(way)], near_part.at[plan, way, turn],
                    near_sem.at[plan, way, turn, 0],
                ))
                near.append(load(
                    log_ref.at[plan, place(at, step), turn, way], near_log.at[plan, way, turn],
                    near_sem.at[plan, way, turn, 1],
                ))
    for plan, axis, at in ring:
        ready.append(load(part_ref.at[plan, at], own_part.at[plan], own_sem.at[plan, 0]))
        ready.append(load(log_ref.at[plan, at], own_log.at[plan], own_sem.at[plan, 1]))
    weights = [
        load(nodes_ref.at[pl.ds(x * 2 * CSIZE, 2 * CSIZE)], rows_ref, weight_sem.at[0]),
        load(wo_hbm, wo_ref, weight_sem.at[1]),
        load(up_hbm, up_ref, weight_sem.at[2]),
        load(down_hbm, down_ref, weight_sem.at[3]),
    ]
    greeted(partners)
    sent = []

    def send(src, dst, send_sem, recv_sem, device):
        copy = pltpu.make_async_remote_copy(
            src_ref=src, dst_ref=dst, send_sem=send_sem, recv_sem=recv_sem,
            device_id=device, device_id_type=MESH,
        )
        copy.start()
        sent.append(copy)

    def arrived(ref, sem):
        pltpu.make_async_remote_copy(
            src_ref=ref, dst_ref=ref, send_sem=x_send.at[0, 0], recv_sem=sem,
            device_id=across(1), device_id_type=MESH,
        ).wait_recv()

    def back(plan, way, turn, kind, src, dst, device):
        send(src, dst, back_send.at[plan, way, turn, kind], back_recv.at[plan, way, turn, kind], device)

    def send_out(turn):
        for plan, axis, at in ring:
            for way, step in ways:
                to, far = ring_at(axis, step), place(at, 2)
                back(plan, way, turn, 0, part_ref.at[plan, far, turn, half(way)], far_part.at[plan, way, turn], to)
                back(plan, way, turn, 1, log_ref.at[plan, far, turn, way], far_log.at[plan, way, turn], to)
        for plan, axis, at in ring:
            for way, step in ways:
                to, next_at = ring_at(axis, step), place(at, step)
                back(
                    plan, way, turn, 2, part_ref.at[plan, next_at, turn, half(1 - way)],
                    part_in.at[plan, way, turn, half(1 - way)], to,
                )
                back(
                    plan, way, turn, 3, log_ref.at[plan, next_at, turn, 1 - way],
                    log_in.at[plan, way, turn, 1 - way], to,
                )

    def combine(turn):
        for plan, axis, at in ring:
            for way, step in ways:
                arrived(far_part.at[plan, way, turn], back_recv.at[plan, way, turn, 0])
                arrived(far_log.at[plan, way, turn], back_recv.at[plan, way, turn, 1])
                one, two = near_log[plan, way, turn], far_log[plan, way, turn]
                best = jnp.maximum(one, two)
                shares = [jnp.exp2(one - best), jnp.exp2(two - best)]
                total = shares[0] + shares[1]
                both_log[plan, way, turn] = best + jnp.log2(total)
                scale = 1.0 / total
                shares = [share * scale for share in shares]
                for to in range(2):
                    for h in heads:
                        row = to * PLAN_HEADS + h
                        both_part[plan, way, turn, to, rows(h), :] = (
                            near_part[plan, way, turn, to, rows(h), :].astype(jnp.float32) * shares[0][row : row + 1]
                            + far_part[plan, way, turn, to, rows(h), :].astype(jnp.float32) * shares[1][row : row + 1]
                        ).astype(jnp.bfloat16)
                to = ring_at(axis, step)
                back(plan, way, turn, 4, both_part.at[plan, way, turn], part_in.at[plan, way, turn, half(way)], to)
                back(plan, way, turn, 5, both_log.at[plan, way, turn], log_in.at[plan, way, turn, way], to)

    mine = pl.ds(pl.multiple_of(x * features, 64), features)

    def merge(turn):
        for plan in range(2):
            for way in range(2):
                arrived(part_in.at[plan, way, turn, half(1 - way)], back_recv.at[plan, way, turn, 2])
                arrived(log_in.at[plan, way, turn, 1 - way], back_recv.at[plan, way, turn, 3])
                arrived(part_in.at[plan, way, turn, half(way)], back_recv.at[plan, way, turn, 4])
                arrived(log_in.at[plan, way, turn, way], back_recv.at[plan, way, turn, 5])
        for plan in range(2):
            for to in range(RING):
                h0 = to // 2
                logs = [own_log[plan, turn, h0]] + [log_in[plan, way, turn, h0] for way in range(2)]
                best = jnp.maximum(jnp.maximum(logs[0], logs[1]), logs[2])
                shares = [jnp.exp2(log - best) for log in logs]
                scale = 1.0 / (shares[0] + shares[1] + shares[2])
                shares = [share * scale for share in shares]
                for h in heads:
                    row = to % 2 * PLAN_HEADS + h
                    total = own_part[plan, turn, to, rows(h), :].astype(jnp.float32) * shares[0][row : row + 1]
                    for way in range(2):
                        total += part_in[plan, way, turn, to, rows(h), :].astype(jnp.float32) * shares[way + 1][row : row + 1]
                    merged[turn, to, rows(h, plan * PLAN_FEATURES), :] = total.astype(jnp.bfloat16)
        for step in (2, 1, 3):
            send(
                merged.at[turn, place(x, step)], gathered.at[turn, mine],
                x_send.at[turn, step - 1], x_recv.at[turn, step - 1], across(step),
            )
        gathered[turn, mine, :] = merged[turn, x]

    wide = up_ref.shape[1] // RING
    out_copies = []

    def begin(turn):
        part = slice(turn * CSIZE, (turn + 1) * CSIZE)
        for step in (1, 2, 3):
            source = place(x, -step)
            arrived(gathered.at[turn, pl.ds(pl.multiple_of(source * features, 64), features)], x_recv.at[turn, step - 1])
        mixed = lax.dot_general(
            gathered[turn], wo_ref[...], (((0,), (0,)), ((), ())), preferred_element_type=jnp.float32
        )
        resid = rows_ref[part, :].astype(jnp.float32) + mixed
        resid_ref[part, :] = resid
        normed_ref[part, :] = norm_rows(resid).astype(jnp.bfloat16)

    def feed(turn, first, last):
        part = slice(turn * CSIZE, (turn + 1) * CSIZE)

        def block(step, carry):
            units = pl.ds(pl.multiple_of(step * wide, 128), wide)
            hidden = jax.nn.gelu(
                jnp.dot(normed_ref[part, :], up_ref[:, units], preferred_element_type=jnp.float32)
            ).astype(jnp.bfloat16)
            resid_ref[part, :] += jnp.dot(hidden, down_ref[units, :], preferred_element_type=jnp.float32)
            return carry

        lax.fori_loop(first, last, block, 0)

    def hand_out(turn):
        part = slice(turn * CSIZE, (turn + 1) * CSIZE)
        staged[:, part] = resid_ref[part, :].astype(jnp.bfloat16).T
        target = out_ref.at[:, pl.ds(pl.multiple_of((x * 2 + turn) * CSIZE, CSIZE), CSIZE)]
        block = lambda j: staged.at[pl.ds(pl.multiple_of(j * features, 64), features), part]
        for step in (2, 1, 3):
            send(
                block(place(x, step)), target, out_send.at[turn, step - 1], out_recv.at[turn, step - 1], across(step)
            )
        out_copies.append(load(block(x), target, out_own.at[turn]))

    send_out(0)
    for copy in near:
        copy.wait()
    combine(0)
    send_out(1)
    for copy in ready:
        copy.wait()
    merge(0)
    combine(1)
    for copy in weights:
        copy.wait()
    begin(0)
    feed(0, 0, 2)
    merge(1)
    feed(0, 2, RING)
    hand_out(0)
    begin(1)
    feed(1, 0, RING)
    hand_out(1)
    for turn in range(2):
        for step in (1, 2, 3):
            source = place(x, -step)
            arrived(out_ref.at[:, pl.ds(pl.multiple_of((source * 2 + turn) * CSIZE, CSIZE), CSIZE)], out_recv.at[turn, step - 1])
    for copy in out_copies:
        copy.wait()
    for copy in sent:
        copy.wait_send()


def tail(parts, logs, nodes, out_weight, up_weight, down_weight):
    any_space = pl.BlockSpec(memory_space=pl.ANY)
    dma, vmem = pltpu.SemaphoreType.DMA, pltpu.VMEM
    width = nodes.shape[1]
    features = 2 * PLAN_FEATURES
    return pl.pallas_call(
        tail_kernel,
        out_shape=jax.ShapeDtypeStruct((features, nodes.shape[0]), jnp.bfloat16),
        in_specs=[any_space] * 6,
        out_specs=any_space,
        scratch_shapes=[
            vmem(out_weight.shape, jnp.bfloat16),
            vmem(up_weight.shape, jnp.bfloat16),
            vmem(down_weight.shape, jnp.bfloat16),
            vmem((2 * CSIZE, width), jnp.bfloat16),
            vmem((2, 2, 2, RING, PLAN_FEATURES, CSIZE), jnp.bfloat16),
            vmem((2, 2, 2, 2, 8, CSIZE), jnp.float32),
            vmem((2, 2, 2, 2, PLAN_FEATURES, CSIZE), jnp.bfloat16),
            vmem((2, 2, 2, 8, CSIZE), jnp.float32),
            vmem((2, 2, RING, PLAN_FEATURES, CSIZE), jnp.bfloat16),
            vmem((2, 2, 2, 8, CSIZE), jnp.float32),
            vmem((2, 2, 2, 2, PLAN_FEATURES, CSIZE), jnp.bfloat16),
            vmem((2, 2, 2, 8, CSIZE), jnp.float32),
            vmem((2, 2, 2, 2, PLAN_FEATURES, CSIZE), jnp.bfloat16),
            vmem((2, 2, 2, 8, CSIZE), jnp.float32),
            vmem((2, RING, features, CSIZE), jnp.bfloat16),
            vmem((2, width, CSIZE), jnp.bfloat16),
            vmem((2 * CSIZE, width), jnp.float32),
            vmem((2 * CSIZE, width), jnp.bfloat16),
            vmem((RING * features, 2 * CSIZE), jnp.bfloat16),
            dma((4,)), dma((2, 2)), dma((2, 2, 2, 2)), dma((2, 2, 2, 6)), dma((2, 2, 2, 6)),
            dma((2, 3)), dma((2, 3)), dma((2, 3)), dma((2, 3)), dma((2,)),
        ],
        compiler_params=pltpu.CompilerParams(
            collective_id=1, has_side_effects=True, vmem_limit_bytes=56 * 2**20
        ),
        name="tail",
    )(parts, logs, nodes, out_weight, up_weight, down_weight)


def per_device(
    nodes, qkv_weight, out_weight, hop_bias, up_weight, down_weight,
    key_owner, key_local, query_owner, query_local, hop_bucket,
):
    lists = [array.reshape(8, 128) for array in (key_owner, key_local, query_owner, query_local)]
    q_all, kv_all, table, items, bias, m, l, acc = gather(
        nodes, qkv_weight.swapaxes(1, 2), hop_bias.T, hop_bucket.reshape(1, -1), *lists
    )
    parts, logs = tiles(items, bias, table, m, l, acc, q_all, kv_all)
    return tail(
        parts.reshape(2, RING, 2, RING, PLAN_FEATURES, CSIZE), logs.reshape(2, RING, 2, 2, 8, CSIZE),
        nodes, out_weight, up_weight, down_weight,
    ).T


def solution(mesh):
    placed = (
        P("owner", None), P(None, None, "head"), P(), P(None, "head"), P(), P(),
        P(), P(), P(), P(), P("owner"),
    )
    return jax.shard_map(
        per_device, mesh=mesh, in_specs=placed, out_specs=P("owner", "head"), check_vma=False
    )
```

```python
import functools
import math

import jax
import jax.numpy as jnp
from jax import lax
from jax.experimental import pallas as pl
from jax.experimental.pallas import tpu as pltpu
from jax.sharding import PartitionSpec as P

CSIZE = 256
EPSILON = 1e-05
RING = 4
LOCAL = 8
PLAN_HEADS = 3
HEAD_SIZE = 32
PLAN_FEATURES = PLAN_HEADS * HEAD_SIZE
LIST_MAX = 640
UNROLL = 4
MESH = pl.DeviceIdType.MESH
LOG2E = math.log2(math.e)
NEVER = -1e30
NOTHING = 64
PIECES = 4


def norm_rows(values):
    center = values - jnp.mean(values, axis=-1, keepdims=True)
    spread = jnp.mean(center * center, axis=-1, keepdims=True)
    return center * lax.rsqrt(spread + EPSILON)


def coordinates():
    me = lax.axis_index("owner")
    return lax.div(me, 8), lax.rem(lax.div(me, 2), 4), lax.rem(me, 2)


def place(at, step):
    return lax.rem(at + step + RING, RING)


def ring_at(axis, step):
    z, y, c = coordinates()
    if axis == "z":
        z = place(z, step)
    else:
        y = place(y, step)
    return ((z * 4 + y) * 2 + c, lax.axis_index("head"))


def sibling():
    z, y, c = coordinates()
    return ((z * 4 + y) * 2 + 1 - c, lax.axis_index("head"))


def greet(partners):
    for partner in partners:
        pl.semaphore_signal(pltpu.get_barrier_semaphore(), inc=1, device_id=partner, device_id_type=MESH)


def greeted(partners):
    pl.semaphore_wait(pltpu.get_barrier_semaphore(), len(partners))


def rows(h, first=0):
    return slice(first + HEAD_SIZE * h, first + HEAD_SIZE * (h + 1))


def attend(pairs):
    heads = range(PLAN_HEADS)
    ones = jnp.ones((16, CSIZE), jnp.bfloat16)
    scored = [
        [
            lax.dot_general(key(h), query(h), (((0,), (0,)), ((), ())), preferred_element_type=jnp.float32)
            for h in heads
        ]
        for query, key, value in pairs
    ]
    done = []
    for (query, key, value), scores in zip(pairs, scored):
        highest = [jnp.max(s, axis=0, keepdims=True) for s in scores]
        weights = [jnp.exp2(s - top).astype(jnp.bfloat16) for s, top in zip(scores, highest)]
        mixed = [
            jnp.dot(jnp.concatenate([value(h), ones], 0), weights[h], preferred_element_type=jnp.float32)
            for h in heads
        ]
        done.append((highest, mixed))
    return done


def make_list(query_owner, query_local, key_owner, key_local):
    z, y, c = coordinates()
    div, rem = lax.div, lax.rem
    qz, qy, qc = div(query_owner, 8), rem(div(query_owner, 2), 4), rem(query_owner, 2)
    kz, ky, kc = div(key_owner, 8), rem(div(key_owner, 2), 4), rem(key_owner, 2)
    iota = lax.broadcasted_iota
    number = iota(jnp.int32, (8, 128), 0) * 128 + iota(jnp.int32, (8, 128), 1)
    mine_a = (qy == y) & (qc == c) & (kz == z)
    mine_b = (qz == z) & (qc == c) & (ky == y)
    item_a = (qz * 8 + query_local) + (ky * 16 + kc * 8 + key_local) * 128 + number * 16384
    item_b = (32 + qy * 8 + query_local) + (64 + kz * 16 + kc * 8 + key_local) * 128 + number * 16384
    zero, one = jnp.zeros((8, 128), jnp.float32), jnp.ones((8, 128), jnp.float32)
    ones = jnp.concatenate([jnp.where(mine_a, one, zero), jnp.where(mine_b, one, zero)], 0)
    items = jnp.concatenate([item_a, item_b], 0).astype(jnp.float32)
    before = jnp.where(iota(jnp.int32, (128, 128), 0) < iota(jnp.int32, (128, 128), 1), 1.0, 0.0)
    inside = jnp.dot(ones, before, preferred_element_type=jnp.float32)
    counts = jnp.sum(ones, axis=1, keepdims=True)
    row = iota(jnp.int32, (16, 128), 0)
    wide = jnp.broadcast_to(counts, (16, 128))
    first = jnp.sum(jnp.where(row < 8, wide, 0.0), axis=0, keepdims=True)
    filled = jnp.floor((first + (UNROLL - 1)) * (1.0 / UNROLL)) * UNROLL
    total = filled + jnp.sum(jnp.where(row >= 8, wide, 0.0), axis=0, keepdims=True)
    ahead = [jnp.zeros((1, 128), jnp.float32)]
    for r in range(15):
        ahead.append(ahead[-1] + wide[r : r + 1] if r != 7 else filled)
    rank = jnp.where(ones > 0, inside + jnp.concatenate(ahead, 0), -1.0).T
    values = items.T - NOTHING
    place = iota(jnp.int32, (128, LIST_MAX), 1).astype(jnp.float32)
    listed = jnp.zeros((128, LIST_MAX), jnp.float32)
    for r in range(16):
        listed += jnp.where(rank[:, r : r + 1] == place, values[:, r : r + 1], 0.0)
    listed = jnp.sum(listed, axis=0, keepdims=True) + NOTHING
    at = iota(jnp.int32, (1, LIST_MAX), 1)
    repeat = lambda v: jnp.concatenate([v] * (LIST_MAX // 128), 1)
    listed = jnp.where(at == LIST_MAX - 2, repeat(filled), listed)
    listed = jnp.where(at == LIST_MAX - 1, repeat(total), listed)
    return listed.astype(jnp.int32)


def gather_kernel(
    nodes_hbm, weight_hbm, bias_in, bucket_ref, ko_ref, kl_ref, qo_ref, ql_ref,
    qg_ref, kvg_ref, table_ref, list_ref, bias_ref, m_ref, l_ref, acc_ref,
    nodes_ref, weight_ref,
    ring_send, ring_recv, pair_send, pair_recv, table_send, table_recv, load_sem, weight_sem,
):
    z, y, c = coordinates()
    heads = range(PLAN_HEADS)
    size = LOCAL // PIECES
    partners = [ring_at(axis, step) for axis in "zy" for step in (1, 2, 3)] + [sibling()]
    greet(partners)

    def local_copy(source, target, sem):
        copy = pltpu.make_async_copy(source, target, sem)
        copy.start()
        return copy

    node_rows = lambda p: pl.ds(p * size * CSIZE, size * CSIZE)
    load_nodes = lambda p: local_copy(nodes_hbm.at[node_rows(p)], nodes_ref.at[node_rows(p)], load_sem.at[p])
    node_loads = [load_nodes(0)]
    weight_load = local_copy(weight_hbm, weight_ref, weight_sem)
    node_loads += [load_nodes(p) for p in range(1, PIECES)]
    table_ref[c, z, y] = jnp.concatenate(
        [bucket_ref[...], jnp.zeros((1, 128 - bucket_ref.shape[1]), jnp.int32)], 1
    )
    for i in range(2 * PLAN_HEADS):
        bias_ref[i, :, : bias_in.shape[1]] = bias_in[i : i + 1] * LOG2E
    sent = []

    def part(p):
        return pl.ds(p * size, size)

    def side(h):
        return pl.ds(h * (LOCAL // 2), LOCAL // 2)

    streams = []
    for plan in range(2):
        q_axis, kv_axis = ("z", "y") if plan == 0 else ("y", "z")
        for kind, axis in (("kv", kv_axis), ("q", q_axis)):
            at = z if axis == "z" else y
            if kind == "q":
                slot = lambda p, r, plan=plan: qg_ref.at[plan, p, r]
            else:
                slot = lambda p, r, plan=plan: kvg_ref.at[plan, p, c, r]
            streams.append((len(streams), plan, kind, axis, at, slot))

    def send(src, dst, send_sem, recv_sem, device):
        copy = pltpu.make_async_remote_copy(
            src_ref=src, dst_ref=dst, send_sem=send_sem, recv_sem=recv_sem,
            device_id=device, device_id_type=MESH,
        )
        copy.start()
        sent.append(copy)

    def arrived(ref, sem):
        pltpu.make_async_remote_copy(
            src_ref=ref, dst_ref=ref, send_sem=ring_send.at[0, 0], recv_sem=sem,
            device_id=sibling(), device_id_type=MESH,
        ).wait_recv()

    weight_load.wait()
    own_at = ((z, y), (y, z))

    def project(cluster, carry):
        normed = norm_rows(nodes_ref[pl.ds(cluster * CSIZE, CSIZE), :].astype(jnp.float32)).astype(jnp.bfloat16)
        for i in range(3):
            projected = lax.dot_general(
                weight_ref[i], normed, (((1,), (1,)), ((), ())), preferred_element_type=jnp.float32
            )
            if i == 0:
                projected = projected * (LOG2E / math.sqrt(HEAD_SIZE))
            projected = projected.astype(jnp.bfloat16)
            for plan in range(2):
                block = projected[plan * PLAN_FEATURES : (plan + 1) * PLAN_FEATURES]
                if i == 0:
                    qg_ref[plan, own_at[plan][0], cluster] = block
                else:
                    kvg_ref[plan, own_at[plan][1], c, cluster, (i - 1) * PLAN_FEATURES : i * PLAN_FEATURES, :] = block
        return carry

    ordered = [s for s in streams if s[2] == "kv"] + [s for s in streams if s[2] == "q"]
    for p in range(PIECES):
        node_loads[p].wait()
        lax.fori_loop(p * size, (p + 1) * size, project, 0)
        if p == 0:
            greeted(partners)
            for step in (1, 2, 3):
                send(table_ref.at[c, z, y], table_ref.at[c, z, y], table_send.at[step - 1], table_recv.at[step - 1], ring_at("y", step))
        for number, plan, kind, axis, at, slot in ordered:
            for way, first in ((1, 0), (-1, PIECES)):
                send(
                    slot(at, part(p)), slot(at, part(p)),
                    ring_send.at[number, first + p], ring_recv.at[number, first + p], ring_at(axis, way),
                )
        if p % (PIECES // 2) == PIECES // 2 - 1:
            h = p // (PIECES // 2)
            for number, plan, kind, axis, at, slot in ordered:
                if kind == "kv":
                    send(slot(at, side(h)), slot(at, side(h)), pair_send.at[plan, h], pair_recv.at[plan, h], sibling())
    list_ref[...] = make_list(qo_ref[...], ql_ref[...], ko_ref[...], kl_ref[...])

    for plan in range(2):
        bias = [bias_ref[plan * PLAN_HEADS + h, :, 0:1] for h in heads]

        def own_tiles(step, carry):
            group = [step * UNROLL + u for u in range(UNROLL)]
            pairs = [
                (
                    lambda h, i=i: qg_ref[plan, own_at[plan][0], i, rows(h), :],
                    lambda h, i=i: kvg_ref[plan, own_at[plan][1], c, i, rows(h), :],
                    lambda h, i=i: kvg_ref[plan, own_at[plan][1], c, i, rows(h, PLAN_FEATURES), :],
                )
                for i in group
            ]
            for i, (highest, mixed) in zip(group, attend(pairs)):
                for h in heads:
                    m_ref[plan, i, h : h + 1, :] = highest[h] + bias[h]
                    l_ref[plan, i, h : h + 1, :] = mixed[h][HEAD_SIZE : HEAD_SIZE + 1]
                    acc_ref[plan, i, rows(h), :] = mixed[h][:HEAD_SIZE]
            return carry

        lax.fori_loop(0, LOCAL // UNROLL, own_tiles, 0)
    for step in (1, 2, 3):
        arrived(table_ref.at[c, z, place(y, -step)], table_recv.at[step - 1])
    for step in (1, 2, 3):
        send(table_ref.at[c, z], table_ref.at[c, z], table_send.at[2 + step], table_recv.at[2 + step], ring_at("z", step))
    for h in range(2):
        for p in range(h * PIECES // 2, (h + 1) * PIECES // 2):
            for number, plan, kind, axis, at, slot in ordered:
                before, after = slot(place(at, -1), part(p)), slot(place(at, 1), part(p))
                arrived(before, ring_recv.at[number, p])
                arrived(after, ring_recv.at[number, PIECES + p])
                onward, way = (before, 1) if h == 0 else (after, -1)
                far = 2 * PIECES + p
                send(onward, onward, ring_send.at[number, far], ring_recv.at[number, far], ring_at(axis, way))
        for number, plan, kind, axis, at, slot in ordered:
            if kind == "kv":
                for index, step in ((1, -1), (2, 1)):
                    block, sem = slot(place(at, step), side(h)), 2 * index + h
                    send(block, block, pair_send.at[plan, sem], pair_recv.at[plan, sem], sibling())
        if h == 0:
            for step in (1, 2, 3):
                arrived(table_ref.at[c, place(z, -step)], table_recv.at[2 + step])
            send(table_ref.at[c], table_ref.at[c], table_send.at[6], table_recv.at[6], sibling())
    for h in range(2):
        for number, plan, kind, axis, at, slot in ordered:
            for p in range(h * PIECES // 2, (h + 1) * PIECES // 2):
                arrived(slot(place(at, 2), part(p)), ring_recv.at[number, 2 * PIECES + p])
            if kind == "kv":
                far = slot(place(at, 2), side(h))
                send(far, far, pair_send.at[plan, 6 + h], pair_recv.at[plan, 6 + h], sibling())
    for number, plan, kind, axis, at, slot in streams:
        if kind == "kv":
            for index, step in enumerate((0, -1, 1, 2)):
                for h in range(2):
                    arrived(kvg_ref.at[plan, place(at, step), 1 - c, side(h)], pair_recv.at[plan, 2 * index + h])
    arrived(table_ref.at[1 - c], table_recv.at[6])
    for copy in sent:
        copy.wait_send()


def gather(nodes, qkv_weight, bias, bucket, key_owner, key_local, query_owner, query_local):
    any_space, in_vmem = pl.BlockSpec(memory_space=pl.ANY), pl.BlockSpec(memory_space=pltpu.VMEM)
    dma, vmem = pltpu.SemaphoreType.DMA, pltpu.VMEM
    q_shape, kv_shape = (PLAN_FEATURES, CSIZE), (2 * PLAN_FEATURES, CSIZE)
    m_shape, acc_shape = (2, LOCAL, 8, CSIZE), (2, LOCAL, PLAN_FEATURES, CSIZE)
    return pl.pallas_call(
        gather_kernel,
        out_shape=[
            vmem((2, RING, LOCAL) + q_shape, jnp.bfloat16),
            vmem((2, RING, 2, LOCAL) + kv_shape, jnp.bfloat16),
            vmem((2, RING, RING, 1, 128), jnp.int32),
            vmem((1, LIST_MAX), jnp.int32),
            vmem((2 * PLAN_HEADS, 1, 128), jnp.float32),
            vmem(m_shape, jnp.float32),
            vmem(m_shape, jnp.float32),
            vmem(acc_shape, jnp.float32),
        ],
        in_specs=[any_space] * 2 + [in_vmem] * 6,
        out_specs=[in_vmem] * 8,
        scratch_shapes=[
            vmem(nodes.shape, jnp.bfloat16),
            vmem(qkv_weight.shape, jnp.bfloat16),
            dma((4, 3 * PIECES)), dma((4, 3 * PIECES)), dma((2, 8)), dma((2, 8)), dma((7,)), dma((7,)),
            dma((PIECES,)), dma(()),
        ],
        compiler_params=pltpu.CompilerParams(
            collective_id=0, has_side_effects=True, vmem_limit_bytes=42 * 2**20
        ),
        name="gather",
    )(nodes, qkv_weight, bias, bucket, key_owner, key_local, query_owner, query_local)


def tile_kernel(
    list_hbm, bias_hbm, table_hbm, m_hbm, l_hbm, acc_hbm, q_ref, kv_ref, part_ref, log_ref,
    list_ref, bias_ref, table_ref, m_ref, l_ref, acc_ref, table_sem, state_sem,
):
    heads = range(PLAN_HEADS)
    z, y, c = coordinates()
    queries = part_ref.shape[0]
    keys = 2 * queries
    waits = ([], [])

    def load(plan, source, target, sem):
        copy = pltpu.make_async_copy(source, target, sem)
        copy.start()
        waits[plan].append(copy)

    load(0, list_hbm, list_ref, table_sem.at[0])
    load(0, table_hbm, table_ref, table_sem.at[1])
    load(0, bias_hbm, bias_ref, table_sem.at[2])
    for plan in range(2):
        own = (z if plan == 0 else y) + plan * RING

        def clear(group, carry):
            @pl.when(group != own)
            def _():
                side = pl.ds(group * LOCAL, LOCAL)
                m_ref[side] = jnp.full((LOCAL, 8, CSIZE), NEVER, jnp.float32)
                l_ref[side] = jnp.zeros((LOCAL, 8, CSIZE), jnp.float32)
                acc_ref[side] = jnp.zeros((LOCAL, PLAN_FEATURES, CSIZE), jnp.float32)
            return carry

        side = pl.ds(own * LOCAL, LOCAL)
        load(plan, m_hbm.at[plan], m_ref.at[side], state_sem.at[plan, 0])
        load(plan, l_hbm.at[plan], l_ref.at[side], state_sem.at[plan, 1])
        load(plan, acc_hbm.at[plan], acc_ref.at[side], state_sem.at[plan, 2])
        lax.fori_loop(plan * RING, (plan + 1) * RING, clear, 0)
    m_ref[queries] = jnp.full((8, CSIZE), NEVER, jnp.float32)
    l_ref[queries] = jnp.zeros((8, CSIZE), jnp.float32)
    acc_ref[queries] = jnp.zeros((PLAN_FEATURES, CSIZE), jnp.float32)

    def batch(step, carry):
        items, pairs = [], []
        for u in range(UNROLL):
            item = list_ref[0, step * UNROLL + u]
            state = lax.bitwise_and(item, 127)
            key = lax.bitwise_and(lax.shift_right_logical(item, 7), 127)
            tile = lax.shift_right_logical(item, 14)
            query = jnp.minimum(state, queries - 1)
            worker = lax.shift_right_logical(tile, 5)
            bucket = table_ref[
                lax.bitwise_and(worker, 1), lax.shift_right_logical(worker, 3),
                lax.bitwise_and(lax.shift_right_logical(worker, 1), 3), 0, lax.bitwise_and(tile, 31),
            ]
            first = jnp.where(key >= keys // 2, PLAN_HEADS, 0)
            items.append((state, [bias_ref[first + h, 0, bucket] for h in heads]))
            pairs.append((
                lambda h, i=query: q_ref[i, rows(h), :],
                lambda h, i=key: kv_ref[i, rows(h), :],
                lambda h, i=key: kv_ref[i, rows(h, PLAN_FEATURES), :],
            ))
        for (state, bias), (highest, mixed) in zip(items, attend(pairs)):
            tops = [top + b for top, b in zip(highest, bias)]
            old_m = [m_ref[state, h : h + 1, :] for h in heads]
            old_l = [l_ref[state, h : h + 1, :] for h in heads]
            old_acc = [acc_ref[state, rows(h), :] for h in heads]
            new_m = [jnp.maximum(a, b) for a, b in zip(old_m, tops)]
            keep = [jnp.exp2(a - b) for a, b in zip(old_m, new_m)]
            fresh = [jnp.exp2(a - b) for a, b in zip(tops, new_m)]
            for h in heads:
                m_ref[state, h : h + 1, :] = new_m[h]
                l_ref[state, h : h + 1, :] = old_l[h] * keep[h] + mixed[h][HEAD_SIZE : HEAD_SIZE + 1] * fresh[h]
                acc_ref[state, rows(h), :] = old_acc[h] * keep[h] + mixed[h][:HEAD_SIZE] * fresh[h]
        return carry

    for copy in waits[0]:
        copy.wait()
    split = lax.div(list_ref[0, LIST_MAX - 2], UNROLL)
    lax.fori_loop(0, split, batch, 0)
    for copy in waits[1]:
        copy.wait()
    lax.fori_loop(split, lax.div(list_ref[0, LIST_MAX - 1] + UNROLL - 1, UNROLL), batch, 0)

    def finish(group, carry):
        for local in range(LOCAL):
            state = group * LOCAL + local
            for h in heads:
                total = l_ref[state, h : h + 1, :]
                held = total > 0
                safe = jnp.where(held, total, 1.0)
                part_ref[group * LOCAL + local % 2 * RING + local // 2, rows(h), :] = (acc_ref[state, rows(h), :] * (1.0 / safe)).astype(jnp.bfloat16)
                row = local // 2 % 2 * PLAN_HEADS + h
                log_ref[group, local % 2, local // 4, row : row + 1, :] = m_ref[state, h : h + 1, :] + jnp.log2(safe)
        return carry

    lax.fori_loop(0, queries // LOCAL, finish, 0)


def tiles(items, bias, table, m, l, acc, q_all, kv_all):
    queries, keys = 2 * RING * LOCAL, 2 * RING * 2 * LOCAL
    in_vmem = pl.BlockSpec(memory_space=pltpu.VMEM)
    part_shape = (queries, PLAN_FEATURES, CSIZE)
    log_shape = (2 * RING, 2, 2, 8, CSIZE)
    dma, vmem = pltpu.SemaphoreType.DMA, pltpu.VMEM
    return pl.pallas_call(
        tile_kernel,
        in_specs=[in_vmem] * 8,
        out_specs=[in_vmem] * 2,
        scratch_shapes=[
                pltpu.SMEM((1, LIST_MAX), jnp.int32),
                pltpu.SMEM((2 * PLAN_HEADS, 1, 128), jnp.float32),
                pltpu.SMEM((2, RING, RING, 1, 128), jnp.int32),
                vmem((queries + 1, 8, CSIZE), jnp.float32),
                vmem((queries + 1, 8, CSIZE), jnp.float32),
                vmem((queries + 1, PLAN_FEATURES, CSIZE), jnp.float32),
            dma((3,)), dma((2, 3)),
        ],
        out_shape=[vmem(part_shape, jnp.bfloat16), vmem(log_shape, jnp.float32)],
        compiler_params=pltpu.CompilerParams(vmem_limit_bytes=16 * 2**20),
        name="tiles",
    )(
        items, bias, table, m, l, acc,
        q_all.reshape(queries, PLAN_FEATURES, CSIZE), kv_all.reshape(keys, 2 * PLAN_FEATURES, CSIZE),
    )


def tail_kernel(
    part_ref, log_ref, nodes_ref, wo_hbm, up_hbm, down_hbm, out_ref,
    wo_ref, up_ref, down_ref, rows_ref, part_in, log_in, far_part, far_log, both_part, both_log, merged, gathered, resid_ref, normed_ref, staged,
    weight_sem, back_send, back_recv, x_send, x_recv, out_send, out_recv, out_own,
):
    z, y, c = coordinates()
    me = lax.axis_index("owner")
    x = lax.axis_index("head")
    heads = range(PLAN_HEADS)
    features = 2 * PLAN_FEATURES

    def load(source, target, sem):
        copy = pltpu.make_async_copy(source, target, sem)
        copy.start()
        return copy

    def across(step):
        return (me, place(x, step))

    partners = [ring_at(axis, step) for axis in "zy" for step in (1, 3)] + [across(step) for step in (1, 2, 3)]
    greet(partners)
    ways = ((0, 1), (1, -1))
    ring = [(0, "z", z), (1, "y", y)]
    half = lambda h: pl.ds(h * (RING // 2), RING // 2)
    weights = [
        load(nodes_ref.at[pl.ds(x * 2 * CSIZE, 2 * CSIZE)], rows_ref, weight_sem.at[0]),
        load(wo_hbm, wo_ref, weight_sem.at[1]),
        load(up_hbm, up_ref, weight_sem.at[2]),
        load(down_hbm, down_ref, weight_sem.at[3]),
    ]
    greeted(partners)
    sent = []

    def send(src, dst, send_sem, recv_sem, device):
        copy = pltpu.make_async_remote_copy(
            src_ref=src, dst_ref=dst, send_sem=send_sem, recv_sem=recv_sem,
            device_id=device, device_id_type=MESH,
        )
        copy.start()
        sent.append(copy)

    def arrived(ref, sem):
        pltpu.make_async_remote_copy(
            src_ref=ref, dst_ref=ref, send_sem=x_send.at[0, 0], recv_sem=sem,
            device_id=across(1), device_id_type=MESH,
        ).wait_recv()

    def back(plan, way, turn, kind, src, dst, device):
        send(src, dst, back_send.at[plan, way, turn, kind], back_recv.at[plan, way, turn, kind], device)

    def send_out(turn):
        for plan, axis, at in ring:
            for way, step in ways:
                to, far = ring_at(axis, step), place(at, 2)
                back(plan, way, turn, 0, part_ref.at[plan, far, turn, half(way)], far_part.at[plan, way, turn], to)
                back(plan, way, turn, 1, log_ref.at[plan, far, turn, way], far_log.at[plan, way, turn], to)
        for plan, axis, at in ring:
            for way, step in ways:
                to, next_at = ring_at(axis, step), place(at, step)
                back(
                    plan, way, turn, 2, part_ref.at[plan, next_at, turn, half(1 - way)],
                    part_in.at[plan, way, turn, half(1 - way)], to,
                )
                back(
                    plan, way, turn, 3, log_ref.at[plan, next_at, turn, 1 - way],
                    log_in.at[plan, way, turn, 1 - way], to,
                )

    def combine(turn):
        for plan, axis, at in ring:
            for way, step in ways:
                arrived(far_part.at[plan, way, turn], back_recv.at[plan, way, turn, 0])
                arrived(far_log.at[plan, way, turn], back_recv.at[plan, way, turn, 1])
                one, two = log_ref[plan, place(at, step), turn, way], far_log[plan, way, turn]
                best = jnp.maximum(one, two)
                shares = [jnp.exp2(one - best), jnp.exp2(two - best)]
                total = shares[0] + shares[1]
                both_log[plan, way, turn] = best + jnp.log2(total)
                scale = 1.0 / total
                shares = [share * scale for share in shares]
                for to in range(2):
                    for h in heads:
                        row = to * PLAN_HEADS + h
                        both_part[plan, way, turn, to, rows(h), :] = (
                            part_ref[plan, place(at, step), turn, way * 2 + to, rows(h), :].astype(jnp.float32) * shares[0][row : row + 1]
                            + far_part[plan, way, turn, to, rows(h), :].astype(jnp.float32) * shares[1][row : row + 1]
                        ).astype(jnp.bfloat16)
                to = ring_at(axis, step)
                back(plan, way, turn, 4, both_part.at[plan, way, turn], part_in.at[plan, way, turn, half(way)], to)
                back(plan, way, turn, 5, both_log.at[plan, way, turn], log_in.at[plan, way, turn, way], to)

    mine = pl.ds(pl.multiple_of(x * features, 64), features)

    def merge(turn):
        for plan in range(2):
            for way in range(2):
                arrived(part_in.at[plan, way, turn, half(1 - way)], back_recv.at[plan, way, turn, 2])
                arrived(log_in.at[plan, way, turn, 1 - way], back_recv.at[plan, way, turn, 3])
                arrived(part_in.at[plan, way, turn, half(way)], back_recv.at[plan, way, turn, 4])
                arrived(log_in.at[plan, way, turn, way], back_recv.at[plan, way, turn, 5])
        for plan, axis, at in ring:
            for to in range(RING):
                h0 = to // 2
                logs = [log_ref[plan, at, turn, h0]] + [log_in[plan, way, turn, h0] for way in range(2)]
                best = jnp.maximum(jnp.maximum(logs[0], logs[1]), logs[2])
                shares = [jnp.exp2(log - best) for log in logs]
                scale = 1.0 / (shares[0] + shares[1] + shares[2])
                shares = [share * scale for share in shares]
                for h in heads:
                    row = to % 2 * PLAN_HEADS + h
                    total = part_ref[plan, at, turn, to, rows(h), :].astype(jnp.float32) * shares[0][row : row + 1]
                    for way in range(2):
                        total += part_in[plan, way, turn, to, rows(h), :].astype(jnp.float32) * shares[way + 1][row : row + 1]
                    merged[turn, to, rows(h, plan * PLAN_FEATURES), :] = total.astype(jnp.bfloat16)
        for step in (2, 1, 3):
            send(
                merged.at[turn, place(x, step)], gathered.at[turn, mine],
                x_send.at[turn, step - 1], x_recv.at[turn, step - 1], across(step),
            )
        gathered[turn, mine, :] = merged[turn, x]

    wide = up_ref.shape[1] // RING
    out_copies = []

    def begin(turn):
        part = slice(turn * CSIZE, (turn + 1) * CSIZE)
        for step in (1, 2, 3):
            source = place(x, -step)
            arrived(gathered.at[turn, pl.ds(pl.multiple_of(source * features, 64), features)], x_recv.at[turn, step - 1])
        mixed = lax.dot_general(
            gathered[turn], wo_ref[...], (((0,), (0,)), ((), ())), preferred_element_type=jnp.float32
        )
        resid = rows_ref[part, :].astype(jnp.float32) + mixed
        resid_ref[part, :] = resid
        normed_ref[part, :] = norm_rows(resid).astype(jnp.bfloat16)

    def feed(turn, first, last):
        part = slice(turn * CSIZE, (turn + 1) * CSIZE)

        def block(step, carry):
            units = pl.ds(pl.multiple_of(step * wide, 128), wide)
            hidden = jax.nn.gelu(
                jnp.dot(normed_ref[part, :], up_ref[:, units], preferred_element_type=jnp.float32)
            ).astype(jnp.bfloat16)
            resid_ref[part, :] += jnp.dot(hidden, down_ref[units, :], preferred_element_type=jnp.float32)
            return carry

        lax.fori_loop(first, last, block, 0)

    def hand_out(turn):
        part = slice(turn * CSIZE, (turn + 1) * CSIZE)
        staged[:, part] = resid_ref[part, :].astype(jnp.bfloat16).T
        target = out_ref.at[:, pl.ds(pl.multiple_of((x * 2 + turn) * CSIZE, CSIZE), CSIZE)]
        block = lambda j: staged.at[pl.ds(pl.multiple_of(j * features, 64), features), part]
        for step in (2, 1, 3):
            send(
                block(place(x, step)), target, out_send.at[turn, step - 1], out_recv.at[turn, step - 1], across(step)
            )
        out_copies.append(load(block(x), target, out_own.at[turn]))

    send_out(0)
    combine(0)
    send_out(1)
    merge(0)
    combine(1)
    for copy in weights:
        copy.wait()
    begin(0)
    feed(0, 0, 2)
    merge(1)
    feed(0, 2, RING)
    hand_out(0)
    begin(1)
    feed(1, 0, RING)
    hand_out(1)
    for turn in range(2):
        for step in (1, 2, 3):
            source = place(x, -step)
            arrived(out_ref.at[:, pl.ds(pl.multiple_of((source * 2 + turn) * CSIZE, CSIZE), CSIZE)], out_recv.at[turn, step - 1])
    for copy in out_copies:
        copy.wait()
    for copy in sent:
        copy.wait_send()


def tail(parts, logs, nodes, out_weight, up_weight, down_weight):
    any_space = pl.BlockSpec(memory_space=pl.ANY)
    dma, vmem = pltpu.SemaphoreType.DMA, pltpu.VMEM
    width = nodes.shape[1]
    features = 2 * PLAN_FEATURES
    return pl.pallas_call(
        tail_kernel,
        out_shape=jax.ShapeDtypeStruct((features, nodes.shape[0]), jnp.bfloat16),
        in_specs=[pl.BlockSpec(memory_space=pltpu.VMEM)] * 2 + [any_space] * 4,
        out_specs=any_space,
        scratch_shapes=[
            vmem(out_weight.shape, jnp.bfloat16),
            vmem(up_weight.shape, jnp.bfloat16),
            vmem(down_weight.shape, jnp.bfloat16),
            vmem((2 * CSIZE, width), jnp.bfloat16),
            vmem((2, 2, 2, RING, PLAN_FEATURES, CSIZE), jnp.bfloat16),
            vmem((2, 2, 2, 2, 8, CSIZE), jnp.float32),
            vmem((2, 2, 2, 2, PLAN_FEATURES, CSIZE), jnp.bfloat16),
            vmem((2, 2, 2, 8, CSIZE), jnp.float32),
            vmem((2, 2, 2, 2, PLAN_FEATURES, CSIZE), jnp.bfloat16),
            vmem((2, 2, 2, 8, CSIZE), jnp.float32),
            vmem((2, RING, features, CSIZE), jnp.bfloat16),
            vmem((2, width, CSIZE), jnp.bfloat16),
            vmem((2 * CSIZE, width), jnp.float32),
            vmem((2 * CSIZE, width), jnp.bfloat16),
            vmem((RING * features, 2 * CSIZE), jnp.bfloat16),
            dma((4,)), dma((2, 2, 2, 6)), dma((2, 2, 2, 6)),
            dma((2, 3)), dma((2, 3)), dma((2, 3)), dma((2, 3)), dma((2,)),
        ],
        compiler_params=pltpu.CompilerParams(
            collective_id=1, has_side_effects=True, vmem_limit_bytes=32 * 2**20
        ),
        name="tail",
    )(parts, logs, nodes, out_weight, up_weight, down_weight)


def per_device(
    nodes, qkv_weight, out_weight, hop_bias, up_weight, down_weight,
    key_owner, key_local, query_owner, query_local, hop_bucket,
):
    lists = [array.reshape(8, 128) for array in (key_owner, key_local, query_owner, query_local)]
    q_all, kv_all, table, items, bias, m, l, acc = gather(
        *[pltpu.with_memory_space_constraint(a, pltpu.HBM) for a in (nodes, qkv_weight.swapaxes(1, 2))], hop_bias.T, hop_bucket.reshape(1, -1), *lists
    )
    parts, logs = tiles(items, bias, table, m, l, acc, q_all, kv_all)
    return tail(
        parts.reshape(2, RING, 2, RING, PLAN_FEATURES, CSIZE), logs.reshape(2, RING, 2, 2, 8, CSIZE),
        *[pltpu.with_memory_space_constraint(a, pltpu.HBM) for a in (nodes, out_weight, up_weight, down_weight)],
    ).T


def solution(mesh):
    placed = (
        P("owner", None), P(None, None, "head"), P(), P(None, "head"), P(), P(),
        P(), P(), P(), P(), P("owner"),
    )
    return jax.shard_map(
        per_device, mesh=mesh, in_specs=placed, out_specs=P("owner", "head"), check_vma=False
    )
```

```python
import functools
import math

import jax
import jax.numpy as jnp
from jax import lax
from jax.experimental import pallas as pl
from jax.experimental.pallas import tpu as pltpu
from jax.sharding import PartitionSpec as P

CSIZE = 256
EPSILON = 1e-05
RING = 4
LOCAL = 8
PLAN_HEADS = 3
HEAD_SIZE = 32
PLAN_FEATURES = PLAN_HEADS * HEAD_SIZE
LIST_MAX = 640
UNROLL = 4
MESH = pl.DeviceIdType.MESH
LOG2E = math.log2(math.e)
NEVER = -1e30
NOTHING = 64
PIECES = 4
BLOCKS = 2
TURNS = ((0, 0, 256), (1, 0, 128), (1, 128, 128))


def norm_rows(values):
    center = values - jnp.mean(values, axis=-1, keepdims=True)
    spread = jnp.mean(center * center, axis=-1, keepdims=True)
    return center * lax.rsqrt(spread + EPSILON)


def coordinates():
    me = lax.axis_index("owner")
    return lax.div(me, 8), lax.rem(lax.div(me, 2), 4), lax.rem(me, 2)


def place(at, step):
    return lax.rem(at + step + RING, RING)


def ring_at(axis, step):
    z, y, c = coordinates()
    if axis == "z":
        z = place(z, step)
    else:
        y = place(y, step)
    return ((z * 4 + y) * 2 + c, lax.axis_index("head"))


def sibling():
    z, y, c = coordinates()
    return ((z * 4 + y) * 2 + 1 - c, lax.axis_index("head"))


def greet(partners):
    for partner in partners:
        pl.semaphore_signal(pltpu.get_barrier_semaphore(), inc=1, device_id=partner, device_id_type=MESH)


def greeted(partners):
    pl.semaphore_wait(pltpu.get_barrier_semaphore(), len(partners))


def rows(h, first=0):
    return slice(first + HEAD_SIZE * h, first + HEAD_SIZE * (h + 1))


def attend(pairs):
    heads = range(PLAN_HEADS)
    ones = jnp.ones((16, CSIZE), jnp.bfloat16)
    scored = [
        [
            lax.dot_general(key(h), query(h), (((0,), (0,)), ((), ())), preferred_element_type=jnp.float32)
            for h in heads
        ]
        for query, key, value in pairs
    ]
    done = []
    for (query, key, value), scores in zip(pairs, scored):
        highest = [jnp.max(s, axis=0, keepdims=True) for s in scores]
        weights = [jnp.exp2(s - top).astype(jnp.bfloat16) for s, top in zip(scores, highest)]
        mixed = [
            jnp.dot(jnp.concatenate([value(h), ones], 0), weights[h], preferred_element_type=jnp.float32)
            for h in heads
        ]
        done.append((highest, mixed))
    return done


def make_list(query_owner, query_local, key_owner, key_local):
    z, y, c = coordinates()
    div, rem = lax.div, lax.rem
    qz, qy, qc = div(query_owner, 8), rem(div(query_owner, 2), 4), rem(query_owner, 2)
    kz, ky, kc = div(key_owner, 8), rem(div(key_owner, 2), 4), rem(key_owner, 2)
    iota = lax.broadcasted_iota
    number = iota(jnp.int32, (8, 128), 0) * 128 + iota(jnp.int32, (8, 128), 1)
    mine_a = (qy == y) & (qc == c) & (kz == z)
    mine_b = (qz == z) & (qc == c) & (ky == y)
    item_a = (qz * 8 + query_local) + (ky * 16 + kc * 8 + key_local) * 128 + number * 16384
    item_b = (32 + qy * 8 + query_local) + (64 + kz * 16 + kc * 8 + key_local) * 128 + number * 16384
    zero, one = jnp.zeros((8, 128), jnp.float32), jnp.ones((8, 128), jnp.float32)
    ones = jnp.concatenate([jnp.where(mine_a, one, zero), jnp.where(mine_b, one, zero)], 0)
    items = jnp.concatenate([item_a, item_b], 0).astype(jnp.float32)
    before = jnp.where(iota(jnp.int32, (128, 128), 0) < iota(jnp.int32, (128, 128), 1), 1.0, 0.0)
    inside = jnp.dot(ones, before, preferred_element_type=jnp.float32)
    counts = jnp.sum(ones, axis=1, keepdims=True)
    row = iota(jnp.int32, (16, 128), 0)
    wide = jnp.broadcast_to(counts, (16, 128))
    first = jnp.sum(jnp.where(row < 8, wide, 0.0), axis=0, keepdims=True)
    filled = jnp.floor((first + (UNROLL - 1)) * (1.0 / UNROLL)) * UNROLL
    total = filled + jnp.sum(jnp.where(row >= 8, wide, 0.0), axis=0, keepdims=True)
    ahead = [jnp.zeros((1, 128), jnp.float32)]
    for r in range(15):
        ahead.append(ahead[-1] + wide[r : r + 1] if r != 7 else filled)
    rank = jnp.where(ones > 0, inside + jnp.concatenate(ahead, 0), -1.0).T
    values = items.T - NOTHING
    place = iota(jnp.int32, (128, LIST_MAX), 1).astype(jnp.float32)
    listed = jnp.zeros((128, LIST_MAX), jnp.float32)
    for r in range(16):
        listed += jnp.where(rank[:, r : r + 1] == place, values[:, r : r + 1], 0.0)
    listed = jnp.sum(listed, axis=0, keepdims=True) + NOTHING
    at = iota(jnp.int32, (1, LIST_MAX), 1)
    repeat = lambda v: jnp.concatenate([v] * (LIST_MAX // 128), 1)
    listed = jnp.where(at == LIST_MAX - 2, repeat(filled), listed)
    listed = jnp.where(at == LIST_MAX - 1, repeat(total), listed)
    return listed.astype(jnp.int32)


def gather_kernel(
    nodes_hbm, weight_hbm, bias_in, bucket_ref, ko_ref, kl_ref, qo_ref, ql_ref,
    qg_ref, kvg_ref, table_ref, list_ref, bias_ref, m_ref, l_ref, acc_ref,
    nodes_ref, weight_ref,
    ring_send, ring_recv, pair_send, pair_recv, table_send, table_recv, load_sem, weight_sem,
):
    z, y, c = coordinates()
    heads = range(PLAN_HEADS)
    size = LOCAL // PIECES
    partners = [ring_at(axis, step) for axis in "zy" for step in (1, 2, 3)] + [sibling()]
    greet(partners)

    def local_copy(source, target, sem):
        copy = pltpu.make_async_copy(source, target, sem)
        copy.start()
        return copy

    node_rows = lambda p: pl.ds(p * size * CSIZE, size * CSIZE)
    load_nodes = lambda p: local_copy(nodes_hbm.at[node_rows(p)], nodes_ref.at[node_rows(p)], load_sem.at[p])
    node_loads = [load_nodes(0)]
    weight_load = local_copy(weight_hbm, weight_ref, weight_sem)
    node_loads += [load_nodes(p) for p in range(1, PIECES)]
    table_ref[c, z, y] = jnp.concatenate(
        [bucket_ref[...], jnp.zeros((1, 128 - bucket_ref.shape[1]), jnp.int32)], 1
    )
    for i in range(2 * PLAN_HEADS):
        bias_ref[i, :, : bias_in.shape[1]] = bias_in[i : i + 1] * LOG2E
    sent = []

    def part(p):
        return pl.ds(p * size, size)

    def side(h):
        return pl.ds(h * (LOCAL // 2), LOCAL // 2)

    streams = []
    for plan in range(2):
        q_axis, kv_axis = ("z", "y") if plan == 0 else ("y", "z")
        for kind, axis in (("kv", kv_axis), ("q", q_axis)):
            at = z if axis == "z" else y
            if kind == "q":
                slot = lambda p, r, plan=plan: qg_ref.at[plan, p, r]
            else:
                slot = lambda p, r, plan=plan: kvg_ref.at[plan, p, c, r]
            streams.append((len(streams), plan, kind, axis, at, slot))

    def send(src, dst, send_sem, recv_sem, device):
        copy = pltpu.make_async_remote_copy(
            src_ref=src, dst_ref=dst, send_sem=send_sem, recv_sem=recv_sem,
            device_id=device, device_id_type=MESH,
        )
        copy.start()
        sent.append(copy)

    def arrived(ref, sem):
        pltpu.make_async_remote_copy(
            src_ref=ref, dst_ref=ref, send_sem=ring_send.at[0, 0], recv_sem=sem,
            device_id=sibling(), device_id_type=MESH,
        ).wait_recv()

    weight_load.wait()
    own_at = ((z, y), (y, z))

    def project(cluster, carry):
        normed = norm_rows(nodes_ref[pl.ds(cluster * CSIZE, CSIZE), :].astype(jnp.float32)).astype(jnp.bfloat16)
        for i in range(3):
            projected = lax.dot_general(
                weight_ref[i], normed, (((1,), (1,)), ((), ())), preferred_element_type=jnp.float32
            )
            if i == 0:
                projected = projected * (LOG2E / math.sqrt(HEAD_SIZE))
            projected = projected.astype(jnp.bfloat16)
            for plan in range(2):
                block = projected[plan * PLAN_FEATURES : (plan + 1) * PLAN_FEATURES]
                if i == 0:
                    qg_ref[plan, own_at[plan][0], cluster] = block
                else:
                    kvg_ref[plan, own_at[plan][1], c, cluster, (i - 1) * PLAN_FEATURES : i * PLAN_FEATURES, :] = block
        return carry

    ordered = [s for s in streams if s[2] == "kv"] + [s for s in streams if s[2] == "q"]
    for p in range(PIECES):
        node_loads[p].wait()
        lax.fori_loop(p * size, (p + 1) * size, project, 0)
        if p == 0:
            greeted(partners)
            for step in (1, 2, 3):
                send(table_ref.at[c, z, y], table_ref.at[c, z, y], table_send.at[step - 1], table_recv.at[step - 1], ring_at("y", step))
        for number, plan, kind, axis, at, slot in ordered:
            for way, first in ((1, 0), (-1, PIECES)):
                send(
                    slot(at, part(p)), slot(at, part(p)),
                    ring_send.at[number, first + p], ring_recv.at[number, first + p], ring_at(axis, way),
                )
        if p % (PIECES // 2) == PIECES // 2 - 1:
            h = p // (PIECES // 2)
            for number, plan, kind, axis, at, slot in ordered:
                if kind == "kv":
                    send(slot(at, side(h)), slot(at, side(h)), pair_send.at[plan, h], pair_recv.at[plan, h], sibling())
    list_ref[...] = make_list(qo_ref[...], ql_ref[...], ko_ref[...], kl_ref[...])

    for plan in range(2):
        bias = [bias_ref[plan * PLAN_HEADS + h, :, 0:1] for h in heads]

        def own_tiles(step, carry):
            group = [step * UNROLL + u for u in range(UNROLL)]
            pairs = [
                (
                    lambda h, i=i: qg_ref[plan, own_at[plan][0], i, rows(h), :],
                    lambda h, i=i: kvg_ref[plan, own_at[plan][1], c, i, rows(h), :],
                    lambda h, i=i: kvg_ref[plan, own_at[plan][1], c, i, rows(h, PLAN_FEATURES), :],
                )
                for i in group
            ]
            for i, (highest, mixed) in zip(group, attend(pairs)):
                for h in heads:
                    m_ref[plan, i, h : h + 1, :] = highest[h] + bias[h]
                    l_ref[plan, i, h : h + 1, :] = mixed[h][HEAD_SIZE : HEAD_SIZE + 1]
                    acc_ref[plan, i, rows(h), :] = mixed[h][:HEAD_SIZE]
            return carry

        lax.fori_loop(0, LOCAL // UNROLL, own_tiles, 0)
    for step in (1, 2, 3):
        arrived(table_ref.at[c, z, place(y, -step)], table_recv.at[step - 1])
    for step in (1, 2, 3):
        send(table_ref.at[c, z], table_ref.at[c, z], table_send.at[2 + step], table_recv.at[2 + step], ring_at("z", step))
    for h in range(2):
        for p in range(h * PIECES // 2, (h + 1) * PIECES // 2):
            for number, plan, kind, axis, at, slot in ordered:
                before, after = slot(place(at, -1), part(p)), slot(place(at, 1), part(p))
                arrived(before, ring_recv.at[number, p])
                arrived(after, ring_recv.at[number, PIECES + p])
                onward, way = (before, 1) if p % 2 == 0 else (after, -1)
                far = 2 * PIECES + p
                send(onward, onward, ring_send.at[number, far], ring_recv.at[number, far], ring_at(axis, way))
        for number, plan, kind, axis, at, slot in ordered:
            if kind == "kv":
                for index, step in ((1, -1), (2, 1)):
                    block, sem = slot(place(at, step), side(h)), 2 * index + h
                    send(block, block, pair_send.at[plan, sem], pair_recv.at[plan, sem], sibling())
        if h == 0:
            for step in (1, 2, 3):
                arrived(table_ref.at[c, place(z, -step)], table_recv.at[2 + step])
            send(table_ref.at[c], table_ref.at[c], table_send.at[6], table_recv.at[6], sibling())
    for h in range(2):
        for number, plan, kind, axis, at, slot in ordered:
            for p in range(h * PIECES // 2, (h + 1) * PIECES // 2):
                arrived(slot(place(at, 2), part(p)), ring_recv.at[number, 2 * PIECES + p])
            if kind == "kv":
                far = slot(place(at, 2), side(h))
                send(far, far, pair_send.at[plan, 6 + h], pair_recv.at[plan, 6 + h], sibling())
    for number, plan, kind, axis, at, slot in streams:
        if kind == "kv":
            for index, step in enumerate((0, -1, 1, 2)):
                for h in range(2):
                    arrived(kvg_ref.at[plan, place(at, step), 1 - c, side(h)], pair_recv.at[plan, 2 * index + h])
    arrived(table_ref.at[1 - c], table_recv.at[6])
    for copy in sent:
        copy.wait_send()


def gather(nodes, qkv_weight, bias, bucket, key_owner, key_local, query_owner, query_local):
    any_space, in_vmem = pl.BlockSpec(memory_space=pl.ANY), pl.BlockSpec(memory_space=pltpu.VMEM)
    dma, vmem = pltpu.SemaphoreType.DMA, pltpu.VMEM
    q_shape, kv_shape = (PLAN_FEATURES, CSIZE), (2 * PLAN_FEATURES, CSIZE)
    m_shape, acc_shape = (2, LOCAL, 8, CSIZE), (2, LOCAL, PLAN_FEATURES, CSIZE)
    return pl.pallas_call(
        gather_kernel,
        out_shape=[
            vmem((2, RING, LOCAL) + q_shape, jnp.bfloat16),
            vmem((2, RING, 2, LOCAL) + kv_shape, jnp.bfloat16),
            vmem((2, RING, RING, 1, 128), jnp.int32),
            vmem((1, LIST_MAX), jnp.int32),
            vmem((2 * PLAN_HEADS, 1, 128), jnp.float32),
            vmem(m_shape, jnp.float32),
            vmem(m_shape, jnp.float32),
            vmem(acc_shape, jnp.float32),
        ],
        in_specs=[any_space] * 2 + [in_vmem] * 6,
        out_specs=[in_vmem] * 8,
        scratch_shapes=[
            vmem(nodes.shape, jnp.bfloat16),
            vmem(qkv_weight.shape, jnp.bfloat16),
            dma((4, 3 * PIECES)), dma((4, 3 * PIECES)), dma((2, 8)), dma((2, 8)), dma((7,)), dma((7,)),
            dma((PIECES,)), dma(()),
        ],
        compiler_params=pltpu.CompilerParams(
            collective_id=0, has_side_effects=True, vmem_limit_bytes=42 * 2**20
        ),
        name="gather",
    )(nodes, qkv_weight, bias, bucket, key_owner, key_local, query_owner, query_local)


def tile_kernel(
    list_hbm, bias_hbm, table_hbm, m_hbm, l_hbm, acc_hbm, q_ref, kv_ref, part_ref, log_ref,
    list_ref, bias_ref, table_ref, m_ref, l_ref, acc_ref, table_sem, state_sem,
):
    heads = range(PLAN_HEADS)
    z, y, c = coordinates()
    queries = part_ref.shape[0]
    keys = 2 * queries
    waits = ([], [])

    def load(plan, source, target, sem):
        copy = pltpu.make_async_copy(source, target, sem)
        copy.start()
        waits[plan].append(copy)

    load(0, list_hbm, list_ref, table_sem.at[0])
    load(0, table_hbm, table_ref, table_sem.at[1])
    load(0, bias_hbm, bias_ref, table_sem.at[2])
    for plan in range(2):
        own = (z if plan == 0 else y) + plan * RING

        def clear(group, carry):
            @pl.when(group != own)
            def _():
                side = pl.ds(group * LOCAL, LOCAL)
                m_ref[side] = jnp.full((LOCAL, 8, CSIZE), NEVER, jnp.float32)
                l_ref[side] = jnp.zeros((LOCAL, 8, CSIZE), jnp.float32)
                acc_ref[side] = jnp.zeros((LOCAL, PLAN_FEATURES, CSIZE), jnp.float32)
            return carry

        side = pl.ds(own * LOCAL, LOCAL)
        load(plan, m_hbm.at[plan], m_ref.at[side], state_sem.at[plan, 0])
        load(plan, l_hbm.at[plan], l_ref.at[side], state_sem.at[plan, 1])
        load(plan, acc_hbm.at[plan], acc_ref.at[side], state_sem.at[plan, 2])
        lax.fori_loop(plan * RING, (plan + 1) * RING, clear, 0)
    m_ref[queries] = jnp.full((8, CSIZE), NEVER, jnp.float32)
    l_ref[queries] = jnp.zeros((8, CSIZE), jnp.float32)
    acc_ref[queries] = jnp.zeros((PLAN_FEATURES, CSIZE), jnp.float32)

    def batch(step, carry):
        items, pairs = [], []
        for u in range(UNROLL):
            item = list_ref[0, step * UNROLL + u]
            state = lax.bitwise_and(item, 127)
            key = lax.bitwise_and(lax.shift_right_logical(item, 7), 127)
            tile = lax.shift_right_logical(item, 14)
            query = jnp.minimum(state, queries - 1)
            worker = lax.shift_right_logical(tile, 5)
            bucket = table_ref[
                lax.bitwise_and(worker, 1), lax.shift_right_logical(worker, 3),
                lax.bitwise_and(lax.shift_right_logical(worker, 1), 3), 0, lax.bitwise_and(tile, 31),
            ]
            first = jnp.where(key >= keys // 2, PLAN_HEADS, 0)
            items.append((state, [bias_ref[first + h, 0, bucket] for h in heads]))
            pairs.append((
                lambda h, i=query: q_ref[i, rows(h), :],
                lambda h, i=key: kv_ref[i, rows(h), :],
                lambda h, i=key: kv_ref[i, rows(h, PLAN_FEATURES), :],
            ))
        for (state, bias), (highest, mixed) in zip(items, attend(pairs)):
            tops = [top + b for top, b in zip(highest, bias)]
            old_m = [m_ref[state, h : h + 1, :] for h in heads]
            old_l = [l_ref[state, h : h + 1, :] for h in heads]
            old_acc = [acc_ref[state, rows(h), :] for h in heads]
            new_m = [jnp.maximum(a, b) for a, b in zip(old_m, tops)]
            keep = [jnp.exp2(a - b) for a, b in zip(old_m, new_m)]
            fresh = [jnp.exp2(a - b) for a, b in zip(tops, new_m)]
            for h in heads:
                m_ref[state, h : h + 1, :] = new_m[h]
                l_ref[state, h : h + 1, :] = old_l[h] * keep[h] + mixed[h][HEAD_SIZE : HEAD_SIZE + 1] * fresh[h]
                acc_ref[state, rows(h), :] = old_acc[h] * keep[h] + mixed[h][:HEAD_SIZE] * fresh[h]
        return carry

    for copy in waits[0]:
        copy.wait()
    split = lax.div(list_ref[0, LIST_MAX - 2], UNROLL)
    lax.fori_loop(0, split, batch, 0)
    for copy in waits[1]:
        copy.wait()
    lax.fori_loop(split, lax.div(list_ref[0, LIST_MAX - 1] + UNROLL - 1, UNROLL), batch, 0)

    def finish(group, carry):
        for local in range(LOCAL):
            state = group * LOCAL + local
            for h in heads:
                total = l_ref[state, h : h + 1, :]
                held = total > 0
                safe = jnp.where(held, total, 1.0)
                part_ref[group * LOCAL + local % 2 * RING + local // 2, rows(h), :] = (acc_ref[state, rows(h), :] * (1.0 / safe)).astype(jnp.bfloat16)
                row = local // 2 % 2 * PLAN_HEADS + h
                log_ref[group, local % 2, local // 4, row : row + 1, :] = m_ref[state, h : h + 1, :] + jnp.log2(safe)
        return carry

    lax.fori_loop(0, queries // LOCAL, finish, 0)


def tiles(items, bias, table, m, l, acc, q_all, kv_all):
    queries, keys = 2 * RING * LOCAL, 2 * RING * 2 * LOCAL
    in_vmem = pl.BlockSpec(memory_space=pltpu.VMEM)
    part_shape = (queries, PLAN_FEATURES, CSIZE)
    log_shape = (2 * RING, 2, 2, 8, CSIZE)
    dma, vmem = pltpu.SemaphoreType.DMA, pltpu.VMEM
    return pl.pallas_call(
        tile_kernel,
        in_specs=[in_vmem] * 8,
        out_specs=[in_vmem] * 2,
        scratch_shapes=[
                pltpu.SMEM((1, LIST_MAX), jnp.int32),
                pltpu.SMEM((2 * PLAN_HEADS, 1, 128), jnp.float32),
                pltpu.SMEM((2, RING, RING, 1, 128), jnp.int32),
                vmem((queries + 1, 8, CSIZE), jnp.float32),
                vmem((queries + 1, 8, CSIZE), jnp.float32),
                vmem((queries + 1, PLAN_FEATURES, CSIZE), jnp.float32),
            dma((3,)), dma((2, 3)),
        ],
        out_shape=[vmem(part_shape, jnp.bfloat16), vmem(log_shape, jnp.float32)],
        compiler_params=pltpu.CompilerParams(vmem_limit_bytes=16 * 2**20),
        name="tiles",
    )(
        items, bias, table, m, l, acc,
        q_all.reshape(queries, PLAN_FEATURES, CSIZE), kv_all.reshape(keys, 2 * PLAN_FEATURES, CSIZE),
    )


def tail_kernel(
    part_ref, log_ref, nodes_ref, wo_hbm, up_hbm, down_hbm, out_ref,
    wo_ref, up_ref, down_ref, rows_ref, part_in, log_in, far_part, far_log, both_part, both_log, merged, gathered, resid_ref, normed_ref, staged,
    weight_sem, back_send, back_recv, x_send, x_recv, out_send, out_recv, out_own,
):
    z, y, c = coordinates()
    me = lax.axis_index("owner")
    x = lax.axis_index("head")
    heads = range(PLAN_HEADS)
    features = 2 * PLAN_FEATURES

    def load(source, target, sem):
        copy = pltpu.make_async_copy(source, target, sem)
        copy.start()
        return copy

    def across(step):
        return (me, place(x, step))

    partners = [ring_at(axis, step) for axis in "zy" for step in (1, 3)] + [across(step) for step in (1, 2, 3)]
    greet(partners)
    ways = ((0, 1), (1, -1))
    ring = [(0, "z", z), (1, "y", y)]
    half = lambda h: pl.ds(h * (RING // 2), RING // 2)
    weights = [
        load(nodes_ref.at[pl.ds(x * 2 * CSIZE, 2 * CSIZE)], rows_ref, weight_sem.at[0]),
        load(wo_hbm, wo_ref, weight_sem.at[1]),
        load(up_hbm, up_ref, weight_sem.at[2]),
        load(down_hbm, down_ref, weight_sem.at[3]),
    ]
    greeted(partners)
    sent = []

    def send(src, dst, send_sem, recv_sem, device):
        copy = pltpu.make_async_remote_copy(
            src_ref=src, dst_ref=dst, send_sem=send_sem, recv_sem=recv_sem,
            device_id=device, device_id_type=MESH,
        )
        copy.start()
        sent.append(copy)

    def arrived(ref, sem):
        pltpu.make_async_remote_copy(
            src_ref=ref, dst_ref=ref, send_sem=x_send.at[0, 0], recv_sem=sem,
            device_id=across(1), device_id_type=MESH,
        ).wait_recv()

    def back(plan, way, turn, kind, src, dst, device):
        send(src, dst, back_send.at[plan, way, turn, kind], back_recv.at[plan, way, turn, kind], device)

    def send_out(turn):
        t, first, count = TURNS[turn]
        lanes = pl.ds(first, count)
        for plan, axis, at in ring:
            for way, step in ways:
                to, far = ring_at(axis, step), place(at, 2)
                back(plan, way, turn, 0, part_ref.at[plan, far, t, half(way), :, lanes], far_part.at[plan, way, t, :, :, lanes], to)
                back(plan, way, turn, 1, log_ref.at[plan, far, t, way, :, lanes], far_log.at[plan, way, t, :, lanes], to)
        for plan, axis, at in ring:
            for way, step in ways:
                to, next_at = ring_at(axis, step), place(at, step)
                back(
                    plan, way, turn, 2, part_ref.at[plan, next_at, t, half(1 - way), :, lanes],
                    part_in.at[plan, way, t, half(1 - way), :, lanes], to,
                )
                back(
                    plan, way, turn, 3, log_ref.at[plan, next_at, t, 1 - way, :, lanes],
                    log_in.at[plan, way, t, 1 - way, :, lanes], to,
                )

    def combine(turn):
        t, first, count = TURNS[turn]
        lanes = pl.ds(first, count)
        span = slice(first, first + count)
        for plan, axis, at in ring:
            for way, step in ways:
                arrived(far_part.at[plan, way, t, :, :, lanes], back_recv.at[plan, way, turn, 0])
                arrived(far_log.at[plan, way, t, :, lanes], back_recv.at[plan, way, turn, 1])
                one, two = log_ref[plan, place(at, step), t, way, :, span], far_log[plan, way, t, :, span]
                best = jnp.maximum(one, two)
                shares = [jnp.exp2(one - best), jnp.exp2(two - best)]
                total = shares[0] + shares[1]
                both_log[plan, way, t, :, span] = best + jnp.log2(total)
                scale = 1.0 / total
                shares = [share * scale for share in shares]
                for to in range(2):
                    for h in heads:
                        row = to * PLAN_HEADS + h
                        both_part[plan, way, t, to, rows(h), span] = (
                            part_ref[plan, place(at, step), t, way * 2 + to, rows(h), span].astype(jnp.float32) * shares[0][row : row + 1]
                            + far_part[plan, way, t, to, rows(h), span].astype(jnp.float32) * shares[1][row : row + 1]
                        ).astype(jnp.bfloat16)
                to = ring_at(axis, step)
                back(
                    plan, way, turn, 4, both_part.at[plan, way, t, :, :, lanes],
                    part_in.at[plan, way, t, half(way), :, lanes], to,
                )
                back(
                    plan, way, turn, 5, both_log.at[plan, way, t, :, lanes], log_in.at[plan, way, t, way, :, lanes], to
                )

    mine = pl.ds(pl.multiple_of(x * features, 64), features)

    def merge(turn):
        t, first, count = TURNS[turn]
        lanes = pl.ds(first, count)
        span = slice(first, first + count)
        for plan in range(2):
            for way in range(2):
                arrived(part_in.at[plan, way, t, half(1 - way), :, lanes], back_recv.at[plan, way, turn, 2])
                arrived(log_in.at[plan, way, t, 1 - way, :, lanes], back_recv.at[plan, way, turn, 3])
                arrived(part_in.at[plan, way, t, half(way), :, lanes], back_recv.at[plan, way, turn, 4])
                arrived(log_in.at[plan, way, t, way, :, lanes], back_recv.at[plan, way, turn, 5])
        for plan, axis, at in ring:
            for to in range(RING):
                h0 = to // 2
                logs = [log_ref[plan, at, t, h0, :, span]] + [log_in[plan, way, t, h0, :, span] for way in range(2)]
                best = jnp.maximum(jnp.maximum(logs[0], logs[1]), logs[2])
                shares = [jnp.exp2(log - best) for log in logs]
                scale = 1.0 / (shares[0] + shares[1] + shares[2])
                shares = [share * scale for share in shares]
                for h in heads:
                    row = to % 2 * PLAN_HEADS + h
                    total = part_ref[plan, at, t, to, rows(h), span].astype(jnp.float32) * shares[0][row : row + 1]
                    for way in range(2):
                        total += part_in[plan, way, t, to, rows(h), span].astype(jnp.float32) * shares[way + 1][row : row + 1]
                    merged[t, to, rows(h, plan * PLAN_FEATURES), span] = total.astype(jnp.bfloat16)
        for step in (2, 1, 3):
            send(
                merged.at[t, place(x, step), :, lanes], gathered.at[t, mine, lanes],
                x_send.at[turn, step - 1], x_recv.at[turn, step - 1], across(step),
            )
        gathered[t, mine, span] = merged[t, x, :, span]

    wide = up_ref.shape[1] // BLOCKS
    out_copies = []

    def begin(turn):
        t, first, count = TURNS[turn]
        lanes = pl.ds(first, count)
        part = slice(t * CSIZE + first, t * CSIZE + first + count)
        for step in (1, 2, 3):
            source = place(x, -step)
            arrived(gathered.at[t, pl.ds(pl.multiple_of(source * features, 64), features), lanes], x_recv.at[turn, step - 1])
        mixed = lax.dot_general(
            gathered[t, :, first : first + count], wo_ref[...], (((0,), (0,)), ((), ())), preferred_element_type=jnp.float32
        )
        resid = rows_ref[part, :].astype(jnp.float32) + mixed
        resid_ref[part, :] = resid
        normed_ref[part, :] = norm_rows(resid).astype(jnp.bfloat16)

    def feed(turn, start, end):
        t, first, count = TURNS[turn]
        part = slice(t * CSIZE + first, t * CSIZE + first + count)

        def block(step, carry):
            units = pl.ds(pl.multiple_of(step * wide, 128), wide)
            hidden = jax.nn.gelu(
                jnp.dot(normed_ref[part, :], up_ref[:, units], preferred_element_type=jnp.float32)
            ).astype(jnp.bfloat16)
            resid_ref[part, :] += jnp.dot(hidden, down_ref[units, :], preferred_element_type=jnp.float32)
            return carry

        lax.fori_loop(start, end, block, 0)

    def hand_out(turn):
        t, first, count = TURNS[turn]
        part = slice(t * CSIZE + first, t * CSIZE + first + count)
        staged[:, part] = resid_ref[part, :].astype(jnp.bfloat16).T
        target = out_ref.at[:, pl.ds(pl.multiple_of((x * 2 + t) * CSIZE + first, 128), count)]
        block = lambda j: staged.at[pl.ds(pl.multiple_of(j * features, 64), features), part]
        for step in (2, 1, 3):
            send(
                block(place(x, step)), target, out_send.at[turn, step - 1], out_recv.at[turn, step - 1], across(step)
            )
        out_copies.append(load(block(x), target, out_own.at[turn]))

    send_out(0)
    combine(0)
    send_out(1)
    send_out(2)
    merge(0)
    combine(1)
    combine(2)
    merge(1)
    for copy in weights:
        copy.wait()
    begin(0)
    feed(0, 0, BLOCKS // 2)
    merge(2)
    feed(0, BLOCKS // 2, BLOCKS)
    hand_out(0)
    for turn in (1, 2):
        begin(turn)
        feed(turn, 0, BLOCKS)
        hand_out(turn)
    for turn, (t, first, count) in enumerate(TURNS):
        for step in (1, 2, 3):
            source = place(x, -step)
            arrived(
                out_ref.at[:, pl.ds(pl.multiple_of((source * 2 + t) * CSIZE + first, 128), count)],
                out_recv.at[turn, step - 1],
            )
    for copy in out_copies:
        copy.wait()
    for copy in sent:
        copy.wait_send()


def tail(parts, logs, nodes, out_weight, up_weight, down_weight):
    any_space = pl.BlockSpec(memory_space=pl.ANY)
    dma, vmem = pltpu.SemaphoreType.DMA, pltpu.VMEM
    width = nodes.shape[1]
    features = 2 * PLAN_FEATURES
    return pl.pallas_call(
        tail_kernel,
        out_shape=jax.ShapeDtypeStruct((features, nodes.shape[0]), jnp.bfloat16),
        in_specs=[pl.BlockSpec(memory_space=pltpu.VMEM)] * 2 + [any_space] * 4,
        out_specs=any_space,
        scratch_shapes=[
            vmem(out_weight.shape, jnp.bfloat16),
            vmem(up_weight.shape, jnp.bfloat16),
            vmem(down_weight.shape, jnp.bfloat16),
            vmem((2 * CSIZE, width), jnp.bfloat16),
            vmem((2, 2, 2, RING, PLAN_FEATURES, CSIZE), jnp.bfloat16),
            vmem((2, 2, 2, 2, 8, CSIZE), jnp.float32),
            vmem((2, 2, 2, 2, PLAN_FEATURES, CSIZE), jnp.bfloat16),
            vmem((2, 2, 2, 8, CSIZE), jnp.float32),
            vmem((2, 2, 2, 2, PLAN_FEATURES, CSIZE), jnp.bfloat16),
            vmem((2, 2, 2, 8, CSIZE), jnp.float32),
            vmem((2, RING, features, CSIZE), jnp.bfloat16),
            vmem((2, width, CSIZE), jnp.bfloat16),
            vmem((2 * CSIZE, width), jnp.float32),
            vmem((2 * CSIZE, width), jnp.bfloat16),
            vmem((RING * features, 2 * CSIZE), jnp.bfloat16),
            dma((4,)), dma((2, 2, 3, 6)), dma((2, 2, 3, 6)),
            dma((3, 3)), dma((3, 3)), dma((3, 3)), dma((3, 3)), dma((3,)),
        ],
        compiler_params=pltpu.CompilerParams(
            collective_id=1, has_side_effects=True, vmem_limit_bytes=32 * 2**20
        ),
        name="tail",
    )(parts, logs, nodes, out_weight, up_weight, down_weight)


def per_device(
    nodes, qkv_weight, out_weight, hop_bias, up_weight, down_weight,
    key_owner, key_local, query_owner, query_local, hop_bucket,
):
    lists = [array.reshape(8, 128) for array in (key_owner, key_local, query_owner, query_local)]
    q_all, kv_all, table, items, bias, m, l, acc = gather(
        *[pltpu.with_memory_space_constraint(a, pltpu.HBM) for a in (nodes, qkv_weight.swapaxes(1, 2))], hop_bias.T, hop_bucket.reshape(1, -1), *lists
    )
    parts, logs = tiles(items, bias, table, m, l, acc, q_all, kv_all)
    return tail(
        parts.reshape(2, RING, 2, RING, PLAN_FEATURES, CSIZE), logs.reshape(2, RING, 2, 2, 8, CSIZE),
        *[pltpu.with_memory_space_constraint(a, pltpu.HBM) for a in (nodes, out_weight, up_weight, down_weight)],
    ).T


def solution(mesh):
    placed = (
        P("owner", None), P(None, None, "head"), P(), P(None, "head"), P(), P(),
        P(), P(), P(), P(), P("owner"),
    )
    return jax.shard_map(
        per_device, mesh=mesh, in_specs=placed, out_specs=P("owner", "head"), check_vma=False
    )
```

```python
import functools
import math

import jax
import jax.numpy as jnp
from jax import lax
from jax.experimental import pallas as pl
from jax.experimental.pallas import tpu as pltpu
from jax.sharding import PartitionSpec as P

CSIZE = 256
EPSILON = 1e-05
RING = 4
LOCAL = 8
PLAN_HEADS = 3
HEAD_SIZE = 32
PLAN_FEATURES = PLAN_HEADS * HEAD_SIZE
LIST_MAX = 640
UNROLL = 4
MESH = pl.DeviceIdType.MESH
LOG2E = math.log2(math.e)
NEVER = -1e30
NOTHING = 64
PIECES = 4
BLOCKS = 2
TURNS = ((0, 0, 256), (1, 0, 128), (1, 128, 128))


def norm_rows(values):
    center = values - jnp.mean(values, axis=-1, keepdims=True)
    spread = jnp.mean(center * center, axis=-1, keepdims=True)
    return center * lax.rsqrt(spread + EPSILON)


def coordinates():
    me = lax.axis_index("owner")
    return lax.div(me, 8), lax.rem(lax.div(me, 2), 4), lax.rem(me, 2)


def place(at, step):
    return lax.rem(at + step + RING, RING)


def ring_at(axis, step):
    z, y, c = coordinates()
    if axis == "z":
        z = place(z, step)
    else:
        y = place(y, step)
    return ((z * 4 + y) * 2 + c, lax.axis_index("head"))


def sibling():
    z, y, c = coordinates()
    return ((z * 4 + y) * 2 + 1 - c, lax.axis_index("head"))


def greet(partners):
    for partner in partners:
        pl.semaphore_signal(pltpu.get_barrier_semaphore(), inc=1, device_id=partner, device_id_type=MESH)


def greeted(partners):
    pl.semaphore_wait(pltpu.get_barrier_semaphore(), len(partners))


def rows(h, first=0):
    return slice(first + HEAD_SIZE * h, first + HEAD_SIZE * (h + 1))


def attend(pairs):
    heads = range(PLAN_HEADS)
    ones = jnp.ones((16, CSIZE), jnp.bfloat16)
    scored = [
        [
            lax.dot_general(key(h), query(h), (((0,), (0,)), ((), ())), preferred_element_type=jnp.float32)
            for h in heads
        ]
        for query, key, value in pairs
    ]
    done = []
    for (query, key, value), scores in zip(pairs, scored):
        highest = [jnp.max(s, axis=0, keepdims=True) for s in scores]
        weights = [jnp.exp2(s - top).astype(jnp.bfloat16) for s, top in zip(scores, highest)]
        mixed = [
            jnp.dot(jnp.concatenate([value(h), ones], 0), weights[h], preferred_element_type=jnp.float32)
            for h in heads
        ]
        done.append((highest, mixed))
    return done


def make_list(query_owner, query_local, key_owner, key_local):
    z, y, c = coordinates()
    div, rem = lax.div, lax.rem
    qz, qy, qc = div(query_owner, 8), rem(div(query_owner, 2), 4), rem(query_owner, 2)
    kz, ky, kc = div(key_owner, 8), rem(div(key_owner, 2), 4), rem(key_owner, 2)
    iota = lax.broadcasted_iota
    number = iota(jnp.int32, (8, 128), 0) * 128 + iota(jnp.int32, (8, 128), 1)

    def seen(d):
        d = rem(d + RING, RING)
        return jnp.where(d == 0, 0, jnp.where(d == RING - 1, 1, d + 1))

    def table(mine, q_seen, k_seen, plan):
        near = k_seen != RING - 1
        state = plan * RING * LOCAL + q_seen * LOCAL + query_local
        item = state + (jnp.where(near, k_seen * 2 * LOCAL, 0) + kc * LOCAL + key_local) * 128 + number * 16384
        early = mine & near & (q_seen != RING - 1)
        flag = lambda f: jnp.where(f, jnp.ones((8, 128), jnp.float32), 0.0)
        return [flag(mine & near), flag(mine & (k_seen == RING - 1)), jnp.where(early, state, -1).astype(jnp.float32), item.astype(jnp.float32)]

    tables = zip(
        table((qy == y) & (qc == c) & (kz == z), seen(qz - z), seen(ky - y), 0),
        table((qz == z) & (qc == c) & (ky == y), seen(qy - y), seen(kz - z), 1),
    )
    near, far, early, items = [jnp.concatenate(pair, 0) for pair in tables]
    early, values = early.T, items.T
    numbers = jnp.concatenate([number, number], 0).astype(jnp.float32).T
    lane = iota(jnp.int32, (128, 128), 1).astype(jnp.float32)
    first = jnp.full((128, 128), 4096.0, jnp.float32)
    for r in range(16):
        first = jnp.minimum(first, jnp.where(early[:, r : r + 1] == lane, numbers[:, r : r + 1], 4096.0))
    first = jnp.min(first, axis=0, keepdims=True)
    slots, chosen = jnp.zeros((128, 128), jnp.float32), jnp.zeros((128, 128), jnp.float32)
    for r in range(16):
        hit = jnp.where((early[:, r : r + 1] == lane) & (numbers[:, r : r + 1] == first), 1.0, 0.0)
        slots += hit * (values[:, r : r + 1] + 1.0)
        chosen += jnp.where(lane == r, jnp.max(hit, axis=1, keepdims=True), 0.0)
    slots = (jnp.sum(slots, axis=0, keepdims=True) - 1.0).astype(jnp.int32)
    near = near * (1.0 - chosen.T[:16])
    before = jnp.where(iota(jnp.int32, (128, 128), 0) < iota(jnp.int32, (128, 128), 1), 1.0, 0.0)

    def ranks(ones, start):
        inside = jnp.dot(ones, before, preferred_element_type=jnp.float32)
        wide = jnp.broadcast_to(jnp.sum(ones, axis=1, keepdims=True), (16, 128))
        ahead = [start]
        for r in range(16):
            ahead.append(ahead[-1] + wide[r : r + 1])
        return inside + jnp.concatenate(ahead[:16], 0), ahead[16]

    near_rank, count = ranks(near, jnp.zeros((1, 128), jnp.float32))
    filled = jnp.floor((count + (UNROLL - 1)) * (1.0 / UNROLL)) * UNROLL
    far_rank, total = ranks(far, filled)
    rank = jnp.where(near > 0, near_rank, jnp.where(far > 0, far_rank, -1.0)).T
    values = values - NOTHING
    place = iota(jnp.int32, (128, LIST_MAX), 1).astype(jnp.float32)
    listed = jnp.zeros((128, LIST_MAX), jnp.float32)
    for r in range(16):
        listed += jnp.where(rank[:, r : r + 1] == place, values[:, r : r + 1], 0.0)
    listed = jnp.sum(listed, axis=0, keepdims=True) + NOTHING
    at = iota(jnp.int32, (1, LIST_MAX), 1)
    repeat = lambda v: jnp.concatenate([v] * (LIST_MAX // 128), 1)
    listed = jnp.where(at == LIST_MAX - 2, repeat(filled), listed)
    listed = jnp.where(at == LIST_MAX - 1, repeat(total), listed)
    return listed.astype(jnp.int32), slots


def gather_kernel(
    nodes_hbm, weight_hbm, bias_in, bucket_ref, ko_ref, kl_ref, qo_ref, ql_ref,
    qg_ref, kn_ref, kf_ref, table_ref, list_ref, bias_ref, m_ref, l_ref, acc_ref,
    nodes_ref, weight_ref, slots_ref, slots_s, table_s, bias_s, scalar_sem,
    ring_send, ring_recv, pair_send, pair_recv, table_send, table_recv, load_sem, weight_sem,
):
    z, y, c = coordinates()
    heads = range(PLAN_HEADS)
    size = LOCAL // PIECES
    partners = [ring_at(axis, step) for axis in "zy" for step in (1, 2, 3)] + [sibling()]
    greet(partners)

    def local_copy(source, target, sem):
        copy = pltpu.make_async_copy(source, target, sem)
        copy.start()
        return copy

    node_rows = lambda p: pl.ds(p * size * CSIZE, size * CSIZE)
    load_nodes = lambda p: local_copy(nodes_hbm.at[node_rows(p)], nodes_ref.at[node_rows(p)], load_sem.at[p])
    node_loads = [load_nodes(0)]
    weight_load = local_copy(weight_hbm, weight_ref, weight_sem)
    node_loads += [load_nodes(p) for p in range(1, PIECES)]
    table_ref[c, z, y] = jnp.concatenate(
        [bucket_ref[...], jnp.zeros((1, 128 - bucket_ref.shape[1]), jnp.int32)], 1
    )
    for i in range(2 * PLAN_HEADS):
        bias_ref[i, :, : bias_in.shape[1]] = bias_in[i : i + 1] * LOG2E
    sent = []

    def part(p):
        return pl.ds(p * size, size)

    def side(h):
        return pl.ds(h * (LOCAL // 2), LOCAL // 2)

    streams = []
    for plan in range(2):
        q_axis, kv_axis = ("z", "y") if plan == 0 else ("y", "z")
        for kind, axis in (("kv", kv_axis), ("q", q_axis)):
            at = z if axis == "z" else y
            if kind == "q":
                slot = lambda p, r, plan=plan: qg_ref.at[plan, p, r]
            else:
                slot = lambda p, r, plan=plan: kf_ref.at[plan, c, r] if p == 3 else kn_ref.at[plan, p, c, r]
            streams.append((len(streams), plan, kind, axis, at, slot))

    def send(src, dst, send_sem, recv_sem, device):
        copy = pltpu.make_async_remote_copy(
            src_ref=src, dst_ref=dst, send_sem=send_sem, recv_sem=recv_sem,
            device_id=device, device_id_type=MESH,
        )
        copy.start()
        sent.append(copy)

    def arrived(ref, sem):
        pltpu.make_async_remote_copy(
            src_ref=ref, dst_ref=ref, send_sem=ring_send.at[0, 0], recv_sem=sem,
            device_id=sibling(), device_id_type=MESH,
        ).wait_recv()

    weight_load.wait()
    def project(cluster, carry):
        normed = norm_rows(nodes_ref[pl.ds(cluster * CSIZE, CSIZE), :].astype(jnp.float32)).astype(jnp.bfloat16)
        for i in range(3):
            projected = lax.dot_general(
                weight_ref[i], normed, (((1,), (1,)), ((), ())), preferred_element_type=jnp.float32
            )
            if i == 0:
                projected = projected * (LOG2E / math.sqrt(HEAD_SIZE))
            projected = projected.astype(jnp.bfloat16)
            for plan in range(2):
                block = projected[plan * PLAN_FEATURES : (plan + 1) * PLAN_FEATURES]
                if i == 0:
                    qg_ref[plan, 0, cluster] = block
                else:
                    kn_ref[plan, 0, c, cluster, (i - 1) * PLAN_FEATURES : i * PLAN_FEATURES, :] = block
        return carry

    ordered = [s for s in streams if s[2] == "kv"] + [s for s in streams if s[2] == "q"]
    for p in range(PIECES):
        node_loads[p].wait()
        lax.fori_loop(p * size, (p + 1) * size, project, 0)
        if p == 0:
            greeted(partners)
            for step in (1, 2, 3):
                send(table_ref.at[c, z, y], table_ref.at[c, z, y], table_send.at[step - 1], table_recv.at[step - 1], ring_at("y", step))
        for number, plan, kind, axis, at, slot in ordered:
            for way, first, seen in ((1, 0, 1), (-1, PIECES, 2)):
                send(
                    slot(0, part(p)), slot(seen, part(p)),
                    ring_send.at[number, first + p], ring_recv.at[number, first + p], ring_at(axis, way),
                )
        if p % (PIECES // 2) == PIECES // 2 - 1:
            h = p // (PIECES // 2)
            for number, plan, kind, axis, at, slot in ordered:
                if kind == "kv":
                    send(slot(0, side(h)), slot(0, side(h)), pair_send.at[plan, h], pair_recv.at[plan, h], sibling())
    listed, slots = make_list(qo_ref[...], ql_ref[...], ko_ref[...], kl_ref[...])
    list_ref[...] = listed
    slots_ref[...] = slots
    m_ref[...] = jnp.full(m_ref.shape, NEVER, jnp.float32)
    l_ref[...] = jnp.zeros(l_ref.shape, jnp.float32)
    acc_ref[...] = jnp.zeros(acc_ref.shape, jnp.float32)
    scalars = [local_copy(slots_ref, slots_s, scalar_sem.at[0]), local_copy(bias_ref, bias_s, scalar_sem.at[1])]

    for plan in range(2):
        bias = [bias_ref[plan * PLAN_HEADS + h, :, 0:1] for h in heads]

        def own_tiles(step, carry):
            group = [step * UNROLL + u for u in range(UNROLL)]
            pairs = [
                (
                    lambda h, i=i: qg_ref[plan, 0, i, rows(h), :],
                    lambda h, i=i: kn_ref[plan, 0, c, i, rows(h), :],
                    lambda h, i=i: kn_ref[plan, 0, c, i, rows(h, PLAN_FEATURES), :],
                )
                for i in group
            ]
            for i, (highest, mixed) in zip(group, attend(pairs)):
                for h in heads:
                    m_ref[plan, i, h : h + 1, :] = highest[h] + bias[h]
                    l_ref[plan, i, h : h + 1, :] = mixed[h][HEAD_SIZE : HEAD_SIZE + 1]
                    acc_ref[plan, i, rows(h), :] = mixed[h][:HEAD_SIZE]
            return carry

        lax.fori_loop(0, LOCAL // UNROLL, own_tiles, 0)
    for step in (1, 2, 3):
        arrived(table_ref.at[c, z, place(y, -step)], table_recv.at[step - 1])
    for step in (1, 2, 3):
        send(table_ref.at[c, z], table_ref.at[c, z], table_send.at[2 + step], table_recv.at[2 + step], ring_at("z", step))
    for h in range(2):
        for p in range(h * PIECES // 2, (h + 1) * PIECES // 2):
            for number, plan, kind, axis, at, slot in ordered:
                before, after = slot(1, part(p)), slot(2, part(p))
                arrived(before, ring_recv.at[number, p])
                arrived(after, ring_recv.at[number, PIECES + p])
                onward, way = (before, 1) if p % 2 == 0 else (after, -1)
                far = 2 * PIECES + p
                send(onward, slot(3, part(p)), ring_send.at[number, far], ring_recv.at[number, far], ring_at(axis, way))
        for number, plan, kind, axis, at, slot in ordered:
            if kind == "kv":
                for index, step in ((1, -1), (2, 1)):
                    block, sem = slot(index, side(h)), 2 * index + h
                    send(block, block, pair_send.at[plan, sem], pair_recv.at[plan, sem], sibling())
        if h == 0:
            for step in (1, 2, 3):
                arrived(table_ref.at[c, place(z, -step)], table_recv.at[2 + step])
            send(table_ref.at[c], table_ref.at[c], table_send.at[6], table_recv.at[6], sibling())
    arrived(table_ref.at[1 - c], table_recv.at[6])
    scalars.append(local_copy(table_ref, table_s, scalar_sem.at[2]))
    for plan in range(2):
        for index in range(3):
            for h in range(2):
                arrived(kn_ref.at[plan, index, 1 - c, side(h)], pair_recv.at[plan, 2 * index + h])
    for copy in scalars:
        copy.wait()
    for plan in range(2):

        def early_tiles(step, carry):
            group, pairs = [], []
            for u in range(UNROLL):
                i = step * UNROLL + u
                item = slots_s[0, plan * RING * LOCAL + i]
                valid = item >= 0
                item = jnp.maximum(item, 0)
                key = lax.bitwise_and(lax.shift_right_logical(item, 7), 127)
                tile = lax.bitwise_and(lax.shift_right_logical(item, 14), 1023)
                worker = lax.shift_right_logical(tile, 5)
                bucket = table_s[
                    lax.bitwise_and(worker, 1), lax.shift_right_logical(worker, 3),
                    lax.bitwise_and(lax.shift_right_logical(worker, 1), 3), 0, lax.bitwise_and(tile, 31),
                ]
                bucket = lax.bitwise_and(bucket, 31)
                place_of = (jnp.minimum(lax.shift_right_logical(key, 4), 2), lax.bitwise_and(lax.shift_right_logical(key, 3), 1), lax.bitwise_and(key, 7))
                group.append((i, valid, [bias_s[plan * PLAN_HEADS + h, 0, bucket] for h in heads]))
                pairs.append((
                    lambda h, i=i: qg_ref[plan, lax.div(i, LOCAL), lax.rem(i, LOCAL), rows(h), :],
                    lambda h, k=place_of: kn_ref[plan, k[0], k[1], k[2], rows(h), :],
                    lambda h, k=place_of: kn_ref[plan, k[0], k[1], k[2], rows(h, PLAN_FEATURES), :],
                ))
            for (i, valid, bias), (highest, mixed) in zip(group, attend(pairs)):
                for h in heads:
                    top = jnp.where(valid, highest[h] + bias[h], NEVER)
                    old_m, old_l, old_acc = m_ref[plan, i, h : h + 1, :], l_ref[plan, i, h : h + 1, :], acc_ref[plan, i, rows(h), :]
                    new_m = jnp.maximum(old_m, top)
                    keep = jnp.exp2(old_m - new_m)
                    fresh = jnp.where(valid, jnp.exp2(top - new_m), 0.0)
                    m_ref[plan, i, h : h + 1, :] = new_m
                    l_ref[plan, i, h : h + 1, :] = old_l * keep + mixed[h][HEAD_SIZE : HEAD_SIZE + 1] * fresh
                    acc_ref[plan, i, rows(h), :] = old_acc * keep + mixed[h][:HEAD_SIZE] * fresh
            return carry

        lax.fori_loop(0, 3 * LOCAL // UNROLL, early_tiles, 0)
        h = plan
        for number, kv_plan, kind, axis, at, slot in ordered:
            for p in range(h * PIECES // 2, (h + 1) * PIECES // 2):
                arrived(slot(3, part(p)), ring_recv.at[number, 2 * PIECES + p])
            if kind == "kv":
                far = slot(3, side(h))
                send(far, far, pair_send.at[kv_plan, 6 + h], pair_recv.at[kv_plan, 6 + h], sibling())
    for plan in range(2):
        for h in range(2):
            arrived(kf_ref.at[plan, 1 - c, side(h)], pair_recv.at[plan, 6 + h])
    for copy in sent:
        copy.wait_send()


def gather(nodes, qkv_weight, bias, bucket, key_owner, key_local, query_owner, query_local):
    any_space, in_vmem = pl.BlockSpec(memory_space=pl.ANY), pl.BlockSpec(memory_space=pltpu.VMEM)
    dma, vmem = pltpu.SemaphoreType.DMA, pltpu.VMEM
    q_shape, kv_shape = (PLAN_FEATURES, CSIZE), (2 * PLAN_FEATURES, CSIZE)
    m_shape, acc_shape = (2, 3 * LOCAL, 8, CSIZE), (2, 3 * LOCAL, PLAN_FEATURES, CSIZE)
    return pl.pallas_call(
        gather_kernel,
        out_shape=[
            vmem((2, RING, LOCAL) + q_shape, jnp.bfloat16),
            vmem((2, 3, 2, LOCAL) + kv_shape, jnp.bfloat16),
            vmem((2, 2, LOCAL) + kv_shape, jnp.bfloat16),
            vmem((2, RING, RING, 1, 128), jnp.int32),
            vmem((1, LIST_MAX), jnp.int32),
            vmem((2 * PLAN_HEADS, 1, 128), jnp.float32),
            vmem(m_shape, jnp.float32),
            vmem(m_shape, jnp.float32),
            vmem(acc_shape, jnp.float32),
        ],
        in_specs=[any_space] * 2 + [in_vmem] * 6,
        out_specs=[in_vmem] * 9,
        scratch_shapes=[
            vmem(nodes.shape, jnp.bfloat16),
            vmem(qkv_weight.shape, jnp.bfloat16),
            vmem((1, 128), jnp.int32),
            pltpu.SMEM((1, 128), jnp.int32),
            pltpu.SMEM((2, RING, RING, 1, 128), jnp.int32),
            pltpu.SMEM((2 * PLAN_HEADS, 1, 128), jnp.float32),
            dma((3,)),
            dma((4, 3 * PIECES)), dma((4, 3 * PIECES)), dma((2, 8)), dma((2, 8)), dma((7,)), dma((7,)),
            dma((PIECES,)), dma(()),
        ],
        compiler_params=pltpu.CompilerParams(
            collective_id=0, has_side_effects=True, vmem_limit_bytes=42 * 2**20
        ),
        name="gather",
    )(nodes, qkv_weight, bias, bucket, key_owner, key_local, query_owner, query_local)


def tile_kernel(
    list_hbm, bias_hbm, table_hbm, m0_ref, l0_ref, acc0_ref, q_ref, kn_ref, kf_ref, part_ref, log_ref,
    list_ref, bias_ref, table_ref, m_ref, l_ref, acc_ref, table_sem,
):
    heads = range(PLAN_HEADS)
    queries = part_ref.shape[0]
    waits = []
    for i, (source, target) in enumerate(((list_hbm, list_ref), (table_hbm, table_ref), (bias_hbm, bias_ref))):
        waits.append(pltpu.make_async_copy(source, target, table_sem.at[i]))
        waits[-1].start()
    m_ref[...] = jnp.full(m_ref.shape, NEVER, jnp.float32)
    l_ref[...] = jnp.zeros(l_ref.shape, jnp.float32)
    acc_ref[...] = jnp.zeros(acc_ref.shape, jnp.float32)

    def batch(kv_ref, step, carry):
        items, pairs = [], []
        for u in range(UNROLL):
            item = list_ref[0, step * UNROLL + u]
            state = lax.bitwise_and(item, 127)
            key = lax.bitwise_and(lax.shift_right_logical(item, 7), 127)
            tile = lax.shift_right_logical(item, 14)
            query = jnp.minimum(state, queries - 1)
            plan = lax.shift_right_logical(query, 5)
            key = plan * (kv_ref.shape[0] // 2) + key
            worker = lax.shift_right_logical(tile, 5)
            bucket = table_ref[
                lax.bitwise_and(worker, 1), lax.shift_right_logical(worker, 3),
                lax.bitwise_and(lax.shift_right_logical(worker, 1), 3), 0, lax.bitwise_and(tile, 31),
            ]
            items.append((state, [bias_ref[plan * PLAN_HEADS + h, 0, bucket] for h in heads]))
            pairs.append((
                lambda h, i=query: q_ref[i, rows(h), :],
                lambda h, i=key: kv_ref[i, rows(h), :],
                lambda h, i=key: kv_ref[i, rows(h, PLAN_FEATURES), :],
            ))
        for (state, bias), (highest, mixed) in zip(items, attend(pairs)):
            tops = [top + b for top, b in zip(highest, bias)]
            old_m = [m_ref[state, h : h + 1, :] for h in heads]
            old_l = [l_ref[state, h : h + 1, :] for h in heads]
            old_acc = [acc_ref[state, rows(h), :] for h in heads]
            new_m = [jnp.maximum(a, b) for a, b in zip(old_m, tops)]
            keep = [jnp.exp2(a - b) for a, b in zip(old_m, new_m)]
            fresh = [jnp.exp2(a - b) for a, b in zip(tops, new_m)]
            for h in heads:
                m_ref[state, h : h + 1, :] = new_m[h]
                l_ref[state, h : h + 1, :] = old_l[h] * keep[h] + mixed[h][HEAD_SIZE : HEAD_SIZE + 1] * fresh[h]
                acc_ref[state, rows(h), :] = old_acc[h] * keep[h] + mixed[h][:HEAD_SIZE] * fresh[h]
        return carry

    for copy in waits:
        copy.wait()
    split = lax.div(list_ref[0, LIST_MAX - 2], UNROLL)
    lax.fori_loop(0, split, functools.partial(batch, kn_ref), 0)
    lax.fori_loop(
        split, lax.div(list_ref[0, LIST_MAX - 1] + UNROLL - 1, UNROLL), functools.partial(batch, kf_ref), 0
    )

    def finish(plan, group, near):
        base = plan * RING + group
        for local in range(LOCAL):
            state = base * LOCAL + local
            for h in heads:
                best, total = m_ref[state, h : h + 1, :], l_ref[state, h : h + 1, :]
                acc = acc_ref[state, rows(h), :]
                if near:
                    other = group * LOCAL + local
                    late, early = best, m0_ref[plan, other, h : h + 1, :]
                    best = jnp.maximum(late, early)
                    shares = jnp.exp2(late - best), jnp.exp2(early - best)
                    total = total * shares[0] + l0_ref[plan, other, h : h + 1, :] * shares[1]
                    acc = acc * shares[0] + acc0_ref[plan, other, rows(h), :] * shares[1]
                safe = jnp.where(total > 0, total, 1.0)
                part_ref[base * LOCAL + local % 2 * RING + local // 2, rows(h), :] = (acc * (1.0 / safe)).astype(jnp.bfloat16)
                row = local // 2 % 2 * PLAN_HEADS + h
                log_ref[base, local % 2, local // 4, row : row + 1, :] = best + jnp.log2(safe)

    for plan in range(2):

        def near_group(group, carry):
            finish(plan, group, True)
            return carry

        lax.fori_loop(0, 3, near_group, 0)
        finish(plan, 3, False)


def tiles(items, bias, table, m, l, acc, q_all, kv_near, kv_far):
    queries, keys = 2 * RING * LOCAL, 2 * 2 * LOCAL
    in_vmem = pl.BlockSpec(memory_space=pltpu.VMEM)
    part_shape = (queries, PLAN_FEATURES, CSIZE)
    log_shape = (2 * RING, 2, 2, 8, CSIZE)
    dma, vmem = pltpu.SemaphoreType.DMA, pltpu.VMEM
    return pl.pallas_call(
        tile_kernel,
        in_specs=[in_vmem] * 9,
        out_specs=[in_vmem] * 2,
        scratch_shapes=[
                pltpu.SMEM((1, LIST_MAX), jnp.int32),
                pltpu.SMEM((2 * PLAN_HEADS, 1, 128), jnp.float32),
                pltpu.SMEM((2, RING, RING, 1, 128), jnp.int32),
                vmem((queries + 1, 8, CSIZE), jnp.float32),
                vmem((queries + 1, 8, CSIZE), jnp.float32),
                vmem((queries + 1, PLAN_FEATURES, CSIZE), jnp.float32),
            dma((3,)),
        ],
        out_shape=[vmem(part_shape, jnp.bfloat16), vmem(log_shape, jnp.float32)],
        compiler_params=pltpu.CompilerParams(vmem_limit_bytes=16 * 2**20),
        name="tiles",
    )(
        items, bias, table, m, l, acc,
        q_all.reshape(queries, PLAN_FEATURES, CSIZE),
        kv_near.reshape(3 * keys, 2 * PLAN_FEATURES, CSIZE), kv_far.reshape(keys, 2 * PLAN_FEATURES, CSIZE),
    )


def tail_kernel(
    part_ref, log_ref, nodes_ref, wo_hbm, up_hbm, down_hbm, out_ref,
    wo_ref, up_ref, down_ref, rows_ref, part_in, log_in, far_part, far_log, both_part, both_log, merged, gathered, resid_ref, normed_ref, staged,
    weight_sem, back_send, back_recv, x_send, x_recv, out_send, out_recv, out_own,
):
    z, y, c = coordinates()
    me = lax.axis_index("owner")
    x = lax.axis_index("head")
    heads = range(PLAN_HEADS)
    features = 2 * PLAN_FEATURES

    def load(source, target, sem):
        copy = pltpu.make_async_copy(source, target, sem)
        copy.start()
        return copy

    def across(step):
        return (me, place(x, step))

    partners = [ring_at(axis, step) for axis in "zy" for step in (1, 3)] + [across(step) for step in (1, 2, 3)]
    greet(partners)
    ways = ((0, 1), (1, -1))
    ring = [(0, "z", z), (1, "y", y)]
    half = lambda h: pl.ds(h * (RING // 2), RING // 2)
    weights = [
        load(nodes_ref.at[pl.ds(x * 2 * CSIZE, 2 * CSIZE)], rows_ref, weight_sem.at[0]),
        load(wo_hbm, wo_ref, weight_sem.at[1]),
        load(up_hbm, up_ref, weight_sem.at[2]),
        load(down_hbm, down_ref, weight_sem.at[3]),
    ]
    greeted(partners)
    sent = []

    def send(src, dst, send_sem, recv_sem, device):
        copy = pltpu.make_async_remote_copy(
            src_ref=src, dst_ref=dst, send_sem=send_sem, recv_sem=recv_sem,
            device_id=device, device_id_type=MESH,
        )
        copy.start()
        sent.append(copy)

    def arrived(ref, sem):
        pltpu.make_async_remote_copy(
            src_ref=ref, dst_ref=ref, send_sem=x_send.at[0, 0], recv_sem=sem,
            device_id=across(1), device_id_type=MESH,
        ).wait_recv()

    def back(plan, way, turn, kind, src, dst, device):
        send(src, dst, back_send.at[plan, way, turn, kind], back_recv.at[plan, way, turn, kind], device)

    def send_out(turn):
        t, first, count = TURNS[turn]
        lanes = pl.ds(first, count)
        for plan, axis, at in ring:
            for way, step in ways:
                to, far = ring_at(axis, step), 3
                back(plan, way, turn, 0, part_ref.at[plan, far, t, half(way), :, lanes], far_part.at[plan, way, t, :, :, lanes], to)
                back(plan, way, turn, 1, log_ref.at[plan, far, t, way, :, lanes], far_log.at[plan, way, t, :, lanes], to)
        for plan, axis, at in ring:
            for way, step in ways:
                to, next_at = ring_at(axis, step), 2 - way
                back(
                    plan, way, turn, 2, part_ref.at[plan, next_at, t, half(1 - way), :, lanes],
                    part_in.at[plan, way, t, half(1 - way), :, lanes], to,
                )
                back(
                    plan, way, turn, 3, log_ref.at[plan, next_at, t, 1 - way, :, lanes],
                    log_in.at[plan, way, t, 1 - way, :, lanes], to,
                )

    def combine(turn):
        t, first, count = TURNS[turn]
        lanes = pl.ds(first, count)
        span = slice(first, first + count)
        for plan, axis, at in ring:
            for way, step in ways:
                arrived(far_part.at[plan, way, t, :, :, lanes], back_recv.at[plan, way, turn, 0])
                arrived(far_log.at[plan, way, t, :, lanes], back_recv.at[plan, way, turn, 1])
                one, two = log_ref[plan, 2 - way, t, way, :, span], far_log[plan, way, t, :, span]
                best = jnp.maximum(one, two)
                shares = [jnp.exp2(one - best), jnp.exp2(two - best)]
                total = shares[0] + shares[1]
                both_log[plan, way, t, :, span] = best + jnp.log2(total)
                scale = 1.0 / total
                shares = [share * scale for share in shares]
                for to in range(2):
                    for h in heads:
                        row = to * PLAN_HEADS + h
                        both_part[plan, way, t, to, rows(h), span] = (
                            part_ref[plan, 2 - way, t, way * 2 + to, rows(h), span].astype(jnp.float32) * shares[0][row : row + 1]
                            + far_part[plan, way, t, to, rows(h), span].astype(jnp.float32) * shares[1][row : row + 1]
                        ).astype(jnp.bfloat16)
                to = ring_at(axis, step)
                back(
                    plan, way, turn, 4, both_part.at[plan, way, t, :, :, lanes],
                    part_in.at[plan, way, t, half(way), :, lanes], to,
                )
                back(
                    plan, way, turn, 5, both_log.at[plan, way, t, :, lanes], log_in.at[plan, way, t, way, :, lanes], to
                )

    mine = pl.ds(pl.multiple_of(x * features, 64), features)

    def merge(turn):
        t, first, count = TURNS[turn]
        lanes = pl.ds(first, count)
        span = slice(first, first + count)
        for plan in range(2):
            for way in range(2):
                arrived(part_in.at[plan, way, t, half(1 - way), :, lanes], back_recv.at[plan, way, turn, 2])
                arrived(log_in.at[plan, way, t, 1 - way, :, lanes], back_recv.at[plan, way, turn, 3])
                arrived(part_in.at[plan, way, t, half(way), :, lanes], back_recv.at[plan, way, turn, 4])
                arrived(log_in.at[plan, way, t, way, :, lanes], back_recv.at[plan, way, turn, 5])
        for plan, axis, at in ring:
            for to in range(RING):
                h0 = to // 2
                logs = [log_ref[plan, 0, t, h0, :, span]] + [log_in[plan, way, t, h0, :, span] for way in range(2)]
                best = jnp.maximum(jnp.maximum(logs[0], logs[1]), logs[2])
                shares = [jnp.exp2(log - best) for log in logs]
                scale = 1.0 / (shares[0] + shares[1] + shares[2])
                shares = [share * scale for share in shares]
                for h in heads:
                    row = to % 2 * PLAN_HEADS + h
                    total = part_ref[plan, 0, t, to, rows(h), span].astype(jnp.float32) * shares[0][row : row + 1]
                    for way in range(2):
                        total += part_in[plan, way, t, to, rows(h), span].astype(jnp.float32) * shares[way + 1][row : row + 1]
                    merged[t, to, rows(h, plan * PLAN_FEATURES), span] = total.astype(jnp.bfloat16)
        for step in (2, 1, 3):
            send(
                merged.at[t, place(x, step), :, lanes], gathered.at[t, mine, lanes],
                x_send.at[turn, step - 1], x_recv.at[turn, step - 1], across(step),
            )
        gathered[t, mine, span] = merged[t, x, :, span]

    wide = up_ref.shape[1] // BLOCKS
    out_copies = []

    def begin(turn):
        t, first, count = TURNS[turn]
        lanes = pl.ds(first, count)
        part = slice(t * CSIZE + first, t * CSIZE + first + count)
        for step in (1, 2, 3):
            source = place(x, -step)
            arrived(gathered.at[t, pl.ds(pl.multiple_of(source * features, 64), features), lanes], x_recv.at[turn, step - 1])
        mixed = lax.dot_general(
            gathered[t, :, first : first + count], wo_ref[...], (((0,), (0,)), ((), ())), preferred_element_type=jnp.float32
        )
        resid = rows_ref[part, :].astype(jnp.float32) + mixed
        resid_ref[part, :] = resid
        normed_ref[part, :] = norm_rows(resid).astype(jnp.bfloat16)

    def feed(turn, start, end):
        t, first, count = TURNS[turn]
        part = slice(t * CSIZE + first, t * CSIZE + first + count)

        def block(step, carry):
            units = pl.ds(pl.multiple_of(step * wide, 128), wide)
            hidden = jax.nn.gelu(
                jnp.dot(normed_ref[part, :], up_ref[:, units], preferred_element_type=jnp.float32)
            ).astype(jnp.bfloat16)
            resid_ref[part, :] += jnp.dot(hidden, down_ref[units, :], preferred_element_type=jnp.float32)
            return carry

        lax.fori_loop(start, end, block, 0)

    def hand_out(turn):
        t, first, count = TURNS[turn]
        part = slice(t * CSIZE + first, t * CSIZE + first + count)
        staged[:, part] = resid_ref[part, :].astype(jnp.bfloat16).T
        target = out_ref.at[:, pl.ds(pl.multiple_of((x * 2 + t) * CSIZE + first, 128), count)]
        block = lambda j: staged.at[pl.ds(pl.multiple_of(j * features, 64), features), part]
        for step in (2, 1, 3):
            send(
                block(place(x, step)), target, out_send.at[turn, step - 1], out_recv.at[turn, step - 1], across(step)
            )
        out_copies.append(load(block(x), target, out_own.at[turn]))

    send_out(0)
    combine(0)
    send_out(1)
    send_out(2)
    merge(0)
    combine(1)
    combine(2)
    merge(1)
    for copy in weights:
        copy.wait()
    begin(0)
    feed(0, 0, BLOCKS // 2)
    merge(2)
    feed(0, BLOCKS // 2, BLOCKS)
    hand_out(0)
    for turn in (1, 2):
        begin(turn)
        feed(turn, 0, BLOCKS)
        hand_out(turn)
    for turn, (t, first, count) in enumerate(TURNS):
        for step in (1, 2, 3):
            source = place(x, -step)
            arrived(
                out_ref.at[:, pl.ds(pl.multiple_of((source * 2 + t) * CSIZE + first, 128), count)],
                out_recv.at[turn, step - 1],
            )
    for copy in out_copies:
        copy.wait()
    for copy in sent:
        copy.wait_send()


def tail(parts, logs, nodes, out_weight, up_weight, down_weight):
    any_space = pl.BlockSpec(memory_space=pl.ANY)
    dma, vmem = pltpu.SemaphoreType.DMA, pltpu.VMEM
    width = nodes.shape[1]
    features = 2 * PLAN_FEATURES
    return pl.pallas_call(
        tail_kernel,
        out_shape=jax.ShapeDtypeStruct((features, nodes.shape[0]), jnp.bfloat16),
        in_specs=[pl.BlockSpec(memory_space=pltpu.VMEM)] * 2 + [any_space] * 4,
        out_specs=any_space,
        scratch_shapes=[
            vmem(out_weight.shape, jnp.bfloat16),
            vmem(up_weight.shape, jnp.bfloat16),
            vmem(down_weight.shape, jnp.bfloat16),
            vmem((2 * CSIZE, width), jnp.bfloat16),
            vmem((2, 2, 2, RING, PLAN_FEATURES, CSIZE), jnp.bfloat16),
            vmem((2, 2, 2, 2, 8, CSIZE), jnp.float32),
            vmem((2, 2, 2, 2, PLAN_FEATURES, CSIZE), jnp.bfloat16),
            vmem((2, 2, 2, 8, CSIZE), jnp.float32),
            vmem((2, 2, 2, 2, PLAN_FEATURES, CSIZE), jnp.bfloat16),
            vmem((2, 2, 2, 8, CSIZE), jnp.float32),
            vmem((2, RING, features, CSIZE), jnp.bfloat16),
            vmem((2, width, CSIZE), jnp.bfloat16),
            vmem((2 * CSIZE, width), jnp.float32),
            vmem((2 * CSIZE, width), jnp.bfloat16),
            vmem((RING * features, 2 * CSIZE), jnp.bfloat16),
            dma((4,)), dma((2, 2, 3, 6)), dma((2, 2, 3, 6)),
            dma((3, 3)), dma((3, 3)), dma((3, 3)), dma((3, 3)), dma((3,)),
        ],
        compiler_params=pltpu.CompilerParams(
            collective_id=1, has_side_effects=True, vmem_limit_bytes=32 * 2**20
        ),
        name="tail",
    )(parts, logs, nodes, out_weight, up_weight, down_weight)


def per_device(
    nodes, qkv_weight, out_weight, hop_bias, up_weight, down_weight,
    key_owner, key_local, query_owner, query_local, hop_bucket,
):
    lists = [array.reshape(8, 128) for array in (key_owner, key_local, query_owner, query_local)]
    q_all, kv_near, kv_far, table, items, bias, m, l, acc = gather(
        *[pltpu.with_memory_space_constraint(a, pltpu.HBM) for a in (nodes, qkv_weight.swapaxes(1, 2))], hop_bias.T, hop_bucket.reshape(1, -1), *lists
    )
    parts, logs = tiles(items, bias, table, m, l, acc, q_all, kv_near, kv_far)
    return tail(
        parts.reshape(2, RING, 2, RING, PLAN_FEATURES, CSIZE), logs.reshape(2, RING, 2, 2, 8, CSIZE),
        *[pltpu.with_memory_space_constraint(a, pltpu.HBM) for a in (nodes, out_weight, up_weight, down_weight)],
    ).T


def solution(mesh):
    placed = (
        P("owner", None), P(None, None, "head"), P(), P(None, "head"), P(), P(),
        P(), P(), P(), P(), P("owner"),
    )
    return jax.shard_map(
        per_device, mesh=mesh, in_specs=placed, out_specs=P("owner", "head"), check_vma=False
    )
```

```python
import functools
import math

import jax
import jax.numpy as jnp
from jax import lax
from jax.experimental import pallas as pl
from jax.experimental.pallas import tpu as pltpu
from jax.sharding import PartitionSpec as P

CSIZE = 256
EPSILON = 1e-05
RING = 4
LOCAL = 8
PLAN_HEADS = 3
HEAD_SIZE = 32
PLAN_FEATURES = PLAN_HEADS * HEAD_SIZE
LIST_MAX = 640
UNROLL = 4
MESH = pl.DeviceIdType.MESH
LOG2E = math.log2(math.e)
NEVER = -1e30
NOTHING = 64
PIECES = 4
BLOCKS = 2
TURNS = ((0, 0, 256), (1, 0, 128), (1, 128, 128))


def norm_rows(values):
    center = values - jnp.mean(values, axis=-1, keepdims=True)
    spread = jnp.mean(center * center, axis=-1, keepdims=True)
    return center * lax.rsqrt(spread + EPSILON)


def coordinates():
    me = lax.axis_index("owner")
    return lax.div(me, 8), lax.rem(lax.div(me, 2), 4), lax.rem(me, 2)


def place(at, step):
    return lax.rem(at + step + RING, RING)


def ring_at(axis, step):
    z, y, c = coordinates()
    if axis == "z":
        z = place(z, step)
    else:
        y = place(y, step)
    return ((z * 4 + y) * 2 + c, lax.axis_index("head"))


def sibling():
    z, y, c = coordinates()
    return ((z * 4 + y) * 2 + 1 - c, lax.axis_index("head"))


def greet(partners):
    for partner in partners:
        pl.semaphore_signal(pltpu.get_barrier_semaphore(), inc=1, device_id=partner, device_id_type=MESH)


def greeted(partners):
    pl.semaphore_wait(pltpu.get_barrier_semaphore(), len(partners))


def rows(h, first=0):
    return slice(first + HEAD_SIZE * h, first + HEAD_SIZE * (h + 1))


def attend(pairs):
    heads = range(PLAN_HEADS)
    ones = jnp.ones((16, CSIZE), jnp.bfloat16)
    scored = [
        [
            lax.dot_general(key(h), query(h), (((0,), (0,)), ((), ())), preferred_element_type=jnp.float32)
            for h in heads
        ]
        for query, key, value in pairs
    ]
    done = []
    for (query, key, value), scores in zip(pairs, scored):
        highest = [jnp.max(s, axis=0, keepdims=True) for s in scores]
        weights = [jnp.exp2(s - top).astype(jnp.bfloat16) for s, top in zip(scores, highest)]
        mixed = [
            jnp.dot(jnp.concatenate([value(h), ones], 0), weights[h], preferred_element_type=jnp.float32)
            for h in heads
        ]
        done.append((highest, mixed))
    return done


def make_list(query_owner, query_local, key_owner, key_local):
    z, y, c = coordinates()
    div, rem = lax.div, lax.rem
    qz, qy, qc = div(query_owner, 8), rem(div(query_owner, 2), 4), rem(query_owner, 2)
    kz, ky, kc = div(key_owner, 8), rem(div(key_owner, 2), 4), rem(key_owner, 2)
    iota = lax.broadcasted_iota
    number = iota(jnp.int32, (8, 128), 0) * 128 + iota(jnp.int32, (8, 128), 1)

    def seen(d):
        d = rem(d + RING, RING)
        return jnp.where(d == 0, 0, jnp.where(d == RING - 1, 1, d + 1))

    def table(mine, q_seen, k_seen, plan):
        near = k_seen != RING - 1
        state = plan * RING * LOCAL + q_seen * LOCAL + query_local
        item = state + (jnp.where(near, k_seen * 2 * LOCAL, 0) + kc * LOCAL + key_local) * 128 + number * 16384
        early = mine & near & (q_seen != RING - 1)
        flag = lambda f: jnp.where(f, jnp.ones((8, 128), jnp.float32), 0.0)
        return [flag(mine & near), flag(mine & (k_seen == RING - 1)), jnp.where(early, state, -1).astype(jnp.float32), item.astype(jnp.float32)]

    tables = zip(
        table((qy == y) & (qc == c) & (kz == z), seen(qz - z), seen(ky - y), 0),
        table((qz == z) & (qc == c) & (ky == y), seen(qy - y), seen(kz - z), 1),
    )
    near, far, early, items = [jnp.concatenate(pair, 0) for pair in tables]
    early, values = early.T, items.T
    numbers = jnp.concatenate([number, number], 0).astype(jnp.float32).T
    lane = iota(jnp.int32, (128, 128), 1).astype(jnp.float32)
    first = jnp.full((128, 128), 4096.0, jnp.float32)
    for r in range(16):
        first = jnp.minimum(first, jnp.where(early[:, r : r + 1] == lane, numbers[:, r : r + 1], 4096.0))
    first = jnp.min(first, axis=0, keepdims=True)
    slots, chosen = jnp.zeros((128, 128), jnp.float32), jnp.zeros((128, 128), jnp.float32)
    for r in range(16):
        hit = jnp.where((early[:, r : r + 1] == lane) & (numbers[:, r : r + 1] == first), 1.0, 0.0)
        slots += hit * (values[:, r : r + 1] + 1.0)
        chosen += jnp.where(lane == r, jnp.max(hit, axis=1, keepdims=True), 0.0)
    slots = (jnp.sum(slots, axis=0, keepdims=True) - 1.0).astype(jnp.int32)
    near = near * (1.0 - chosen.T[:16])
    before = jnp.where(iota(jnp.int32, (128, 128), 0) < iota(jnp.int32, (128, 128), 1), 1.0, 0.0)

    def ranks(ones, start):
        inside = jnp.dot(ones, before, preferred_element_type=jnp.float32)
        wide = jnp.broadcast_to(jnp.sum(ones, axis=1, keepdims=True), (16, 128))
        ahead = [start]
        for r in range(16):
            ahead.append(ahead[-1] + wide[r : r + 1])
        return inside + jnp.concatenate(ahead[:16], 0), ahead[16]

    near_rank, count = ranks(near, jnp.zeros((1, 128), jnp.float32))
    filled = jnp.floor((count + (UNROLL - 1)) * (1.0 / UNROLL)) * UNROLL
    far_rank, total = ranks(far, filled)
    rank = jnp.where(near > 0, near_rank, jnp.where(far > 0, far_rank, -1.0)).T
    values = values - NOTHING
    place = iota(jnp.int32, (128, LIST_MAX), 1).astype(jnp.float32)
    listed = jnp.zeros((128, LIST_MAX), jnp.float32)
    for r in range(16):
        listed += jnp.where(rank[:, r : r + 1] == place, values[:, r : r + 1], 0.0)
    listed = jnp.sum(listed, axis=0, keepdims=True) + NOTHING
    at = iota(jnp.int32, (1, LIST_MAX), 1)
    repeat = lambda v: jnp.concatenate([v] * (LIST_MAX // 128), 1)
    listed = jnp.where(at == LIST_MAX - 2, repeat(filled), listed)
    listed = jnp.where(at == LIST_MAX - 1, repeat(total), listed)
    return listed.astype(jnp.int32), slots


def gather_kernel(
    nodes_hbm, weight_hbm, bias_in, bucket_ref, ko_ref, kl_ref, qo_ref, ql_ref,
    qg_ref, kn_ref, kf_ref, table_ref, list_ref, bias_ref, m_ref, l_ref, acc_ref,
    nodes_ref, weight_ref, slots_ref, slots_s, table_s, bias_s, scalar_sem,
    ring_send, ring_recv, pair_send, pair_recv, table_send, table_recv, load_sem, weight_sem,
):
    z, y, c = coordinates()
    heads = range(PLAN_HEADS)
    size = LOCAL // PIECES
    partners = [ring_at(axis, step) for axis in "zy" for step in (1, 2, 3)] + [sibling()]
    greet(partners)

    def local_copy(source, target, sem):
        copy = pltpu.make_async_copy(source, target, sem)
        copy.start()
        return copy

    node_rows = lambda p: pl.ds(p * size * CSIZE, size * CSIZE)
    load_nodes = lambda p: local_copy(nodes_hbm.at[node_rows(p)], nodes_ref.at[node_rows(p)], load_sem.at[p])
    node_loads = [load_nodes(0)]
    weight_load = local_copy(weight_hbm, weight_ref, weight_sem)
    node_loads += [load_nodes(p) for p in range(1, PIECES)]
    table_ref[c, z, y] = jnp.concatenate(
        [bucket_ref[...], jnp.zeros((1, 128 - bucket_ref.shape[1]), jnp.int32)], 1
    )
    for i in range(2 * PLAN_HEADS):
        bias_ref[i, :, : bias_in.shape[1]] = bias_in[i : i + 1] * LOG2E
    sent = []

    def part(p):
        return pl.ds(p * size, size)

    def side(h):
        return pl.ds(h * (LOCAL // 2), LOCAL // 2)

    streams = []
    for plan in range(2):
        q_axis, kv_axis = ("z", "y") if plan == 0 else ("y", "z")
        for kind, axis in (("kv", kv_axis), ("q", q_axis)):
            at = z if axis == "z" else y
            if kind == "q":
                slot = lambda p, r, plan=plan: qg_ref.at[plan, p, r]
            else:
                slot = lambda p, r, plan=plan: kf_ref.at[plan, c, r] if p == 3 else kn_ref.at[plan, p, c, r]
            streams.append((len(streams), plan, kind, axis, at, slot))

    def send(src, dst, send_sem, recv_sem, device):
        copy = pltpu.make_async_remote_copy(
            src_ref=src, dst_ref=dst, send_sem=send_sem, recv_sem=recv_sem,
            device_id=device, device_id_type=MESH,
        )
        copy.start()
        sent.append(copy)

    def arrived(ref, sem):
        pltpu.make_async_remote_copy(
            src_ref=ref, dst_ref=ref, send_sem=ring_send.at[0, 0], recv_sem=sem,
            device_id=sibling(), device_id_type=MESH,
        ).wait_recv()

    weight_load.wait()
    def project(cluster, carry):
        normed = norm_rows(nodes_ref[pl.ds(cluster * CSIZE, CSIZE), :].astype(jnp.float32)).astype(jnp.bfloat16)
        for i in range(3):
            projected = lax.dot_general(
                weight_ref[i], normed, (((1,), (1,)), ((), ())), preferred_element_type=jnp.float32
            )
            if i == 0:
                projected = projected * (LOG2E / math.sqrt(HEAD_SIZE))
            projected = projected.astype(jnp.bfloat16)
            for plan in range(2):
                block = projected[plan * PLAN_FEATURES : (plan + 1) * PLAN_FEATURES]
                if i == 0:
                    qg_ref[plan, 0, cluster] = block
                else:
                    kn_ref[plan, 0, c, cluster, (i - 1) * PLAN_FEATURES : i * PLAN_FEATURES, :] = block
        return carry

    ordered = [s for s in streams if s[2] == "kv"] + [s for s in streams if s[2] == "q"]
    for p in range(PIECES):
        node_loads[p].wait()
        lax.fori_loop(p * size, (p + 1) * size, project, 0)
        if p == 0:
            greeted(partners)
            for step in (1, 2, 3):
                send(table_ref.at[c, z, y], table_ref.at[c, z, y], table_send.at[step - 1], table_recv.at[step - 1], ring_at("y", step))
        for number, plan, kind, axis, at, slot in ordered:
            for way, first, seen in ((1, 0, 1), (-1, PIECES, 2)):
                send(
                    slot(0, part(p)), slot(seen, part(p)),
                    ring_send.at[number, first + p], ring_recv.at[number, first + p], ring_at(axis, way),
                )
        if p % (PIECES // 2) == PIECES // 2 - 1:
            h = p // (PIECES // 2)
            for number, plan, kind, axis, at, slot in ordered:
                if kind == "kv":
                    send(slot(0, side(h)), slot(0, side(h)), pair_send.at[plan, h], pair_recv.at[plan, h], sibling())
    listed, slots = make_list(qo_ref[...], ql_ref[...], ko_ref[...], kl_ref[...])
    list_ref[...] = listed
    slots_ref[...] = slots
    m_ref[...] = jnp.full(m_ref.shape, NEVER, jnp.float32)
    l_ref[...] = jnp.zeros(l_ref.shape, jnp.float32)
    acc_ref[...] = jnp.zeros(acc_ref.shape, jnp.float32)
    scalars = [local_copy(slots_ref, slots_s, scalar_sem.at[0]), local_copy(bias_ref, bias_s, scalar_sem.at[1])]

    for plan in range(2):
        bias = [bias_ref[plan * PLAN_HEADS + h, :, 0:1] for h in heads]

        def own_tiles(step, carry):
            group = [step * UNROLL + u for u in range(UNROLL)]
            pairs = [
                (
                    lambda h, i=i: qg_ref[plan, 0, i, rows(h), :],
                    lambda h, i=i: kn_ref[plan, 0, c, i, rows(h), :],
                    lambda h, i=i: kn_ref[plan, 0, c, i, rows(h, PLAN_FEATURES), :],
                )
                for i in group
            ]
            for i, (highest, mixed) in zip(group, attend(pairs)):
                for h in heads:
                    m_ref[plan, i, h : h + 1, :] = highest[h] + bias[h]
                    l_ref[plan, i, h : h + 1, :] = mixed[h][HEAD_SIZE : HEAD_SIZE + 1]
                    acc_ref[plan, i, rows(h), :] = mixed[h][:HEAD_SIZE]
            return carry

        lax.fori_loop(0, LOCAL // UNROLL, own_tiles, 0)
    for step in (1, 2, 3):
        arrived(table_ref.at[c, z, place(y, -step)], table_recv.at[step - 1])
    for step in (1, 2, 3):
        send(table_ref.at[c, z], table_ref.at[c, z], table_send.at[2 + step], table_recv.at[2 + step], ring_at("z", step))
    for h in range(2):
        for p in range(h * PIECES // 2, (h + 1) * PIECES // 2):
            for number, plan, kind, axis, at, slot in ordered:
                before, after = slot(1, part(p)), slot(2, part(p))
                arrived(before, ring_recv.at[number, p])
                arrived(after, ring_recv.at[number, PIECES + p])
                onward, way = (before, 1) if p % 2 == 0 else (after, -1)
                far = 2 * PIECES + p
                send(onward, slot(3, part(p)), ring_send.at[number, far], ring_recv.at[number, far], ring_at(axis, way))
        for number, plan, kind, axis, at, slot in ordered:
            if kind == "kv":
                for index, step in ((1, -1), (2, 1)):
                    block, sem = slot(index, side(h)), 2 * index + h
                    send(block, block, pair_send.at[plan, sem], pair_recv.at[plan, sem], sibling())
        if h == 0:
            for step in (1, 2, 3):
                arrived(table_ref.at[c, place(z, -step)], table_recv.at[2 + step])
            send(table_ref.at[c], table_ref.at[c], table_send.at[6], table_recv.at[6], sibling())
    arrived(table_ref.at[1 - c], table_recv.at[6])
    scalars.append(local_copy(table_ref, table_s, scalar_sem.at[2]))
    for plan in range(2):
        for index in range(3):
            for h in range(2):
                arrived(kn_ref.at[plan, index, 1 - c, side(h)], pair_recv.at[plan, 2 * index + h])
    for copy in scalars:
        copy.wait()
    def early(plan, start, end):

        def early_tiles(step, carry):
            group, pairs = [], []
            for u in range(UNROLL):
                i = step * UNROLL + u
                item = slots_s[0, plan * RING * LOCAL + i]
                valid = item >= 0
                item = jnp.maximum(item, 0)
                key = lax.bitwise_and(lax.shift_right_logical(item, 7), 127)
                tile = lax.bitwise_and(lax.shift_right_logical(item, 14), 1023)
                worker = lax.shift_right_logical(tile, 5)
                bucket = table_s[
                    lax.bitwise_and(worker, 1), lax.shift_right_logical(worker, 3),
                    lax.bitwise_and(lax.shift_right_logical(worker, 1), 3), 0, lax.bitwise_and(tile, 31),
                ]
                bucket = lax.bitwise_and(bucket, 31)
                place_of = (jnp.minimum(lax.shift_right_logical(key, 4), 2), lax.bitwise_and(lax.shift_right_logical(key, 3), 1), lax.bitwise_and(key, 7))
                group.append((i, valid, [bias_s[plan * PLAN_HEADS + h, 0, bucket] for h in heads]))
                pairs.append((
                    lambda h, i=i: qg_ref[plan, lax.div(i, LOCAL), lax.rem(i, LOCAL), rows(h), :],
                    lambda h, k=place_of: kn_ref[plan, k[0], k[1], k[2], rows(h), :],
                    lambda h, k=place_of: kn_ref[plan, k[0], k[1], k[2], rows(h, PLAN_FEATURES), :],
                ))
            for (i, valid, bias), (highest, mixed) in zip(group, attend(pairs)):
                for h in heads:
                    top = jnp.where(valid, highest[h] + bias[h], NEVER)
                    old_m, old_l, old_acc = m_ref[plan, i, h : h + 1, :], l_ref[plan, i, h : h + 1, :], acc_ref[plan, i, rows(h), :]
                    new_m = jnp.maximum(old_m, top)
                    keep = jnp.exp2(old_m - new_m)
                    fresh = jnp.where(valid, jnp.exp2(top - new_m), 0.0)
                    m_ref[plan, i, h : h + 1, :] = new_m
                    l_ref[plan, i, h : h + 1, :] = old_l * keep + mixed[h][HEAD_SIZE : HEAD_SIZE + 1] * fresh
                    acc_ref[plan, i, rows(h), :] = old_acc * keep + mixed[h][:HEAD_SIZE] * fresh
            return carry

        lax.fori_loop(start, end, early_tiles, 0)

    def pass_far(h):
        for number, plan, kind, axis, at, slot in ordered:
            for p in range(h * PIECES // 2, (h + 1) * PIECES // 2):
                arrived(slot(3, part(p)), ring_recv.at[number, 2 * PIECES + p])
            if kind == "kv":
                far = slot(3, side(h))
                send(far, far, pair_send.at[plan, 6 + h], pair_recv.at[plan, 6 + h], sibling())

    steps = 3 * LOCAL // UNROLL
    early(0, 0, steps - 1)
    pass_far(0)
    early(0, steps - 1, steps)
    early(1, 0, steps // 2 - 1)
    pass_far(1)
    early(1, steps // 2 - 1, steps)
    for plan in range(2):
        for h in range(2):
            arrived(kf_ref.at[plan, 1 - c, side(h)], pair_recv.at[plan, 6 + h])
    for copy in sent:
        copy.wait_send()


def gather(nodes, qkv_weight, bias, bucket, key_owner, key_local, query_owner, query_local):
    any_space, in_vmem = pl.BlockSpec(memory_space=pl.ANY), pl.BlockSpec(memory_space=pltpu.VMEM)
    dma, vmem = pltpu.SemaphoreType.DMA, pltpu.VMEM
    q_shape, kv_shape = (PLAN_FEATURES, CSIZE), (2 * PLAN_FEATURES, CSIZE)
    m_shape, acc_shape = (2, 3 * LOCAL, 8, CSIZE), (2, 3 * LOCAL, PLAN_FEATURES, CSIZE)
    return pl.pallas_call(
        gather_kernel,
        out_shape=[
            vmem((2, RING, LOCAL) + q_shape, jnp.bfloat16),
            vmem((2, 3, 2, LOCAL) + kv_shape, jnp.bfloat16),
            vmem((2, 2, LOCAL) + kv_shape, jnp.bfloat16),
            vmem((2, RING, RING, 1, 128), jnp.int32),
            vmem((1, LIST_MAX), jnp.int32),
            vmem((2 * PLAN_HEADS, 1, 128), jnp.float32),
            vmem(m_shape, jnp.float32),
            vmem(m_shape, jnp.float32),
            vmem(acc_shape, jnp.float32),
        ],
        in_specs=[any_space] * 2 + [in_vmem] * 6,
        out_specs=[in_vmem] * 9,
        scratch_shapes=[
            vmem(nodes.shape, jnp.bfloat16),
            vmem(qkv_weight.shape, jnp.bfloat16),
            vmem((1, 128), jnp.int32),
            pltpu.SMEM((1, 128), jnp.int32),
            pltpu.SMEM((2, RING, RING, 1, 128), jnp.int32),
            pltpu.SMEM((2 * PLAN_HEADS, 1, 128), jnp.float32),
            dma((3,)),
            dma((4, 3 * PIECES)), dma((4, 3 * PIECES)), dma((2, 8)), dma((2, 8)), dma((7,)), dma((7,)),
            dma((PIECES,)), dma(()),
        ],
        compiler_params=pltpu.CompilerParams(
            collective_id=0, has_side_effects=True, vmem_limit_bytes=42 * 2**20
        ),
        name="gather",
    )(nodes, qkv_weight, bias, bucket, key_owner, key_local, query_owner, query_local)


def tile_kernel(
    list_hbm, bias_hbm, table_hbm, m0_ref, l0_ref, acc0_ref, q_ref, kn_ref, kf_ref, part_ref, log_ref,
    list_ref, bias_ref, table_ref, m_ref, l_ref, acc_ref, table_sem,
):
    heads = range(PLAN_HEADS)
    queries = part_ref.shape[0]
    waits = []
    for i, (source, target) in enumerate(((list_hbm, list_ref), (table_hbm, table_ref), (bias_hbm, bias_ref))):
        waits.append(pltpu.make_async_copy(source, target, table_sem.at[i]))
        waits[-1].start()
    m_ref[...] = jnp.full(m_ref.shape, NEVER, jnp.float32)
    l_ref[...] = jnp.zeros(l_ref.shape, jnp.float32)
    acc_ref[...] = jnp.zeros(acc_ref.shape, jnp.float32)

    def batch(kv_ref, step, carry):
        items, pairs = [], []
        for u in range(UNROLL):
            item = list_ref[0, step * UNROLL + u]
            state = lax.bitwise_and(item, 127)
            key = lax.bitwise_and(lax.shift_right_logical(item, 7), 127)
            tile = lax.shift_right_logical(item, 14)
            query = jnp.minimum(state, queries - 1)
            plan = lax.shift_right_logical(query, 5)
            key = plan * (kv_ref.shape[0] // 2) + key
            worker = lax.shift_right_logical(tile, 5)
            bucket = table_ref[
                lax.bitwise_and(worker, 1), lax.shift_right_logical(worker, 3),
                lax.bitwise_and(lax.shift_right_logical(worker, 1), 3), 0, lax.bitwise_and(tile, 31),
            ]
            items.append((state, [bias_ref[plan * PLAN_HEADS + h, 0, bucket] for h in heads]))
            pairs.append((
                lambda h, i=query: q_ref[i, rows(h), :],
                lambda h, i=key: kv_ref[i, rows(h), :],
                lambda h, i=key: kv_ref[i, rows(h, PLAN_FEATURES), :],
            ))
        for (state, bias), (highest, mixed) in zip(items, attend(pairs)):
            tops = [top + b for top, b in zip(highest, bias)]
            old_m = [m_ref[state, h : h + 1, :] for h in heads]
            old_l = [l_ref[state, h : h + 1, :] for h in heads]
            old_acc = [acc_ref[state, rows(h), :] for h in heads]
            new_m = [jnp.maximum(a, b) for a, b in zip(old_m, tops)]
            keep = [jnp.exp2(a - b) for a, b in zip(old_m, new_m)]
            fresh = [jnp.exp2(a - b) for a, b in zip(tops, new_m)]
            for h in heads:
                m_ref[state, h : h + 1, :] = new_m[h]
                l_ref[state, h : h + 1, :] = old_l[h] * keep[h] + mixed[h][HEAD_SIZE : HEAD_SIZE + 1] * fresh[h]
                acc_ref[state, rows(h), :] = old_acc[h] * keep[h] + mixed[h][:HEAD_SIZE] * fresh[h]
        return carry

    for copy in waits:
        copy.wait()
    split = lax.div(list_ref[0, LIST_MAX - 2], UNROLL)
    lax.fori_loop(0, split, functools.partial(batch, kn_ref), 0)
    lax.fori_loop(
        split, lax.div(list_ref[0, LIST_MAX - 1] + UNROLL - 1, UNROLL), functools.partial(batch, kf_ref), 0
    )

    def finish(plan, group, near):
        base = plan * RING + group
        for local in range(LOCAL):
            state = base * LOCAL + local
            for h in heads:
                best, total = m_ref[state, h : h + 1, :], l_ref[state, h : h + 1, :]
                acc = acc_ref[state, rows(h), :]
                if near:
                    other = group * LOCAL + local
                    late, early = best, m0_ref[plan, other, h : h + 1, :]
                    best = jnp.maximum(late, early)
                    shares = jnp.exp2(late - best), jnp.exp2(early - best)
                    total = total * shares[0] + l0_ref[plan, other, h : h + 1, :] * shares[1]
                    acc = acc * shares[0] + acc0_ref[plan, other, rows(h), :] * shares[1]
                safe = jnp.where(total > 0, total, 1.0)
                part_ref[base * LOCAL + local % 2 * RING + local // 2, rows(h), :] = (acc * (1.0 / safe)).astype(jnp.bfloat16)
                row = local // 2 % 2 * PLAN_HEADS + h
                log_ref[base, local % 2, local // 4, row : row + 1, :] = best + jnp.log2(safe)

    for plan in range(2):

        def near_group(group, carry):
            finish(plan, group, True)
            return carry

        lax.fori_loop(0, 3, near_group, 0)
        finish(plan, 3, False)


def tiles(items, bias, table, m, l, acc, q_all, kv_near, kv_far):
    queries, keys = 2 * RING * LOCAL, 2 * 2 * LOCAL
    in_vmem = pl.BlockSpec(memory_space=pltpu.VMEM)
    part_shape = (queries, PLAN_FEATURES, CSIZE)
    log_shape = (2 * RING, 2, 2, 8, CSIZE)
    dma, vmem = pltpu.SemaphoreType.DMA, pltpu.VMEM
    return pl.pallas_call(
        tile_kernel,
        in_specs=[in_vmem] * 9,
        out_specs=[in_vmem] * 2,
        scratch_shapes=[
                pltpu.SMEM((1, LIST_MAX), jnp.int32),
                pltpu.SMEM((2 * PLAN_HEADS, 1, 128), jnp.float32),
                pltpu.SMEM((2, RING, RING, 1, 128), jnp.int32),
                vmem((queries + 1, 8, CSIZE), jnp.float32),
                vmem((queries + 1, 8, CSIZE), jnp.float32),
                vmem((queries + 1, PLAN_FEATURES, CSIZE), jnp.float32),
            dma((3,)),
        ],
        out_shape=[vmem(part_shape, jnp.bfloat16), vmem(log_shape, jnp.float32)],
        compiler_params=pltpu.CompilerParams(vmem_limit_bytes=16 * 2**20),
        name="tiles",
    )(
        items, bias, table, m, l, acc,
        q_all.reshape(queries, PLAN_FEATURES, CSIZE),
        kv_near.reshape(3 * keys, 2 * PLAN_FEATURES, CSIZE), kv_far.reshape(keys, 2 * PLAN_FEATURES, CSIZE),
    )


def tail_kernel(
    part_ref, log_ref, nodes_ref, wo_hbm, up_hbm, down_hbm, out_ref,
    wo_ref, up_ref, down_ref, rows_ref, part_in, log_in, far_part, far_log, both_part, both_log, merged, gathered, resid_ref, normed_ref, staged,
    weight_sem, back_send, back_recv, x_send, x_recv, out_send, out_recv, out_own,
):
    z, y, c = coordinates()
    me = lax.axis_index("owner")
    x = lax.axis_index("head")
    heads = range(PLAN_HEADS)
    features = 2 * PLAN_FEATURES

    def load(source, target, sem):
        copy = pltpu.make_async_copy(source, target, sem)
        copy.start()
        return copy

    def across(step):
        return (me, place(x, step))

    partners = [ring_at(axis, step) for axis in "zy" for step in (1, 3)] + [across(step) for step in (1, 2, 3)]
    greet(partners)
    ways = ((0, 1), (1, -1))
    ring = [(0, "z", z), (1, "y", y)]
    half = lambda h: pl.ds(h * (RING // 2), RING // 2)
    weights = [
        load(nodes_ref.at[pl.ds(x * 2 * CSIZE, 2 * CSIZE)], rows_ref, weight_sem.at[0]),
        load(wo_hbm, wo_ref, weight_sem.at[1]),
        load(up_hbm, up_ref, weight_sem.at[2]),
        load(down_hbm, down_ref, weight_sem.at[3]),
    ]
    greeted(partners)
    sent = []

    def send(src, dst, send_sem, recv_sem, device):
        copy = pltpu.make_async_remote_copy(
            src_ref=src, dst_ref=dst, send_sem=send_sem, recv_sem=recv_sem,
            device_id=device, device_id_type=MESH,
        )
        copy.start()
        sent.append(copy)

    def arrived(ref, sem):
        pltpu.make_async_remote_copy(
            src_ref=ref, dst_ref=ref, send_sem=x_send.at[0, 0], recv_sem=sem,
            device_id=across(1), device_id_type=MESH,
        ).wait_recv()

    def back(plan, way, turn, kind, src, dst, device):
        send(src, dst, back_send.at[plan, way, turn, kind], back_recv.at[plan, way, turn, kind], device)

    def send_out(turn):
        t, first, count = TURNS[turn]
        lanes = pl.ds(first, count)
        for plan, axis, at in ring:
            for way, step in ways:
                to, far = ring_at(axis, step), 3
                back(plan, way, turn, 0, part_ref.at[plan, far, t, half(way), :, lanes], far_part.at[plan, way, t, :, :, lanes], to)
                back(plan, way, turn, 1, log_ref.at[plan, far, t, way, :, lanes], far_log.at[plan, way, t, :, lanes], to)
        for plan, axis, at in ring:
            for way, step in ways:
                to, next_at = ring_at(axis, step), 2 - way
                back(
                    plan, way, turn, 2, part_ref.at[plan, next_at, t, half(1 - way), :, lanes],
                    part_in.at[plan, way, t, half(1 - way), :, lanes], to,
                )
                back(
                    plan, way, turn, 3, log_ref.at[plan, next_at, t, 1 - way, :, lanes],
                    log_in.at[plan, way, t, 1 - way, :, lanes], to,
                )

    def combine(turn):
        t, first, count = TURNS[turn]
        lanes = pl.ds(first, count)
        span = slice(first, first + count)
        for plan, axis, at in ring:
            for way, step in ways:
                arrived(far_part.at[plan, way, t, :, :, lanes], back_recv.at[plan, way, turn, 0])
                arrived(far_log.at[plan, way, t, :, lanes], back_recv.at[plan, way, turn, 1])
                one, two = log_ref[plan, 2 - way, t, way, :, span], far_log[plan, way, t, :, span]
                best = jnp.maximum(one, two)
                shares = [jnp.exp2(one - best), jnp.exp2(two - best)]
                total = shares[0] + shares[1]
                both_log[plan, way, t, :, span] = best + jnp.log2(total)
                scale = 1.0 / total
                shares = [share * scale for share in shares]
                for to in range(2):
                    for h in heads:
                        row = to * PLAN_HEADS + h
                        both_part[plan, way, t, to, rows(h), span] = (
                            part_ref[plan, 2 - way, t, way * 2 + to, rows(h), span].astype(jnp.float32) * shares[0][row : row + 1]
                            + far_part[plan, way, t, to, rows(h), span].astype(jnp.float32) * shares[1][row : row + 1]
                        ).astype(jnp.bfloat16)
                to = ring_at(axis, step)
                back(
                    plan, way, turn, 4, both_part.at[plan, way, t, :, :, lanes],
                    part_in.at[plan, way, t, half(way), :, lanes], to,
                )
                back(
                    plan, way, turn, 5, both_log.at[plan, way, t, :, lanes], log_in.at[plan, way, t, way, :, lanes], to
                )

    mine = pl.ds(pl.multiple_of(x * features, 64), features)

    def merge(turn):
        t, first, count = TURNS[turn]
        lanes = pl.ds(first, count)
        span = slice(first, first + count)
        for plan in range(2):
            for way in range(2):
                arrived(part_in.at[plan, way, t, half(1 - way), :, lanes], back_recv.at[plan, way, turn, 2])
                arrived(log_in.at[plan, way, t, 1 - way, :, lanes], back_recv.at[plan, way, turn, 3])
                arrived(part_in.at[plan, way, t, half(way), :, lanes], back_recv.at[plan, way, turn, 4])
                arrived(log_in.at[plan, way, t, way, :, lanes], back_recv.at[plan, way, turn, 5])
        for plan, axis, at in ring:
            for to in range(RING):
                h0 = to // 2
                logs = [log_ref[plan, 0, t, h0, :, span]] + [log_in[plan, way, t, h0, :, span] for way in range(2)]
                best = jnp.maximum(jnp.maximum(logs[0], logs[1]), logs[2])
                shares = [jnp.exp2(log - best) for log in logs]
                scale = 1.0 / (shares[0] + shares[1] + shares[2])
                shares = [share * scale for share in shares]
                for h in heads:
                    row = to % 2 * PLAN_HEADS + h
                    total = part_ref[plan, 0, t, to, rows(h), span].astype(jnp.float32) * shares[0][row : row + 1]
                    for way in range(2):
                        total += part_in[plan, way, t, to, rows(h), span].astype(jnp.float32) * shares[way + 1][row : row + 1]
                    merged[t, to, rows(h, plan * PLAN_FEATURES), span] = total.astype(jnp.bfloat16)
        for step in (2, 1, 3):
            send(
                merged.at[t, place(x, step), :, lanes], gathered.at[t, mine, lanes],
                x_send.at[turn, step - 1], x_recv.at[turn, step - 1], across(step),
            )
        gathered[t, mine, span] = merged[t, x, :, span]

    wide = up_ref.shape[1] // BLOCKS
    out_copies = []

    def begin(turn):
        t, first, count = TURNS[turn]
        lanes = pl.ds(first, count)
        part = slice(t * CSIZE + first, t * CSIZE + first + count)
        for step in (1, 2, 3):
            source = place(x, -step)
            arrived(gathered.at[t, pl.ds(pl.multiple_of(source * features, 64), features), lanes], x_recv.at[turn, step - 1])
        mixed = lax.dot_general(
            gathered[t, :, first : first + count], wo_ref[...], (((0,), (0,)), ((), ())), preferred_element_type=jnp.float32
        )
        resid = rows_ref[part, :].astype(jnp.float32) + mixed
        resid_ref[part, :] = resid
        normed_ref[part, :] = norm_rows(resid).astype(jnp.bfloat16)

    def feed(turn, start, end):
        t, first, count = TURNS[turn]
        part = slice(t * CSIZE + first, t * CSIZE + first + count)

        def block(step, carry):
            units = pl.ds(pl.multiple_of(step * wide, 128), wide)
            hidden = jax.nn.gelu(
                jnp.dot(normed_ref[part, :], up_ref[:, units], preferred_element_type=jnp.float32)
            ).astype(jnp.bfloat16)
            resid_ref[part, :] += jnp.dot(hidden, down_ref[units, :], preferred_element_type=jnp.float32)
            return carry

        lax.fori_loop(start, end, block, 0)

    def hand_out(turn):
        t, first, count = TURNS[turn]
        part = slice(t * CSIZE + first, t * CSIZE + first + count)
        staged[:, part] = resid_ref[part, :].astype(jnp.bfloat16).T
        target = out_ref.at[:, pl.ds(pl.multiple_of((x * 2 + t) * CSIZE + first, 128), count)]
        block = lambda j: staged.at[pl.ds(pl.multiple_of(j * features, 64), features), part]
        for step in (2, 1, 3):
            send(
                block(place(x, step)), target, out_send.at[turn, step - 1], out_recv.at[turn, step - 1], across(step)
            )
        out_copies.append(load(block(x), target, out_own.at[turn]))

    send_out(0)
    combine(0)
    send_out(1)
    send_out(2)
    merge(0)
    combine(1)
    combine(2)
    merge(1)
    for copy in weights:
        copy.wait()
    begin(0)
    feed(0, 0, BLOCKS // 2)
    merge(2)
    feed(0, BLOCKS // 2, BLOCKS)
    hand_out(0)
    for turn in (1, 2):
        begin(turn)
        feed(turn, 0, BLOCKS)
        hand_out(turn)
    for turn, (t, first, count) in enumerate(TURNS):
        for step in (1, 2, 3):
            source = place(x, -step)
            arrived(
                out_ref.at[:, pl.ds(pl.multiple_of((source * 2 + t) * CSIZE + first, 128), count)],
                out_recv.at[turn, step - 1],
            )
    for copy in out_copies:
        copy.wait()
    for copy in sent:
        copy.wait_send()


def tail(parts, logs, nodes, out_weight, up_weight, down_weight):
    any_space = pl.BlockSpec(memory_space=pl.ANY)
    dma, vmem = pltpu.SemaphoreType.DMA, pltpu.VMEM
    width = nodes.shape[1]
    features = 2 * PLAN_FEATURES
    return pl.pallas_call(
        tail_kernel,
        out_shape=jax.ShapeDtypeStruct((features, nodes.shape[0]), jnp.bfloat16),
        in_specs=[pl.BlockSpec(memory_space=pltpu.VMEM)] * 2 + [any_space] * 4,
        out_specs=any_space,
        scratch_shapes=[
            vmem(out_weight.shape, jnp.bfloat16),
            vmem(up_weight.shape, jnp.bfloat16),
            vmem(down_weight.shape, jnp.bfloat16),
            vmem((2 * CSIZE, width), jnp.bfloat16),
            vmem((2, 2, 2, RING, PLAN_FEATURES, CSIZE), jnp.bfloat16),
            vmem((2, 2, 2, 2, 8, CSIZE), jnp.float32),
            vmem((2, 2, 2, 2, PLAN_FEATURES, CSIZE), jnp.bfloat16),
            vmem((2, 2, 2, 8, CSIZE), jnp.float32),
            vmem((2, 2, 2, 2, PLAN_FEATURES, CSIZE), jnp.bfloat16),
            vmem((2, 2, 2, 8, CSIZE), jnp.float32),
            vmem((2, RING, features, CSIZE), jnp.bfloat16),
            vmem((2, width, CSIZE), jnp.bfloat16),
            vmem((2 * CSIZE, width), jnp.float32),
            vmem((2 * CSIZE, width), jnp.bfloat16),
            vmem((RING * features, 2 * CSIZE), jnp.bfloat16),
            dma((4,)), dma((2, 2, 3, 6)), dma((2, 2, 3, 6)),
            dma((3, 3)), dma((3, 3)), dma((3, 3)), dma((3, 3)), dma((3,)),
        ],
        compiler_params=pltpu.CompilerParams(
            collective_id=1, has_side_effects=True, vmem_limit_bytes=32 * 2**20
        ),
        name="tail",
    )(parts, logs, nodes, out_weight, up_weight, down_weight)


def per_device(
    nodes, qkv_weight, out_weight, hop_bias, up_weight, down_weight,
    key_owner, key_local, query_owner, query_local, hop_bucket,
):
    lists = [array.reshape(8, 128) for array in (key_owner, key_local, query_owner, query_local)]
    q_all, kv_near, kv_far, table, items, bias, m, l, acc = gather(
        *[pltpu.with_memory_space_constraint(a, pltpu.HBM) for a in (nodes, qkv_weight.swapaxes(1, 2))], hop_bias.T, hop_bucket.reshape(1, -1), *lists
    )
    parts, logs = tiles(items, bias, table, m, l, acc, q_all, kv_near, kv_far)
    return tail(
        parts.reshape(2, RING, 2, RING, PLAN_FEATURES, CSIZE), logs.reshape(2, RING, 2, 2, 8, CSIZE),
        *[pltpu.with_memory_space_constraint(a, pltpu.HBM) for a in (nodes, out_weight, up_weight, down_weight)],
    ).T


def solution(mesh):
    placed = (
        P("owner", None), P(None, None, "head"), P(), P(None, "head"), P(), P(),
        P(), P(), P(), P(), P("owner"),
    )
    return jax.shard_map(
        per_device, mesh=mesh, in_specs=placed, out_specs=P("owner", "head"), check_vma=False
    )
```

```python
import functools
import math

import jax
import jax.numpy as jnp
from jax import lax
from jax.experimental import pallas as pl
from jax.experimental.pallas import tpu as pltpu
from jax.sharding import PartitionSpec as P

CSIZE = 256
EPSILON = 1e-05
RING = 4
LOCAL = 8
PLAN_HEADS = 3
HEAD_SIZE = 32
PLAN_FEATURES = PLAN_HEADS * HEAD_SIZE
LIST_MAX = 640
UNROLL = 4
MESH = pl.DeviceIdType.MESH
LOG2E = math.log2(math.e)
NEVER = -1e30
NOTHING = 64
PIECES = 4
BLOCKS = 2
TURNS = ((0, 0, 256), (1, 0, 128), (1, 128, 128))


def norm_rows(values):
    center = values - jnp.mean(values, axis=-1, keepdims=True)
    spread = jnp.mean(center * center, axis=-1, keepdims=True)
    return center * lax.rsqrt(spread + EPSILON)


def coordinates():
    me = lax.axis_index("owner")
    return lax.div(me, 8), lax.rem(lax.div(me, 2), 4), lax.rem(me, 2)


def place(at, step):
    return lax.rem(at + step + RING, RING)


def ring_at(axis, step):
    z, y, c = coordinates()
    if axis == "z":
        z = place(z, step)
    else:
        y = place(y, step)
    return ((z * 4 + y) * 2 + c, lax.axis_index("head"))


def sibling():
    z, y, c = coordinates()
    return ((z * 4 + y) * 2 + 1 - c, lax.axis_index("head"))


def greet(partners):
    for partner in partners:
        pl.semaphore_signal(pltpu.get_barrier_semaphore(), inc=1, device_id=partner, device_id_type=MESH)


def greeted(partners):
    pl.semaphore_wait(pltpu.get_barrier_semaphore(), len(partners))


def rows(h, first=0):
    return slice(first + HEAD_SIZE * h, first + HEAD_SIZE * (h + 1))


def attend(pairs):
    heads = range(PLAN_HEADS)
    ones = jnp.ones((16, CSIZE), jnp.bfloat16)
    scored = [
        [
            lax.dot_general(key(h), query(h), (((0,), (0,)), ((), ())), preferred_element_type=jnp.float32)
            for h in heads
        ]
        for query, key, value in pairs
    ]
    done = []
    for (query, key, value), scores in zip(pairs, scored):
        highest = [jnp.max(s, axis=0, keepdims=True) for s in scores]
        weights = [jnp.exp2(s - top).astype(jnp.bfloat16) for s, top in zip(scores, highest)]
        mixed = [
            jnp.dot(jnp.concatenate([value(h), ones], 0), weights[h], preferred_element_type=jnp.float32)
            for h in heads
        ]
        done.append((highest, mixed))
    return done


def make_list(query_owner, query_local, key_owner, key_local):
    z, y, c = coordinates()
    div, rem = lax.div, lax.rem
    qz, qy, qc = div(query_owner, 8), rem(div(query_owner, 2), 4), rem(query_owner, 2)
    kz, ky, kc = div(key_owner, 8), rem(div(key_owner, 2), 4), rem(key_owner, 2)
    iota = lax.broadcasted_iota
    number = iota(jnp.int32, (8, 128), 0) * 128 + iota(jnp.int32, (8, 128), 1)

    def seen(d):
        d = rem(d + RING, RING)
        return jnp.where(d == 0, 0, jnp.where(d == RING - 1, 1, d + 1))

    def table(mine, q_seen, k_seen, plan):
        near = k_seen != RING - 1
        state = plan * RING * LOCAL + q_seen * LOCAL + query_local
        item = state + (jnp.where(near, k_seen * 2 * LOCAL, 0) + kc * LOCAL + key_local) * 128 + number * 16384
        early = mine & near & (q_seen != RING - 1)
        flag = lambda f: jnp.where(f, jnp.ones((8, 128), jnp.float32), 0.0)
        return [flag(mine & near), flag(mine & (k_seen == RING - 1)), jnp.where(early, state, -1).astype(jnp.float32), item.astype(jnp.float32)]

    tables = zip(
        table((qy == y) & (qc == c) & (kz == z), seen(qz - z), seen(ky - y), 0),
        table((qz == z) & (qc == c) & (ky == y), seen(qy - y), seen(kz - z), 1),
    )
    near, far, early, items = [jnp.concatenate(pair, 0) for pair in tables]
    early, values = early.T, items.T
    numbers = jnp.concatenate([number, number], 0).astype(jnp.float32).T
    lane = iota(jnp.int32, (128, 128), 1).astype(jnp.float32)
    first = jnp.full((128, 128), 4096.0, jnp.float32)
    for r in range(16):
        first = jnp.minimum(first, jnp.where(early[:, r : r + 1] == lane, numbers[:, r : r + 1], 4096.0))
    first = jnp.min(first, axis=0, keepdims=True)
    slots, chosen = jnp.zeros((128, 128), jnp.float32), jnp.zeros((128, 128), jnp.float32)
    for r in range(16):
        hit = jnp.where((early[:, r : r + 1] == lane) & (numbers[:, r : r + 1] == first), 1.0, 0.0)
        slots += hit * (values[:, r : r + 1] + 1.0)
        chosen += jnp.where(lane == r, jnp.max(hit, axis=1, keepdims=True), 0.0)
    slots = (jnp.sum(slots, axis=0, keepdims=True) - 1.0).astype(jnp.int32)
    near = near * (1.0 - chosen.T[:16])
    before = jnp.where(iota(jnp.int32, (128, 128), 0) < iota(jnp.int32, (128, 128), 1), 1.0, 0.0)

    def ranks(ones, start):
        inside = jnp.dot(ones, before, preferred_element_type=jnp.float32)
        wide = jnp.broadcast_to(jnp.sum(ones, axis=1, keepdims=True), (16, 128))
        ahead = [start]
        for r in range(16):
            ahead.append(ahead[-1] + wide[r : r + 1])
        return inside + jnp.concatenate(ahead[:16], 0), ahead[16]

    near_rank, count = ranks(near, jnp.zeros((1, 128), jnp.float32))
    filled = jnp.floor((count + (UNROLL - 1)) * (1.0 / UNROLL)) * UNROLL
    far_rank, total = ranks(far, filled)
    rank = jnp.where(near > 0, near_rank, jnp.where(far > 0, far_rank, -1.0)).T
    values = values - NOTHING
    place = iota(jnp.int32, (128, LIST_MAX), 1).astype(jnp.float32)
    listed = jnp.zeros((128, LIST_MAX), jnp.float32)
    for r in range(16):
        listed += jnp.where(rank[:, r : r + 1] == place, values[:, r : r + 1], 0.0)
    listed = jnp.sum(listed, axis=0, keepdims=True) + NOTHING
    at = iota(jnp.int32, (1, LIST_MAX), 1)
    repeat = lambda v: jnp.concatenate([v] * (LIST_MAX // 128), 1)
    listed = jnp.where(at == LIST_MAX - 2, repeat(filled), listed)
    listed = jnp.where(at == LIST_MAX - 1, repeat(total), listed)
    return listed.astype(jnp.int32), slots


def gather_kernel(
    nodes_hbm, weight_hbm, bias_in, bucket_ref, ko_ref, kl_ref, qo_ref, ql_ref,
    qg_ref, kn_ref, kf_ref, table_ref, list_ref, bias_ref, m_ref, l_ref, acc_ref,
    nodes_ref, weight_ref, slots_ref, slots_s, table_s, bias_s, scalar_sem,
    ring_send, ring_recv, pair_send, pair_recv, table_send, table_recv, load_sem, weight_sem,
):
    z, y, c = coordinates()
    heads = range(PLAN_HEADS)
    size = LOCAL // PIECES
    partners = [ring_at(axis, step) for axis in "zy" for step in (1, 2, 3)] + [sibling()]
    greet(partners)

    def local_copy(source, target, sem):
        copy = pltpu.make_async_copy(source, target, sem)
        copy.start()
        return copy

    node_rows = lambda p: pl.ds(p * size * CSIZE, size * CSIZE)
    load_nodes = lambda p: local_copy(nodes_hbm.at[node_rows(p)], nodes_ref.at[node_rows(p)], load_sem.at[p])
    node_loads = [load_nodes(0)]
    weight_load = local_copy(weight_hbm, weight_ref, weight_sem)
    node_loads += [load_nodes(p) for p in range(1, PIECES)]
    table_ref[c, z, y] = jnp.concatenate(
        [bucket_ref[...], jnp.zeros((1, 128 - bucket_ref.shape[1]), jnp.int32)], 1
    )
    for i in range(2 * PLAN_HEADS):
        bias_ref[i, :, : bias_in.shape[1]] = bias_in[i : i + 1] * LOG2E
    sent = []

    def part(p):
        return pl.ds(p * size, size)

    def side(h):
        return pl.ds(h * (LOCAL // 2), LOCAL // 2)

    streams = []
    for plan in range(2):
        q_axis, kv_axis = ("z", "y") if plan == 0 else ("y", "z")
        for kind, axis in (("kv", kv_axis), ("q", q_axis)):
            at = z if axis == "z" else y
            if kind == "q":
                slot = lambda p, r, plan=plan: qg_ref.at[plan, p, r]
            else:
                slot = lambda p, r, plan=plan: kf_ref.at[plan, c, r] if p == 3 else kn_ref.at[plan, p, c, r]
            streams.append((len(streams), plan, kind, axis, at, slot))

    def send(src, dst, send_sem, recv_sem, device):
        copy = pltpu.make_async_remote_copy(
            src_ref=src, dst_ref=dst, send_sem=send_sem, recv_sem=recv_sem,
            device_id=device, device_id_type=MESH,
        )
        copy.start()
        sent.append(copy)

    def arrived(ref, sem):
        pltpu.make_async_remote_copy(
            src_ref=ref, dst_ref=ref, send_sem=ring_send.at[0, 0], recv_sem=sem,
            device_id=sibling(), device_id_type=MESH,
        ).wait_recv()

    weight_load.wait()
    def project(cluster, carry):
        normed = norm_rows(nodes_ref[pl.ds(cluster * CSIZE, CSIZE), :].astype(jnp.float32)).astype(jnp.bfloat16)
        for i in range(3):
            projected = lax.dot_general(
                weight_ref[i], normed, (((1,), (1,)), ((), ())), preferred_element_type=jnp.float32
            )
            if i == 0:
                projected = projected * (LOG2E / math.sqrt(HEAD_SIZE))
            projected = projected.astype(jnp.bfloat16)
            for plan in range(2):
                block = projected[plan * PLAN_FEATURES : (plan + 1) * PLAN_FEATURES]
                if i == 0:
                    qg_ref[plan, 0, cluster] = block
                else:
                    kn_ref[plan, 0, c, cluster, (i - 1) * PLAN_FEATURES : i * PLAN_FEATURES, :] = block
        return carry

    ordered = [s for s in streams if s[2] == "kv"] + [s for s in streams if s[2] == "q"]
    for p in range(PIECES):
        node_loads[p].wait()
        lax.fori_loop(p * size, (p + 1) * size, project, 0)
        if p == 0:
            greeted(partners)
            for step in (1, 2, 3):
                send(table_ref.at[c, z, y], table_ref.at[c, z, y], table_send.at[step - 1], table_recv.at[step - 1], ring_at("y", step))
        for number, plan, kind, axis, at, slot in ordered:
            for way, first, seen in ((1, 0, 1), (-1, PIECES, 2)):
                send(
                    slot(0, part(p)), slot(seen, part(p)),
                    ring_send.at[number, first + p], ring_recv.at[number, first + p], ring_at(axis, way),
                )
        if p % (PIECES // 2) == PIECES // 2 - 1:
            h = p // (PIECES // 2)
            for number, plan, kind, axis, at, slot in ordered:
                if kind == "kv":
                    send(slot(0, side(h)), slot(0, side(h)), pair_send.at[plan, h], pair_recv.at[plan, h], sibling())
    listed, slots = make_list(qo_ref[...], ql_ref[...], ko_ref[...], kl_ref[...])
    list_ref[...] = listed
    slots_ref[...] = slots
    m_ref[...] = jnp.full(m_ref.shape, NEVER, jnp.float32)
    l_ref[...] = jnp.zeros(l_ref.shape, jnp.float32)
    acc_ref[...] = jnp.zeros(acc_ref.shape, jnp.float32)
    scalars = [local_copy(slots_ref, slots_s, scalar_sem.at[0]), local_copy(bias_ref, bias_s, scalar_sem.at[1])]

    for plan in range(2):
        bias = [bias_ref[plan * PLAN_HEADS + h, :, 0:1] for h in heads]

        def own_tiles(step, carry):
            group = [step * UNROLL + u for u in range(UNROLL)]
            pairs = [
                (
                    lambda h, i=i: qg_ref[plan, 0, i, rows(h), :],
                    lambda h, i=i: kn_ref[plan, 0, c, i, rows(h), :],
                    lambda h, i=i: kn_ref[plan, 0, c, i, rows(h, PLAN_FEATURES), :],
                )
                for i in group
            ]
            for i, (highest, mixed) in zip(group, attend(pairs)):
                for h in heads:
                    m_ref[plan * RING * LOCAL + i, h : h + 1, :] = highest[h] + bias[h]
                    l_ref[plan * RING * LOCAL + i, h : h + 1, :] = mixed[h][HEAD_SIZE : HEAD_SIZE + 1]
                    acc_ref[plan * RING * LOCAL + i, rows(h), :] = mixed[h][:HEAD_SIZE]
            return carry

        lax.fori_loop(0, LOCAL // UNROLL, own_tiles, 0)
    for step in (1, 2, 3):
        arrived(table_ref.at[c, z, place(y, -step)], table_recv.at[step - 1])
    for step in (1, 2, 3):
        send(table_ref.at[c, z], table_ref.at[c, z], table_send.at[2 + step], table_recv.at[2 + step], ring_at("z", step))
    for h in range(2):
        for p in range(h * PIECES // 2, (h + 1) * PIECES // 2):
            for number, plan, kind, axis, at, slot in ordered:
                before, after = slot(1, part(p)), slot(2, part(p))
                arrived(before, ring_recv.at[number, p])
                arrived(after, ring_recv.at[number, PIECES + p])
                onward, way = (before, 1) if p % 2 == 0 else (after, -1)
                far = 2 * PIECES + p
                send(onward, slot(3, part(p)), ring_send.at[number, far], ring_recv.at[number, far], ring_at(axis, way))
        for number, plan, kind, axis, at, slot in ordered:
            if kind == "kv":
                for index, step in ((1, -1), (2, 1)):
                    block, sem = slot(index, side(h)), 2 * index + h
                    send(block, block, pair_send.at[plan, sem], pair_recv.at[plan, sem], sibling())
        if h == 0:
            for step in (1, 2, 3):
                arrived(table_ref.at[c, place(z, -step)], table_recv.at[2 + step])
            send(table_ref.at[c], table_ref.at[c], table_send.at[6], table_recv.at[6], sibling())
    arrived(table_ref.at[1 - c], table_recv.at[6])
    scalars.append(local_copy(table_ref, table_s, scalar_sem.at[2]))
    for plan in range(2):
        for index in range(3):
            for h in range(2):
                arrived(kn_ref.at[plan, index, 1 - c, side(h)], pair_recv.at[plan, 2 * index + h])
    for copy in scalars:
        copy.wait()
    def early(plan, start, end):

        def early_tiles(step, carry):
            group, pairs = [], []
            for u in range(UNROLL):
                i = step * UNROLL + u
                item = slots_s[0, plan * RING * LOCAL + i]
                valid = item >= 0
                item = jnp.maximum(item, 0)
                key = lax.bitwise_and(lax.shift_right_logical(item, 7), 127)
                tile = lax.bitwise_and(lax.shift_right_logical(item, 14), 1023)
                worker = lax.shift_right_logical(tile, 5)
                bucket = table_s[
                    lax.bitwise_and(worker, 1), lax.shift_right_logical(worker, 3),
                    lax.bitwise_and(lax.shift_right_logical(worker, 1), 3), 0, lax.bitwise_and(tile, 31),
                ]
                bucket = lax.bitwise_and(bucket, 31)
                place_of = (jnp.minimum(lax.shift_right_logical(key, 4), 2), lax.bitwise_and(lax.shift_right_logical(key, 3), 1), lax.bitwise_and(key, 7))
                group.append((i, valid, [bias_s[plan * PLAN_HEADS + h, 0, bucket] for h in heads]))
                pairs.append((
                    lambda h, i=i: qg_ref[plan, lax.div(i, LOCAL), lax.rem(i, LOCAL), rows(h), :],
                    lambda h, k=place_of: kn_ref[plan, k[0], k[1], k[2], rows(h), :],
                    lambda h, k=place_of: kn_ref[plan, k[0], k[1], k[2], rows(h, PLAN_FEATURES), :],
                ))
            for (i, valid, bias), (highest, mixed) in zip(group, attend(pairs)):
                for h in heads:
                    top = jnp.where(valid, highest[h] + bias[h], NEVER)
                    old_m, old_l, old_acc = m_ref[plan * RING * LOCAL + i, h : h + 1, :], l_ref[plan * RING * LOCAL + i, h : h + 1, :], acc_ref[plan * RING * LOCAL + i, rows(h), :]
                    new_m = jnp.maximum(old_m, top)
                    keep = jnp.exp2(old_m - new_m)
                    fresh = jnp.where(valid, jnp.exp2(top - new_m), 0.0)
                    m_ref[plan * RING * LOCAL + i, h : h + 1, :] = new_m
                    l_ref[plan * RING * LOCAL + i, h : h + 1, :] = old_l * keep + mixed[h][HEAD_SIZE : HEAD_SIZE + 1] * fresh
                    acc_ref[plan * RING * LOCAL + i, rows(h), :] = old_acc * keep + mixed[h][:HEAD_SIZE] * fresh
            return carry

        lax.fori_loop(start, end, early_tiles, 0)

    def pass_far(h):
        for number, plan, kind, axis, at, slot in ordered:
            for p in range(h * PIECES // 2, (h + 1) * PIECES // 2):
                arrived(slot(3, part(p)), ring_recv.at[number, 2 * PIECES + p])
            if kind == "kv":
                far = slot(3, side(h))
                send(far, far, pair_send.at[plan, 6 + h], pair_recv.at[plan, 6 + h], sibling())

    steps = 3 * LOCAL // UNROLL
    early(0, 0, steps - 1)
    pass_far(0)
    early(0, steps - 1, steps)
    early(1, 0, steps // 2 - 1)
    pass_far(1)
    early(1, steps // 2 - 1, steps)
    for plan in range(2):
        for h in range(2):
            arrived(kf_ref.at[plan, 1 - c, side(h)], pair_recv.at[plan, 6 + h])
    for copy in sent:
        copy.wait_send()


def gather(nodes, qkv_weight, bias, bucket, key_owner, key_local, query_owner, query_local):
    any_space, in_vmem = pl.BlockSpec(memory_space=pl.ANY), pl.BlockSpec(memory_space=pltpu.VMEM)
    dma, vmem = pltpu.SemaphoreType.DMA, pltpu.VMEM
    q_shape, kv_shape = (PLAN_FEATURES, CSIZE), (2 * PLAN_FEATURES, CSIZE)
    states = 2 * RING * LOCAL + 1
    m_shape, acc_shape = (states, 8, CSIZE), (states, PLAN_FEATURES, CSIZE)
    return pl.pallas_call(
        gather_kernel,
        out_shape=[
            vmem((2, RING, LOCAL) + q_shape, jnp.bfloat16),
            vmem((2, 3, 2, LOCAL) + kv_shape, jnp.bfloat16),
            vmem((2, 2, LOCAL) + kv_shape, jnp.bfloat16),
            vmem((2, RING, RING, 1, 128), jnp.int32),
            vmem((1, LIST_MAX), jnp.int32),
            vmem((2 * PLAN_HEADS, 1, 128), jnp.float32),
            vmem(m_shape, jnp.float32),
            vmem(m_shape, jnp.float32),
            vmem(acc_shape, jnp.float32),
        ],
        in_specs=[any_space] * 2 + [in_vmem] * 6,
        out_specs=[in_vmem] * 9,
        scratch_shapes=[
            vmem(nodes.shape, jnp.bfloat16),
            vmem(qkv_weight.shape, jnp.bfloat16),
            vmem((1, 128), jnp.int32),
            pltpu.SMEM((1, 128), jnp.int32),
            pltpu.SMEM((2, RING, RING, 1, 128), jnp.int32),
            pltpu.SMEM((2 * PLAN_HEADS, 1, 128), jnp.float32),
            dma((3,)),
            dma((4, 3 * PIECES)), dma((4, 3 * PIECES)), dma((2, 8)), dma((2, 8)), dma((7,)), dma((7,)),
            dma((PIECES,)), dma(()),
        ],
        compiler_params=pltpu.CompilerParams(
            collective_id=0, has_side_effects=True, vmem_limit_bytes=36 * 2**20
        ),
        name="gather",
    )(nodes, qkv_weight, bias, bucket, key_owner, key_local, query_owner, query_local)


def tile_kernel(
    list_hbm, bias_hbm, table_hbm, m_in, l_in, acc_in, q_ref, kn_ref, kf_ref,
    part_ref, log_ref, m_ref, l_ref, acc_ref, list_ref, bias_ref, table_ref, table_sem,
):
    heads = range(PLAN_HEADS)
    queries = part_ref.shape[0]
    waits = []
    for i, (source, target) in enumerate(((list_hbm, list_ref), (table_hbm, table_ref), (bias_hbm, bias_ref))):
        waits.append(pltpu.make_async_copy(source, target, table_sem.at[i]))
        waits[-1].start()

    def batch(kv_ref, step, carry):
        items, pairs = [], []
        for u in range(UNROLL):
            item = list_ref[0, step * UNROLL + u]
            state = lax.bitwise_and(item, 127)
            key = lax.bitwise_and(lax.shift_right_logical(item, 7), 127)
            tile = lax.shift_right_logical(item, 14)
            query = jnp.minimum(state, queries - 1)
            plan = lax.shift_right_logical(query, 5)
            key = plan * (kv_ref.shape[0] // 2) + key
            worker = lax.shift_right_logical(tile, 5)
            bucket = table_ref[
                lax.bitwise_and(worker, 1), lax.shift_right_logical(worker, 3),
                lax.bitwise_and(lax.shift_right_logical(worker, 1), 3), 0, lax.bitwise_and(tile, 31),
            ]
            items.append((state, [bias_ref[plan * PLAN_HEADS + h, 0, bucket] for h in heads]))
            pairs.append((
                lambda h, i=query: q_ref[i, rows(h), :],
                lambda h, i=key: kv_ref[i, rows(h), :],
                lambda h, i=key: kv_ref[i, rows(h, PLAN_FEATURES), :],
            ))
        for (state, bias), (highest, mixed) in zip(items, attend(pairs)):
            tops = [top + b for top, b in zip(highest, bias)]
            old_m = [m_ref[state, h : h + 1, :] for h in heads]
            old_l = [l_ref[state, h : h + 1, :] for h in heads]
            old_acc = [acc_ref[state, rows(h), :] for h in heads]
            new_m = [jnp.maximum(a, b) for a, b in zip(old_m, tops)]
            keep = [jnp.exp2(a - b) for a, b in zip(old_m, new_m)]
            fresh = [jnp.exp2(a - b) for a, b in zip(tops, new_m)]
            for h in heads:
                m_ref[state, h : h + 1, :] = new_m[h]
                l_ref[state, h : h + 1, :] = old_l[h] * keep[h] + mixed[h][HEAD_SIZE : HEAD_SIZE + 1] * fresh[h]
                acc_ref[state, rows(h), :] = old_acc[h] * keep[h] + mixed[h][:HEAD_SIZE] * fresh[h]
        return carry

    for copy in waits:
        copy.wait()
    split = lax.div(list_ref[0, LIST_MAX - 2], UNROLL)
    lax.fori_loop(0, split, functools.partial(batch, kn_ref), 0)
    lax.fori_loop(
        split, lax.div(list_ref[0, LIST_MAX - 1] + UNROLL - 1, UNROLL), functools.partial(batch, kf_ref), 0
    )

    def finish(group, carry):
        for local in range(LOCAL):
            state = group * LOCAL + local
            for h in heads:
                total = l_ref[state, h : h + 1, :]
                safe = jnp.where(total > 0, total, 1.0)
                part_ref[group * LOCAL + local % 2 * RING + local // 2, rows(h), :] = (
                    acc_ref[state, rows(h), :] * (1.0 / safe)
                ).astype(jnp.bfloat16)
                row = local // 2 % 2 * PLAN_HEADS + h
                log_ref[group, local % 2, local // 4, row : row + 1, :] = m_ref[state, h : h + 1, :] + jnp.log2(safe)
        return carry

    lax.fori_loop(0, queries // LOCAL, finish, 0)


def tiles(items, bias, table, m, l, acc, q_all, kv_near, kv_far):
    queries, keys = 2 * RING * LOCAL, 2 * 2 * LOCAL
    in_vmem = pl.BlockSpec(memory_space=pltpu.VMEM)
    part_shape = (queries, PLAN_FEATURES, CSIZE)
    log_shape = (2 * RING, 2, 2, 8, CSIZE)
    dma, vmem = pltpu.SemaphoreType.DMA, pltpu.VMEM
    return pl.pallas_call(
        tile_kernel,
        in_specs=[in_vmem] * 9,
        out_specs=[in_vmem] * 5,
        input_output_aliases={3: 2, 4: 3, 5: 4},
        scratch_shapes=[
            pltpu.SMEM((1, LIST_MAX), jnp.int32),
            pltpu.SMEM((2 * PLAN_HEADS, 1, 128), jnp.float32),
            pltpu.SMEM((2, RING, RING, 1, 128), jnp.int32),
            dma((3,)),
        ],
        out_shape=[vmem(part_shape, jnp.bfloat16), vmem(log_shape, jnp.float32)]
        + [vmem(state.shape, jnp.float32) for state in (m, l, acc)],
        compiler_params=pltpu.CompilerParams(vmem_limit_bytes=8 * 2**20),
        name="tiles",
    )(
        items, bias, table, m, l, acc,
        q_all.reshape(queries, PLAN_FEATURES, CSIZE),
        kv_near.reshape(3 * keys, 2 * PLAN_FEATURES, CSIZE), kv_far.reshape(keys, 2 * PLAN_FEATURES, CSIZE),
    )


def tail_kernel(
    part_ref, log_ref, nodes_ref, wo_hbm, up_hbm, down_hbm, out_ref,
    wo_ref, up_ref, down_ref, rows_ref, part_in, log_in, far_part, far_log, both_part, both_log, merged, gathered, resid_ref, normed_ref, staged,
    weight_sem, back_send, back_recv, x_send, x_recv, out_send, out_recv, out_own,
):
    z, y, c = coordinates()
    me = lax.axis_index("owner")
    x = lax.axis_index("head")
    heads = range(PLAN_HEADS)
    features = 2 * PLAN_FEATURES

    def load(source, target, sem):
        copy = pltpu.make_async_copy(source, target, sem)
        copy.start()
        return copy

    def across(step):
        return (me, place(x, step))

    partners = [ring_at(axis, step) for axis in "zy" for step in (1, 3)] + [across(step) for step in (1, 2, 3)]
    greet(partners)
    ways = ((0, 1), (1, -1))
    ring = [(0, "z", z), (1, "y", y)]
    half = lambda h: pl.ds(h * (RING // 2), RING // 2)
    weights = [
        load(nodes_ref.at[pl.ds(x * 2 * CSIZE, 2 * CSIZE)], rows_ref, weight_sem.at[0]),
        load(wo_hbm, wo_ref, weight_sem.at[1]),
        load(up_hbm, up_ref, weight_sem.at[2]),
        load(down_hbm, down_ref, weight_sem.at[3]),
    ]
    greeted(partners)
    sent = []

    def send(src, dst, send_sem, recv_sem, device):
        copy = pltpu.make_async_remote_copy(
            src_ref=src, dst_ref=dst, send_sem=send_sem, recv_sem=recv_sem,
            device_id=device, device_id_type=MESH,
        )
        copy.start()
        sent.append(copy)

    def arrived(ref, sem):
        pltpu.make_async_remote_copy(
            src_ref=ref, dst_ref=ref, send_sem=x_send.at[0, 0], recv_sem=sem,
            device_id=across(1), device_id_type=MESH,
        ).wait_recv()

    def back(plan, way, turn, kind, src, dst, device):
        send(src, dst, back_send.at[plan, way, turn, kind], back_recv.at[plan, way, turn, kind], device)

    def send_out(turn):
        t, first, count = TURNS[turn]
        lanes = pl.ds(first, count)
        for plan, axis, at in ring:
            for way, step in ways:
                to, far = ring_at(axis, step), 3
                back(plan, way, turn, 0, part_ref.at[plan, far, t, half(way), :, lanes], far_part.at[plan, way, t, :, :, lanes], to)
                back(plan, way, turn, 1, log_ref.at[plan, far, t, way, :, lanes], far_log.at[plan, way, t, :, lanes], to)
        for plan, axis, at in ring:
            for way, step in ways:
                to, next_at = ring_at(axis, step), 2 - way
                back(
                    plan, way, turn, 2, part_ref.at[plan, next_at, t, half(1 - way), :, lanes],
                    part_in.at[plan, way, t, half(1 - way), :, lanes], to,
                )
                back(
                    plan, way, turn, 3, log_ref.at[plan, next_at, t, 1 - way, :, lanes],
                    log_in.at[plan, way, t, 1 - way, :, lanes], to,
                )

    def combine(turn):
        t, first, count = TURNS[turn]
        lanes = pl.ds(first, count)
        span = slice(first, first + count)
        for plan, axis, at in ring:
            for way, step in ways:
                arrived(far_part.at[plan, way, t, :, :, lanes], back_recv.at[plan, way, turn, 0])
                arrived(far_log.at[plan, way, t, :, lanes], back_recv.at[plan, way, turn, 1])
                one, two = log_ref[plan, 2 - way, t, way, :, span], far_log[plan, way, t, :, span]
                best = jnp.maximum(one, two)
                shares = [jnp.exp2(one - best), jnp.exp2(two - best)]
                total = shares[0] + shares[1]
                both_log[plan, way, t, :, span] = best + jnp.log2(total)
                scale = 1.0 / total
                shares = [share * scale for share in shares]
                for to in range(2):
                    for h in heads:
                        row = to * PLAN_HEADS + h
                        both_part[plan, way, t, to, rows(h), span] = (
                            part_ref[plan, 2 - way, t, way * 2 + to, rows(h), span].astype(jnp.float32) * shares[0][row : row + 1]
                            + far_part[plan, way, t, to, rows(h), span].astype(jnp.float32) * shares[1][row : row + 1]
                        ).astype(jnp.bfloat16)
                to = ring_at(axis, step)
                back(
                    plan, way, turn, 4, both_part.at[plan, way, t, :, :, lanes],
                    part_in.at[plan, way, t, half(way), :, lanes], to,
                )
                back(
                    plan, way, turn, 5, both_log.at[plan, way, t, :, lanes], log_in.at[plan, way, t, way, :, lanes], to
                )

    mine = pl.ds(pl.multiple_of(x * features, 64), features)

    def merge(turn):
        t, first, count = TURNS[turn]
        lanes = pl.ds(first, count)
        span = slice(first, first + count)
        for plan in range(2):
            for way in range(2):
                arrived(part_in.at[plan, way, t, half(1 - way), :, lanes], back_recv.at[plan, way, turn, 2])
                arrived(log_in.at[plan, way, t, 1 - way, :, lanes], back_recv.at[plan, way, turn, 3])
                arrived(part_in.at[plan, way, t, half(way), :, lanes], back_recv.at[plan, way, turn, 4])
                arrived(log_in.at[plan, way, t, way, :, lanes], back_recv.at[plan, way, turn, 5])
        for plan, axis, at in ring:
            for to in range(RING):
                h0 = to // 2
                logs = [log_ref[plan, 0, t, h0, :, span]] + [log_in[plan, way, t, h0, :, span] for way in range(2)]
                best = jnp.maximum(jnp.maximum(logs[0], logs[1]), logs[2])
                shares = [jnp.exp2(log - best) for log in logs]
                scale = 1.0 / (shares[0] + shares[1] + shares[2])
                shares = [share * scale for share in shares]
                for h in heads:
                    row = to % 2 * PLAN_HEADS + h
                    total = part_ref[plan, 0, t, to, rows(h), span].astype(jnp.float32) * shares[0][row : row + 1]
                    for way in range(2):
                        total += part_in[plan, way, t, to, rows(h), span].astype(jnp.float32) * shares[way + 1][row : row + 1]
                    merged[t, to, rows(h, plan * PLAN_FEATURES), span] = total.astype(jnp.bfloat16)
        for step in (2, 1, 3):
            send(
                merged.at[t, place(x, step), :, lanes], gathered.at[t, mine, lanes],
                x_send.at[turn, step - 1], x_recv.at[turn, step - 1], across(step),
            )
        gathered[t, mine, span] = merged[t, x, :, span]

    wide = up_ref.shape[1] // BLOCKS
    out_copies = []

    def begin(turn):
        t, first, count = TURNS[turn]
        lanes = pl.ds(first, count)
        part = slice(t * CSIZE + first, t * CSIZE + first + count)
        for step in (1, 2, 3):
            source = place(x, -step)
            arrived(gathered.at[t, pl.ds(pl.multiple_of(source * features, 64), features), lanes], x_recv.at[turn, step - 1])
        mixed = lax.dot_general(
            gathered[t, :, first : first + count], wo_ref[...], (((0,), (0,)), ((), ())), preferred_element_type=jnp.float32
        )
        resid = rows_ref[part, :].astype(jnp.float32) + mixed
        resid_ref[part, :] = resid
        normed_ref[part, :] = norm_rows(resid).astype(jnp.bfloat16)

    def feed(turn, start, end):
        t, first, count = TURNS[turn]
        part = slice(t * CSIZE + first, t * CSIZE + first + count)

        def block(step, carry):
            units = pl.ds(pl.multiple_of(step * wide, 128), wide)
            hidden = jax.nn.gelu(
                jnp.dot(normed_ref[part, :], up_ref[:, units], preferred_element_type=jnp.float32)
            ).astype(jnp.bfloat16)
            resid_ref[part, :] += jnp.dot(hidden, down_ref[units, :], preferred_element_type=jnp.float32)
            return carry

        lax.fori_loop(start, end, block, 0)

    def hand_out(turn):
        t, first, count = TURNS[turn]
        part = slice(t * CSIZE + first, t * CSIZE + first + count)
        staged[:, part] = resid_ref[part, :].astype(jnp.bfloat16).T
        target = out_ref.at[:, pl.ds(pl.multiple_of((x * 2 + t) * CSIZE + first, 128), count)]
        block = lambda j: staged.at[pl.ds(pl.multiple_of(j * features, 64), features), part]
        for step in (2, 1, 3):
            send(
                block(place(x, step)), target, out_send.at[turn, step - 1], out_recv.at[turn, step - 1], across(step)
            )
        out_copies.append(load(block(x), target, out_own.at[turn]))

    send_out(0)
    combine(0)
    send_out(1)
    send_out(2)
    merge(0)
    combine(1)
    combine(2)
    merge(1)
    for copy in weights:
        copy.wait()
    begin(0)
    feed(0, 0, BLOCKS // 2)
    merge(2)
    feed(0, BLOCKS // 2, BLOCKS)
    hand_out(0)
    for turn in (1, 2):
        begin(turn)
        feed(turn, 0, BLOCKS)
        hand_out(turn)
    for turn, (t, first, count) in enumerate(TURNS):
        for step in (1, 2, 3):
            source = place(x, -step)
            arrived(
                out_ref.at[:, pl.ds(pl.multiple_of((source * 2 + t) * CSIZE + first, 128), count)],
                out_recv.at[turn, step - 1],
            )
    for copy in out_copies:
        copy.wait()
    for copy in sent:
        copy.wait_send()


def tail(parts, logs, nodes, out_weight, up_weight, down_weight):
    any_space = pl.BlockSpec(memory_space=pl.ANY)
    dma, vmem = pltpu.SemaphoreType.DMA, pltpu.VMEM
    width = nodes.shape[1]
    features = 2 * PLAN_FEATURES
    return pl.pallas_call(
        tail_kernel,
        out_shape=jax.ShapeDtypeStruct((features, nodes.shape[0]), jnp.bfloat16),
        in_specs=[pl.BlockSpec(memory_space=pltpu.VMEM)] * 2 + [any_space] * 4,
        out_specs=any_space,
        scratch_shapes=[
            vmem(out_weight.shape, jnp.bfloat16),
            vmem(up_weight.shape, jnp.bfloat16),
            vmem(down_weight.shape, jnp.bfloat16),
            vmem((2 * CSIZE, width), jnp.bfloat16),
            vmem((2, 2, 2, RING, PLAN_FEATURES, CSIZE), jnp.bfloat16),
            vmem((2, 2, 2, 2, 8, CSIZE), jnp.float32),
            vmem((2, 2, 2, 2, PLAN_FEATURES, CSIZE), jnp.bfloat16),
            vmem((2, 2, 2, 8, CSIZE), jnp.float32),
            vmem((2, 2, 2, 2, PLAN_FEATURES, CSIZE), jnp.bfloat16),
            vmem((2, 2, 2, 8, CSIZE), jnp.float32),
            vmem((2, RING, features, CSIZE), jnp.bfloat16),
            vmem((2, width, CSIZE), jnp.bfloat16),
            vmem((2 * CSIZE, width), jnp.float32),
            vmem((2 * CSIZE, width), jnp.bfloat16),
            vmem((RING * features, 2 * CSIZE), jnp.bfloat16),
            dma((4,)), dma((2, 2, 3, 6)), dma((2, 2, 3, 6)),
            dma((3, 3)), dma((3, 3)), dma((3, 3)), dma((3, 3)), dma((3,)),
        ],
        compiler_params=pltpu.CompilerParams(
            collective_id=1, has_side_effects=True, vmem_limit_bytes=36 * 2**20
        ),
        name="tail",
    )(parts, logs, nodes, out_weight, up_weight, down_weight)


def per_device(
    nodes, qkv_weight, out_weight, hop_bias, up_weight, down_weight,
    key_owner, key_local, query_owner, query_local, hop_bucket,
):
    lists = [array.reshape(8, 128) for array in (key_owner, key_local, query_owner, query_local)]
    q_all, kv_near, kv_far, table, items, bias, m, l, acc = gather(
        *[pltpu.with_memory_space_constraint(a, pltpu.HBM) for a in (nodes, qkv_weight.swapaxes(1, 2))], hop_bias.T, hop_bucket.reshape(1, -1), *lists
    )
    parts, logs, *_ = tiles(items, bias, table, m, l, acc, q_all, kv_near, kv_far)
    return tail(
        parts.reshape(2, RING, 2, RING, PLAN_FEATURES, CSIZE), logs.reshape(2, RING, 2, 2, 8, CSIZE),
        *[pltpu.with_memory_space_constraint(a, pltpu.HBM) for a in (nodes, out_weight, up_weight, down_weight)],
    ).T


def solution(mesh):
    placed = (
        P("owner", None), P(None, None, "head"), P(), P(None, "head"), P(), P(),
        P(), P(), P(), P(), P("owner"),
    )
    return jax.shard_map(
        per_device, mesh=mesh, in_specs=placed, out_specs=P("owner", "head"), check_vma=False
    )
```

```python
import functools
import math

import jax
import jax.numpy as jnp
from jax import lax
from jax.experimental import pallas as pl
from jax.experimental.pallas import tpu as pltpu
from jax.sharding import PartitionSpec as P

CSIZE = 256
EPSILON = 1e-05
RING = 4
LOCAL = 8
PLAN_HEADS = 3
HEAD_SIZE = 32
PLAN_FEATURES = PLAN_HEADS * HEAD_SIZE
LIST_MAX = 640
UNROLL = 4
MESH = pl.DeviceIdType.MESH
LOG2E = math.log2(math.e)
NEVER = -1e30
NOTHING = 64
PIECES = 4
BLOCKS = 2
TURNS = ((0, 0, 256), (1, 0, 128), (1, 128, 128))


def norm_rows(values):
    center = values - jnp.mean(values, axis=-1, keepdims=True)
    spread = jnp.mean(center * center, axis=-1, keepdims=True)
    return center * lax.rsqrt(spread + EPSILON)


def coordinates():
    me = lax.axis_index("owner")
    return lax.div(me, 8), lax.rem(lax.div(me, 2), 4), lax.rem(me, 2)


def place(at, step):
    return lax.rem(at + step + RING, RING)


def ring_at(axis, step):
    z, y, c = coordinates()
    if axis == "z":
        z = place(z, step)
    else:
        y = place(y, step)
    return ((z * 4 + y) * 2 + c, lax.axis_index("head"))


def sibling():
    z, y, c = coordinates()
    return ((z * 4 + y) * 2 + 1 - c, lax.axis_index("head"))


def greet(partners):
    for partner in partners:
        pl.semaphore_signal(pltpu.get_barrier_semaphore(), inc=1, device_id=partner, device_id_type=MESH)


def greeted(partners):
    pl.semaphore_wait(pltpu.get_barrier_semaphore(), len(partners))


def rows(h, first=0):
    return slice(first + HEAD_SIZE * h, first + HEAD_SIZE * (h + 1))


def attend(pairs):
    heads = range(PLAN_HEADS)
    ones = jnp.ones((16, CSIZE), jnp.bfloat16)
    scored = [
        [
            lax.dot_general(key(h), query(h), (((0,), (0,)), ((), ())), preferred_element_type=jnp.float32)
            for h in heads
        ]
        for query, key, value in pairs
    ]
    done = []
    for (query, key, value), scores in zip(pairs, scored):
        highest = [jnp.max(s, axis=0, keepdims=True) for s in scores]
        weights = [jnp.exp2(s - top).astype(jnp.bfloat16) for s, top in zip(scores, highest)]
        mixed = [
            jnp.dot(jnp.concatenate([value(h), ones], 0), weights[h], preferred_element_type=jnp.float32)
            for h in heads
        ]
        done.append((highest, mixed))
    return done


def make_list(query_owner, query_local, key_owner, key_local):
    z, y, c = coordinates()
    div, rem = lax.div, lax.rem
    qz, qy, qc = div(query_owner, 8), rem(div(query_owner, 2), 4), rem(query_owner, 2)
    kz, ky, kc = div(key_owner, 8), rem(div(key_owner, 2), 4), rem(key_owner, 2)
    iota = lax.broadcasted_iota
    number = iota(jnp.int32, (8, 128), 0) * 128 + iota(jnp.int32, (8, 128), 1)

    def seen(d):
        d = rem(d + RING, RING)
        return jnp.where(d == 0, 0, jnp.where(d == RING - 1, 1, d + 1))

    def table(mine, q_seen, k_seen, plan):
        near = k_seen != RING - 1
        state = plan * RING * LOCAL + q_seen * LOCAL + query_local
        item = state + (jnp.where(near, k_seen * 2 * LOCAL, 0) + kc * LOCAL + key_local) * 128 + number * 16384
        early = mine & near & (q_seen != RING - 1)
        flag = lambda f: jnp.where(f, jnp.ones((8, 128), jnp.float32), 0.0)
        return [flag(mine & near), flag(mine & (k_seen == RING - 1)), jnp.where(early, state, -1).astype(jnp.float32), item.astype(jnp.float32)]

    tables = zip(
        table((qy == y) & (qc == c) & (kz == z), seen(qz - z), seen(ky - y), 0),
        table((qz == z) & (qc == c) & (ky == y), seen(qy - y), seen(kz - z), 1),
    )
    near, far, early, items = [jnp.concatenate(pair, 0) for pair in tables]
    early, values = early.T, items.T
    numbers = jnp.concatenate([number, number], 0).astype(jnp.float32).T
    lane = iota(jnp.int32, (128, 128), 1).astype(jnp.float32)
    first = jnp.full((128, 128), 4096.0, jnp.float32)
    for r in range(16):
        first = jnp.minimum(first, jnp.where(early[:, r : r + 1] == lane, numbers[:, r : r + 1], 4096.0))
    first = jnp.min(first, axis=0, keepdims=True)
    slots, chosen = jnp.zeros((128, 128), jnp.float32), jnp.zeros((128, 128), jnp.float32)
    for r in range(16):
        hit = jnp.where((early[:, r : r + 1] == lane) & (numbers[:, r : r + 1] == first), 1.0, 0.0)
        slots += hit * (values[:, r : r + 1] + 1.0)
        chosen += jnp.where(lane == r, jnp.max(hit, axis=1, keepdims=True), 0.0)
    slots = (jnp.sum(slots, axis=0, keepdims=True) - 1.0).astype(jnp.int32)
    near = near * (1.0 - chosen.T[:16])
    before = jnp.where(iota(jnp.int32, (128, 128), 0) < iota(jnp.int32, (128, 128), 1), 1.0, 0.0)

    def ranks(ones, start):
        inside = jnp.dot(ones, before, preferred_element_type=jnp.float32)
        wide = jnp.broadcast_to(jnp.sum(ones, axis=1, keepdims=True), (16, 128))
        ahead = [start]
        for r in range(16):
            ahead.append(ahead[-1] + wide[r : r + 1])
        return inside + jnp.concatenate(ahead[:16], 0), ahead[16]

    near_rank, count = ranks(near, jnp.zeros((1, 128), jnp.float32))
    filled = jnp.floor((count + (UNROLL - 1)) * (1.0 / UNROLL)) * UNROLL
    far_rank, total = ranks(far, filled)
    rank = jnp.where(near > 0, near_rank, jnp.where(far > 0, far_rank, -1.0)).T
    values = values - NOTHING
    place = iota(jnp.int32, (128, LIST_MAX), 1).astype(jnp.float32)
    listed = jnp.zeros((128, LIST_MAX), jnp.float32)
    for r in range(16):
        listed += jnp.where(rank[:, r : r + 1] == place, values[:, r : r + 1], 0.0)
    listed = jnp.sum(listed, axis=0, keepdims=True) + NOTHING
    at = iota(jnp.int32, (1, LIST_MAX), 1)
    repeat = lambda v: jnp.concatenate([v] * (LIST_MAX // 128), 1)
    listed = jnp.where(at == LIST_MAX - 2, repeat(filled), listed)
    listed = jnp.where(at == LIST_MAX - 1, repeat(total), listed)
    return listed.astype(jnp.int32), slots


def gather_kernel(
    nodes_hbm, weight_hbm, bias_in, bucket_ref, ko_ref, kl_ref, qo_ref, ql_ref,
    qg_ref, kn_ref, kf_ref, table_ref, list_ref, bias_ref, m_ref, l_ref, acc_ref,
    nodes_ref, weight_ref, slots_ref, slots_s, table_s, bias_s, scalar_sem,
    ring_send, ring_recv, pair_send, pair_recv, table_send, table_recv, load_sem, weight_sem,
):
    z, y, c = coordinates()
    heads = range(PLAN_HEADS)
    size = LOCAL // PIECES
    partners = [ring_at(axis, step) for axis in "zy" for step in (1, 2, 3)] + [sibling()]
    greet(partners)

    def local_copy(source, target, sem):
        copy = pltpu.make_async_copy(source, target, sem)
        copy.start()
        return copy

    node_rows = lambda p: pl.ds(p * size * CSIZE, size * CSIZE)
    load_nodes = lambda p: local_copy(nodes_hbm.at[node_rows(p)], nodes_ref.at[node_rows(p)], load_sem.at[p])
    node_loads = [load_nodes(0)]
    weight_load = local_copy(weight_hbm, weight_ref, weight_sem)
    node_loads += [load_nodes(p) for p in range(1, PIECES)]
    table_ref[c, z, y] = jnp.concatenate(
        [bucket_ref[...], jnp.zeros((1, 128 - bucket_ref.shape[1]), jnp.int32)], 1
    )
    for i in range(2 * PLAN_HEADS):
        bias_ref[i, :, : bias_in.shape[1]] = bias_in[i : i + 1] * LOG2E
    sent = []

    def part(p):
        return pl.ds(p * size, size)

    def side(h):
        return pl.ds(h * (LOCAL // 2), LOCAL // 2)

    streams = []
    for plan in range(2):
        q_axis, kv_axis = ("z", "y") if plan == 0 else ("y", "z")
        for kind, axis in (("kv", kv_axis), ("q", q_axis)):
            at = z if axis == "z" else y
            if kind == "q":
                slot = lambda p, r, plan=plan: qg_ref.at[plan, p, r]
            else:
                slot = lambda p, r, plan=plan: kf_ref.at[plan, c, r] if p == 3 else kn_ref.at[plan, p, c, r]
            streams.append((len(streams), plan, kind, axis, at, slot))

    def send(src, dst, send_sem, recv_sem, device):
        copy = pltpu.make_async_remote_copy(
            src_ref=src, dst_ref=dst, send_sem=send_sem, recv_sem=recv_sem,
            device_id=device, device_id_type=MESH,
        )
        copy.start()
        sent.append(copy)

    def arrived(ref, sem):
        pltpu.make_async_remote_copy(
            src_ref=ref, dst_ref=ref, send_sem=ring_send.at[0, 0], recv_sem=sem,
            device_id=sibling(), device_id_type=MESH,
        ).wait_recv()

    weight_load.wait()
    def project(cluster, carry):
        normed = norm_rows(nodes_ref[pl.ds(cluster * CSIZE, CSIZE), :].astype(jnp.float32)).astype(jnp.bfloat16)
        for i in range(3):
            projected = lax.dot_general(
                weight_ref[i], normed, (((1,), (1,)), ((), ())), preferred_element_type=jnp.float32
            )
            if i == 0:
                projected = projected * (LOG2E / math.sqrt(HEAD_SIZE))
            projected = projected.astype(jnp.bfloat16)
            for plan in range(2):
                block = projected[plan * PLAN_FEATURES : (plan + 1) * PLAN_FEATURES]
                if i == 0:
                    qg_ref[plan, 0, cluster] = block
                else:
                    kn_ref[plan, 0, c, cluster, (i - 1) * PLAN_FEATURES : i * PLAN_FEATURES, :] = block
        return carry

    ordered = [s for s in streams if s[2] == "kv"] + [s for s in streams if s[2] == "q"]
    for p in range(PIECES):
        node_loads[p].wait()
        lax.fori_loop(p * size, (p + 1) * size, project, 0)
        if p == 0:
            greeted(partners)
            for step in (1, 2, 3):
                send(table_ref.at[c, z, y], table_ref.at[c, z, y], table_send.at[step - 1], table_recv.at[step - 1], ring_at("y", step))
        for number, plan, kind, axis, at, slot in ordered:
            for way, first, seen in ((1, 0, 1), (-1, PIECES, 2)):
                send(
                    slot(0, part(p)), slot(seen, part(p)),
                    ring_send.at[number, first + p], ring_recv.at[number, first + p], ring_at(axis, way),
                )
        if p % (PIECES // 2) == PIECES // 2 - 1:
            h = p // (PIECES // 2)
            for number, plan, kind, axis, at, slot in ordered:
                if kind == "kv":
                    send(slot(0, side(h)), slot(0, side(h)), pair_send.at[plan, h], pair_recv.at[plan, h], sibling())
    listed, slots = make_list(qo_ref[...], ql_ref[...], ko_ref[...], kl_ref[...])
    list_ref[...] = listed
    slots_ref[...] = slots
    m_ref[...] = jnp.full(m_ref.shape, NEVER, jnp.float32)
    l_ref[...] = jnp.zeros(l_ref.shape, jnp.float32)
    acc_ref[...] = jnp.zeros(acc_ref.shape, jnp.float32)
    scalars = [local_copy(slots_ref, slots_s, scalar_sem.at[0]), local_copy(bias_ref, bias_s, scalar_sem.at[1])]

    for plan in range(2):
        bias = [bias_ref[plan * PLAN_HEADS + h, :, 0:1] for h in heads]

        def own_tiles(step, carry):
            group = [step * UNROLL + u for u in range(UNROLL)]
            pairs = [
                (
                    lambda h, i=i: qg_ref[plan, 0, i, rows(h), :],
                    lambda h, i=i: kn_ref[plan, 0, c, i, rows(h), :],
                    lambda h, i=i: kn_ref[plan, 0, c, i, rows(h, PLAN_FEATURES), :],
                )
                for i in group
            ]
            for i, (highest, mixed) in zip(group, attend(pairs)):
                for h in heads:
                    m_ref[plan * RING * LOCAL + i, h : h + 1, :] = highest[h] + bias[h]
                    l_ref[plan * RING * LOCAL + i, h : h + 1, :] = mixed[h][HEAD_SIZE : HEAD_SIZE + 1]
                    acc_ref[plan * RING * LOCAL + i, rows(h), :] = mixed[h][:HEAD_SIZE]
            return carry

        lax.fori_loop(0, LOCAL // UNROLL, own_tiles, 0)
    for step in (1, 2, 3):
        arrived(table_ref.at[c, z, place(y, -step)], table_recv.at[step - 1])
    for step in (1, 2, 3):
        send(table_ref.at[c, z], table_ref.at[c, z], table_send.at[2 + step], table_recv.at[2 + step], ring_at("z", step))
    for h in range(2):
        for p in range(h * PIECES // 2, (h + 1) * PIECES // 2):
            for number, plan, kind, axis, at, slot in ordered:
                before, after = slot(1, part(p)), slot(2, part(p))
                arrived(before, ring_recv.at[number, p])
                arrived(after, ring_recv.at[number, PIECES + p])
                onward, way = (before, 1) if p % 2 == 0 else (after, -1)
                far = 2 * PIECES + p
                send(onward, slot(3, part(p)), ring_send.at[number, far], ring_recv.at[number, far], ring_at(axis, way))
                if kind == "kv" and p % (PIECES // 2) == PIECES // 2 - 1:
                    for index in (1, 2):
                        block, sem = slot(index, side(h)), 2 * index + h
                        send(block, block, pair_send.at[plan, sem], pair_recv.at[plan, sem], sibling())
        if h == 0:
            for step in (1, 2, 3):
                arrived(table_ref.at[c, place(z, -step)], table_recv.at[2 + step])
            send(table_ref.at[c], table_ref.at[c], table_send.at[6], table_recv.at[6], sibling())
    arrived(table_ref.at[1 - c], table_recv.at[6])
    scalars.append(local_copy(table_ref, table_s, scalar_sem.at[2]))
    for plan in range(2):
        for index in range(3):
            for h in range(2):
                arrived(kn_ref.at[plan, index, 1 - c, side(h)], pair_recv.at[plan, 2 * index + h])
    for copy in scalars:
        copy.wait()
    def early(plan, start, end):

        def early_tiles(step, carry):
            group, pairs = [], []
            for u in range(UNROLL):
                i = step * UNROLL + u
                item = slots_s[0, plan * RING * LOCAL + i]
                valid = item >= 0
                item = jnp.maximum(item, 0)
                key = lax.bitwise_and(lax.shift_right_logical(item, 7), 127)
                tile = lax.bitwise_and(lax.shift_right_logical(item, 14), 1023)
                worker = lax.shift_right_logical(tile, 5)
                bucket = table_s[
                    lax.bitwise_and(worker, 1), lax.shift_right_logical(worker, 3),
                    lax.bitwise_and(lax.shift_right_logical(worker, 1), 3), 0, lax.bitwise_and(tile, 31),
                ]
                bucket = lax.bitwise_and(bucket, 31)
                place_of = (jnp.minimum(lax.shift_right_logical(key, 4), 2), lax.bitwise_and(lax.shift_right_logical(key, 3), 1), lax.bitwise_and(key, 7))
                group.append((i, valid, [bias_s[plan * PLAN_HEADS + h, 0, bucket] for h in heads]))
                pairs.append((
                    lambda h, i=i: qg_ref[plan, lax.div(i, LOCAL), lax.rem(i, LOCAL), rows(h), :],
                    lambda h, k=place_of: kn_ref[plan, k[0], k[1], k[2], rows(h), :],
                    lambda h, k=place_of: kn_ref[plan, k[0], k[1], k[2], rows(h, PLAN_FEATURES), :],
                ))
            for (i, valid, bias), (highest, mixed) in zip(group, attend(pairs)):
                for h in heads:
                    top = jnp.where(valid, highest[h] + bias[h], NEVER)
                    old_m, old_l, old_acc = m_ref[plan * RING * LOCAL + i, h : h + 1, :], l_ref[plan * RING * LOCAL + i, h : h + 1, :], acc_ref[plan * RING * LOCAL + i, rows(h), :]
                    new_m = jnp.maximum(old_m, top)
                    keep = jnp.exp2(old_m - new_m)
                    fresh = jnp.where(valid, jnp.exp2(top - new_m), 0.0)
                    m_ref[plan * RING * LOCAL + i, h : h + 1, :] = new_m
                    l_ref[plan * RING * LOCAL + i, h : h + 1, :] = old_l * keep + mixed[h][HEAD_SIZE : HEAD_SIZE + 1] * fresh
                    acc_ref[plan * RING * LOCAL + i, rows(h), :] = old_acc * keep + mixed[h][:HEAD_SIZE] * fresh
            return carry

        lax.fori_loop(start, end, early_tiles, 0)

    def pass_far(h):
        for number, plan, kind, axis, at, slot in ordered:
            for p in range(h * PIECES // 2, (h + 1) * PIECES // 2):
                arrived(slot(3, part(p)), ring_recv.at[number, 2 * PIECES + p])
            if kind == "kv":
                far = slot(3, side(h))
                send(far, far, pair_send.at[plan, 6 + h], pair_recv.at[plan, 6 + h], sibling())

    steps = 3 * LOCAL // UNROLL
    early(0, 0, steps - 1)
    pass_far(0)
    early(0, steps - 1, steps)
    early(1, 0, steps // 2 - 1)
    pass_far(1)
    early(1, steps // 2 - 1, steps)
    for plan in range(2):
        for h in range(2):
            arrived(kf_ref.at[plan, 1 - c, side(h)], pair_recv.at[plan, 6 + h])
    for copy in sent:
        copy.wait_send()


def gather(nodes, qkv_weight, bias, bucket, key_owner, key_local, query_owner, query_local):
    any_space, in_vmem = pl.BlockSpec(memory_space=pl.ANY), pl.BlockSpec(memory_space=pltpu.VMEM)
    dma, vmem = pltpu.SemaphoreType.DMA, pltpu.VMEM
    q_shape, kv_shape = (PLAN_FEATURES, CSIZE), (2 * PLAN_FEATURES, CSIZE)
    states = 2 * RING * LOCAL + 1
    m_shape, acc_shape = (states, 8, CSIZE), (states, PLAN_FEATURES, CSIZE)
    return pl.pallas_call(
        gather_kernel,
        out_shape=[
            vmem((2, RING, LOCAL) + q_shape, jnp.bfloat16),
            vmem((2, 3, 2, LOCAL) + kv_shape, jnp.bfloat16),
            vmem((2, 2, LOCAL) + kv_shape, jnp.bfloat16),
            vmem((2, RING, RING, 1, 128), jnp.int32),
            vmem((1, LIST_MAX), jnp.int32),
            vmem((2 * PLAN_HEADS, 1, 128), jnp.float32),
            vmem(m_shape, jnp.float32),
            vmem(m_shape, jnp.float32),
            vmem(acc_shape, jnp.float32),
        ],
        in_specs=[any_space] * 2 + [in_vmem] * 6,
        out_specs=[in_vmem] * 9,
        scratch_shapes=[
            vmem(nodes.shape, jnp.bfloat16),
            vmem(qkv_weight.shape, jnp.bfloat16),
            vmem((1, 128), jnp.int32),
            pltpu.SMEM((1, 128), jnp.int32),
            pltpu.SMEM((2, RING, RING, 1, 128), jnp.int32),
            pltpu.SMEM((2 * PLAN_HEADS, 1, 128), jnp.float32),
            dma((3,)),
            dma((4, 3 * PIECES)), dma((4, 3 * PIECES)), dma((2, 8)), dma((2, 8)), dma((7,)), dma((7,)),
            dma((PIECES,)), dma(()),
        ],
        compiler_params=pltpu.CompilerParams(
            collective_id=0, has_side_effects=True, vmem_limit_bytes=36 * 2**20
        ),
        name="gather",
    )(nodes, qkv_weight, bias, bucket, key_owner, key_local, query_owner, query_local)


def tile_kernel(
    list_hbm, bias_hbm, table_hbm, m_in, l_in, acc_in, q_ref, kn_ref, kf_ref,
    part_ref, log_ref, m_ref, l_ref, acc_ref, list_ref, bias_ref, table_ref, table_sem,
):
    heads = range(PLAN_HEADS)
    queries = part_ref.shape[0]
    waits = []
    for i, (source, target) in enumerate(((list_hbm, list_ref), (table_hbm, table_ref), (bias_hbm, bias_ref))):
        waits.append(pltpu.make_async_copy(source, target, table_sem.at[i]))
        waits[-1].start()

    def batch(kv_ref, step, carry):
        items, pairs = [], []
        for u in range(UNROLL):
            item = list_ref[0, step * UNROLL + u]
            state = lax.bitwise_and(item, 127)
            key = lax.bitwise_and(lax.shift_right_logical(item, 7), 127)
            tile = lax.shift_right_logical(item, 14)
            query = jnp.minimum(state, queries - 1)
            plan = lax.shift_right_logical(query, 5)
            key = plan * (kv_ref.shape[0] // 2) + key
            worker = lax.shift_right_logical(tile, 5)
            bucket = table_ref[
                lax.bitwise_and(worker, 1), lax.shift_right_logical(worker, 3),
                lax.bitwise_and(lax.shift_right_logical(worker, 1), 3), 0, lax.bitwise_and(tile, 31),
            ]
            items.append((state, [bias_ref[plan * PLAN_HEADS + h, 0, bucket] for h in heads]))
            pairs.append((
                lambda h, i=query: q_ref[i, rows(h), :],
                lambda h, i=key: kv_ref[i, rows(h), :],
                lambda h, i=key: kv_ref[i, rows(h, PLAN_FEATURES), :],
            ))
        for (state, bias), (highest, mixed) in zip(items, attend(pairs)):
            tops = [top + b for top, b in zip(highest, bias)]
            old_m = [m_ref[state, h : h + 1, :] for h in heads]
            old_l = [l_ref[state, h : h + 1, :] for h in heads]
            old_acc = [acc_ref[state, rows(h), :] for h in heads]
            new_m = [jnp.maximum(a, b) for a, b in zip(old_m, tops)]
            keep = [jnp.exp2(a - b) for a, b in zip(old_m, new_m)]
            fresh = [jnp.exp2(a - b) for a, b in zip(tops, new_m)]
            for h in heads:
                m_ref[state, h : h + 1, :] = new_m[h]
                l_ref[state, h : h + 1, :] = old_l[h] * keep[h] + mixed[h][HEAD_SIZE : HEAD_SIZE + 1] * fresh[h]
                acc_ref[state, rows(h), :] = old_acc[h] * keep[h] + mixed[h][:HEAD_SIZE] * fresh[h]
        return carry

    for copy in waits:
        copy.wait()
    split = lax.div(list_ref[0, LIST_MAX - 2], UNROLL)
    lax.fori_loop(0, split, functools.partial(batch, kn_ref), 0)
    lax.fori_loop(
        split, lax.div(list_ref[0, LIST_MAX - 1] + UNROLL - 1, UNROLL), functools.partial(batch, kf_ref), 0
    )

    def finish(group, carry):
        for local in range(LOCAL):
            state = group * LOCAL + local
            for h in heads:
                total = l_ref[state, h : h + 1, :]
                safe = jnp.where(total > 0, total, 1.0)
                part_ref[group * LOCAL + local % 2 * RING + local // 2, rows(h), :] = (
                    acc_ref[state, rows(h), :] * (1.0 / safe)
                ).astype(jnp.bfloat16)
                row = local // 2 % 2 * PLAN_HEADS + h
                log_ref[group, local % 2, local // 4, row : row + 1, :] = m_ref[state, h : h + 1, :] + jnp.log2(safe)
        return carry

    lax.fori_loop(0, queries // LOCAL, finish, 0)


def tiles(items, bias, table, m, l, acc, q_all, kv_near, kv_far):
    queries, keys = 2 * RING * LOCAL, 2 * 2 * LOCAL
    in_vmem = pl.BlockSpec(memory_space=pltpu.VMEM)
    part_shape = (queries, PLAN_FEATURES, CSIZE)
    log_shape = (2 * RING, 2, 2, 8, CSIZE)
    dma, vmem = pltpu.SemaphoreType.DMA, pltpu.VMEM
    return pl.pallas_call(
        tile_kernel,
        in_specs=[in_vmem] * 9,
        out_specs=[in_vmem] * 5,
        input_output_aliases={3: 2, 4: 3, 5: 4},
        scratch_shapes=[
            pltpu.SMEM((1, LIST_MAX), jnp.int32),
            pltpu.SMEM((2 * PLAN_HEADS, 1, 128), jnp.float32),
            pltpu.SMEM((2, RING, RING, 1, 128), jnp.int32),
            dma((3,)),
        ],
        out_shape=[vmem(part_shape, jnp.bfloat16), vmem(log_shape, jnp.float32)]
        + [vmem(state.shape, jnp.float32) for state in (m, l, acc)],
        compiler_params=pltpu.CompilerParams(vmem_limit_bytes=8 * 2**20),
        name="tiles",
    )(
        items, bias, table, m, l, acc,
        q_all.reshape(queries, PLAN_FEATURES, CSIZE),
        kv_near.reshape(3 * keys, 2 * PLAN_FEATURES, CSIZE), kv_far.reshape(keys, 2 * PLAN_FEATURES, CSIZE),
    )


def tail_kernel(
    part_ref, log_ref, nodes_ref, wo_hbm, up_hbm, down_hbm, out_ref,
    wo_ref, up_ref, down_ref, rows_ref, part_in, log_in, far_part, far_log, both_part, both_log, merged, gathered, resid_ref, normed_ref, staged,
    weight_sem, back_send, back_recv, x_send, x_recv, out_send, out_recv, out_own,
):
    z, y, c = coordinates()
    me = lax.axis_index("owner")
    x = lax.axis_index("head")
    heads = range(PLAN_HEADS)
    features = 2 * PLAN_FEATURES

    def load(source, target, sem):
        copy = pltpu.make_async_copy(source, target, sem)
        copy.start()
        return copy

    def across(step):
        return (me, place(x, step))

    partners = [ring_at(axis, step) for axis in "zy" for step in (1, 3)] + [across(step) for step in (1, 2, 3)]
    greet(partners)
    ways = ((0, 1), (1, -1))
    ring = [(0, "z", z), (1, "y", y)]
    half = lambda h: pl.ds(h * (RING // 2), RING // 2)
    weights = [
        load(nodes_ref.at[pl.ds(x * 2 * CSIZE, 2 * CSIZE)], rows_ref, weight_sem.at[0]),
        load(wo_hbm, wo_ref, weight_sem.at[1]),
        load(up_hbm, up_ref, weight_sem.at[2]),
        load(down_hbm, down_ref, weight_sem.at[3]),
    ]
    greeted(partners)
    sent = []

    def send(src, dst, send_sem, recv_sem, device):
        copy = pltpu.make_async_remote_copy(
            src_ref=src, dst_ref=dst, send_sem=send_sem, recv_sem=recv_sem,
            device_id=device, device_id_type=MESH,
        )
        copy.start()
        sent.append(copy)

    def arrived(ref, sem):
        pltpu.make_async_remote_copy(
            src_ref=ref, dst_ref=ref, send_sem=x_send.at[0, 0], recv_sem=sem,
            device_id=across(1), device_id_type=MESH,
        ).wait_recv()

    def back(plan, way, turn, kind, src, dst, device):
        send(src, dst, back_send.at[plan, way, turn, kind], back_recv.at[plan, way, turn, kind], device)

    def send_out(turn):
        t, first, count = TURNS[turn]
        lanes = pl.ds(first, count)
        for plan, axis, at in ring:
            for way, step in ways:
                to, far = ring_at(axis, step), 3
                back(plan, way, turn, 0, part_ref.at[plan, far, t, half(way), :, lanes], far_part.at[plan, way, t, :, :, lanes], to)
                back(plan, way, turn, 1, log_ref.at[plan, far, t, way, :, lanes], far_log.at[plan, way, t, :, lanes], to)
        for plan, axis, at in ring:
            for way, step in ways:
                to, next_at = ring_at(axis, step), 2 - way
                back(
                    plan, way, turn, 2, part_ref.at[plan, next_at, t, half(1 - way), :, lanes],
                    part_in.at[plan, way, t, half(1 - way), :, lanes], to,
                )
                back(
                    plan, way, turn, 3, log_ref.at[plan, next_at, t, 1 - way, :, lanes],
                    log_in.at[plan, way, t, 1 - way, :, lanes], to,
                )

    def combine(turn):
        t, first, count = TURNS[turn]
        lanes = pl.ds(first, count)
        span = slice(first, first + count)
        for plan, axis, at in ring:
            for way, step in ways:
                arrived(far_part.at[plan, way, t, :, :, lanes], back_recv.at[plan, way, turn, 0])
                arrived(far_log.at[plan, way, t, :, lanes], back_recv.at[plan, way, turn, 1])
                one, two = log_ref[plan, 2 - way, t, way, :, span], far_log[plan, way, t, :, span]
                best = jnp.maximum(one, two)
                shares = [jnp.exp2(one - best), jnp.exp2(two - best)]
                total = shares[0] + shares[1]
                both_log[plan, way, t, :, span] = best + jnp.log2(total)
                scale = 1.0 / total
                shares = [share * scale for share in shares]
                for to in range(2):
                    for h in heads:
                        row = to * PLAN_HEADS + h
                        both_part[plan, way, t, to, rows(h), span] = (
                            part_ref[plan, 2 - way, t, way * 2 + to, rows(h), span].astype(jnp.float32) * shares[0][row : row + 1]
                            + far_part[plan, way, t, to, rows(h), span].astype(jnp.float32) * shares[1][row : row + 1]
                        ).astype(jnp.bfloat16)
                to = ring_at(axis, step)
                back(
                    plan, way, turn, 4, both_part.at[plan, way, t, :, :, lanes],
                    part_in.at[plan, way, t, half(way), :, lanes], to,
                )
                back(
                    plan, way, turn, 5, both_log.at[plan, way, t, :, lanes], log_in.at[plan, way, t, way, :, lanes], to
                )

    mine = pl.ds(pl.multiple_of(x * features, 64), features)

    def merge(turn):
        t, first, count = TURNS[turn]
        lanes = pl.ds(first, count)
        span = slice(first, first + count)
        for plan in range(2):
            for way in range(2):
                arrived(part_in.at[plan, way, t, half(1 - way), :, lanes], back_recv.at[plan, way, turn, 2])
                arrived(log_in.at[plan, way, t, 1 - way, :, lanes], back_recv.at[plan, way, turn, 3])
                arrived(part_in.at[plan, way, t, half(way), :, lanes], back_recv.at[plan, way, turn, 4])
                arrived(log_in.at[plan, way, t, way, :, lanes], back_recv.at[plan, way, turn, 5])
        for plan, axis, at in ring:
            for to in range(RING):
                h0 = to // 2
                logs = [log_ref[plan, 0, t, h0, :, span]] + [log_in[plan, way, t, h0, :, span] for way in range(2)]
                best = jnp.maximum(jnp.maximum(logs[0], logs[1]), logs[2])
                shares = [jnp.exp2(log - best) for log in logs]
                scale = 1.0 / (shares[0] + shares[1] + shares[2])
                shares = [share * scale for share in shares]
                for h in heads:
                    row = to % 2 * PLAN_HEADS + h
                    total = part_ref[plan, 0, t, to, rows(h), span].astype(jnp.float32) * shares[0][row : row + 1]
                    for way in range(2):
                        total += part_in[plan, way, t, to, rows(h), span].astype(jnp.float32) * shares[way + 1][row : row + 1]
                    merged[t, to, rows(h, plan * PLAN_FEATURES), span] = total.astype(jnp.bfloat16)
        for step in (2, 1, 3):
            send(
                merged.at[t, place(x, step), :, lanes], gathered.at[t, mine, lanes],
                x_send.at[turn, step - 1], x_recv.at[turn, step - 1], across(step),
            )
        gathered[t, mine, span] = merged[t, x, :, span]

    wide = up_ref.shape[1] // BLOCKS
    out_copies = []

    def begin(turn):
        t, first, count = TURNS[turn]
        lanes = pl.ds(first, count)
        part = slice(t * CSIZE + first, t * CSIZE + first + count)
        for step in (1, 2, 3):
            source = place(x, -step)
            arrived(gathered.at[t, pl.ds(pl.multiple_of(source * features, 64), features), lanes], x_recv.at[turn, step - 1])
        mixed = lax.dot_general(
            gathered[t, :, first : first + count], wo_ref[...], (((0,), (0,)), ((), ())), preferred_element_type=jnp.float32
        )
        resid = rows_ref[part, :].astype(jnp.float32) + mixed
        resid_ref[part, :] = resid
        normed_ref[part, :] = norm_rows(resid).astype(jnp.bfloat16)

    def feed(turn, start, end):
        t, first, count = TURNS[turn]
        part = slice(t * CSIZE + first, t * CSIZE + first + count)

        def block(step, carry):
            units = pl.ds(pl.multiple_of(step * wide, 128), wide)
            hidden = jax.nn.gelu(
                jnp.dot(normed_ref[part, :], up_ref[:, units], preferred_element_type=jnp.float32)
            ).astype(jnp.bfloat16)
            resid_ref[part, :] += jnp.dot(hidden, down_ref[units, :], preferred_element_type=jnp.float32)
            return carry

        lax.fori_loop(start, end, block, 0)

    def hand_out(turn):
        t, first, count = TURNS[turn]
        part = slice(t * CSIZE + first, t * CSIZE + first + count)
        staged[:, part] = resid_ref[part, :].astype(jnp.bfloat16).T
        target = out_ref.at[:, pl.ds(pl.multiple_of((x * 2 + t) * CSIZE + first, 128), count)]
        block = lambda j: staged.at[pl.ds(pl.multiple_of(j * features, 64), features), part]
        for step in (2, 1, 3):
            send(
                block(place(x, step)), target, out_send.at[turn, step - 1], out_recv.at[turn, step - 1], across(step)
            )
        out_copies.append(load(block(x), target, out_own.at[turn]))

    send_out(0)
    combine(0)
    send_out(1)
    send_out(2)
    merge(0)
    combine(1)
    combine(2)
    merge(1)
    for copy in weights:
        copy.wait()
    begin(0)
    feed(0, 0, BLOCKS // 2)
    merge(2)
    feed(0, BLOCKS // 2, BLOCKS)
    hand_out(0)
    for turn in (1, 2):
        begin(turn)
        feed(turn, 0, BLOCKS)
        hand_out(turn)
    for turn, (t, first, count) in enumerate(TURNS):
        for step in (1, 2, 3):
            source = place(x, -step)
            arrived(
                out_ref.at[:, pl.ds(pl.multiple_of((source * 2 + t) * CSIZE + first, 128), count)],
                out_recv.at[turn, step - 1],
            )
    for copy in out_copies:
        copy.wait()
    for copy in sent:
        copy.wait_send()


def tail(parts, logs, nodes, out_weight, up_weight, down_weight):
    any_space = pl.BlockSpec(memory_space=pl.ANY)
    dma, vmem = pltpu.SemaphoreType.DMA, pltpu.VMEM
    width = nodes.shape[1]
    features = 2 * PLAN_FEATURES
    return pl.pallas_call(
        tail_kernel,
        out_shape=jax.ShapeDtypeStruct((features, nodes.shape[0]), jnp.bfloat16),
        in_specs=[pl.BlockSpec(memory_space=pltpu.VMEM)] * 2 + [any_space] * 4,
        out_specs=any_space,
        scratch_shapes=[
            vmem(out_weight.shape, jnp.bfloat16),
            vmem(up_weight.shape, jnp.bfloat16),
            vmem(down_weight.shape, jnp.bfloat16),
            vmem((2 * CSIZE, width), jnp.bfloat16),
            vmem((2, 2, 2, RING, PLAN_FEATURES, CSIZE), jnp.bfloat16),
            vmem((2, 2, 2, 2, 8, CSIZE), jnp.float32),
            vmem((2, 2, 2, 2, PLAN_FEATURES, CSIZE), jnp.bfloat16),
            vmem((2, 2, 2, 8, CSIZE), jnp.float32),
            vmem((2, 2, 2, 2, PLAN_FEATURES, CSIZE), jnp.bfloat16),
            vmem((2, 2, 2, 8, CSIZE), jnp.float32),
            vmem((2, RING, features, CSIZE), jnp.bfloat16),
            vmem((2, width, CSIZE), jnp.bfloat16),
            vmem((2 * CSIZE, width), jnp.float32),
            vmem((2 * CSIZE, width), jnp.bfloat16),
            vmem((RING * features, 2 * CSIZE), jnp.bfloat16),
            dma((4,)), dma((2, 2, 3, 6)), dma((2, 2, 3, 6)),
            dma((3, 3)), dma((3, 3)), dma((3, 3)), dma((3, 3)), dma((3,)),
        ],
        compiler_params=pltpu.CompilerParams(
            collective_id=1, has_side_effects=True, vmem_limit_bytes=36 * 2**20
        ),
        name="tail",
    )(parts, logs, nodes, out_weight, up_weight, down_weight)


def per_device(
    nodes, qkv_weight, out_weight, hop_bias, up_weight, down_weight,
    key_owner, key_local, query_owner, query_local, hop_bucket,
):
    lists = [array.reshape(8, 128) for array in (key_owner, key_local, query_owner, query_local)]
    q_all, kv_near, kv_far, table, items, bias, m, l, acc = gather(
        *[pltpu.with_memory_space_constraint(a, pltpu.HBM) for a in (nodes, qkv_weight.swapaxes(1, 2))], hop_bias.T, hop_bucket.reshape(1, -1), *lists
    )
    parts, logs, *_ = tiles(items, bias, table, m, l, acc, q_all, kv_near, kv_far)
    return tail(
        parts.reshape(2, RING, 2, RING, PLAN_FEATURES, CSIZE), logs.reshape(2, RING, 2, 2, 8, CSIZE),
        *[pltpu.with_memory_space_constraint(a, pltpu.HBM) for a in (nodes, out_weight, up_weight, down_weight)],
    ).T


def solution(mesh):
    placed = (
        P("owner", None), P(None, None, "head"), P(), P(None, "head"), P(), P(),
        P(), P(), P(), P(), P("owner"),
    )
    return jax.shard_map(
        per_device, mesh=mesh, in_specs=placed, out_specs=P("owner", "head"), check_vma=False
    )
```
